32 devices in a mesh: section: 2 (over x), expert: 8 (over z, y), dp: 2 (over core).
Axes of the slice: x: 2, y: 2, z: 4, core: 2. Of those that a mesh axis runs over, the one named last changes fastest.
Arguments:
- blocks: bfloat16 [2, 2048, 3072], P('section', ('dp', 'expert')), parts along dimension 1, may hold values from -6 to 6
- norm_gain: bfloat16 [2, 3072], P('section'), may hold values from 0.25 to 1.75
- w_gate: bfloat16 [2, 3072, 1536], P('section', None, 'expert'), may hold values from -0.109375 to 0.109375
- w_up: bfloat16 [2, 3072, 1536], P('section', None, 'expert'), may hold values from -0.109375 to 0.109375
- w_down: bfloat16 [2, 1536, 3072], P('section', 'expert'), may hold values from -0.15625 to 0.15625
- route_ids: int32 [2, 2048, 2], P('section', ('dp', 'expert')), parts along dimension 1, may hold values from 0 to 8, as said below
- route_weights: float32 [2, 2048, 2], P('section', ('dp', 'expert')), parts along dimension 1, may hold values from 0.05 to 1
Outputs:
- mixed: bfloat16 [2, 2048, 3072], P('section', ('dp', 'expert')), parts along dimension 1
The draws below stay inside these ranges and needn't reach their ends.
There are 2 independent parts, one for each index of `dp`. The reference program is written for one: setup_inputs(seed, part) draws one part's arguments, and reference() takes and returns one part's arrays. A program takes and returns all parts, laid end to end along the dimension named above; an argument that names none is the same for every part. Nothing has to cross between parts.
Inputs may be any that keep to these rules, and one draw needn't show every extreme that they name: `route_ids`: each token names 2 different ids. Within each aligned block of 128 tokens of a section (the tokens of one device), every computing expert (ids below 1) is named exactly 32 times and every zero-computation id at most 32 times.
All inputs are finite; a program needn't handle non-finite values.
Results may differ from the reference program's by a relative error of at most 0.0085.
Values may be sent and summed in bfloat16 or wider, within the bound.
No kernel may reach another device: no remote copies, remote signals or barrier semaphores. Data moves between devices by JAX's collectives and lax.ppermute only.
A program may use at most 64 MiB of HBM per device.

```python
import jax
import jax.numpy as jnp
from jax import lax

D = 3072
HID = 1536
HSLICE = 192
EXPERTS = 1
ZEROS = 8
TOPK = 2
TOK_DEV = 128
CAP = 32
TOKENS = 1024
N_SECTION = 2
N_EXPERT = 8


def route_plan(key):
    block_count = N_SECTION * N_EXPERT
    block_keys = jax.random.split(jax.random.fold_in(key, 11), block_count)
    ranks = jax.vmap(lambda k: jax.random.permutation(k, TOK_DEV))(block_keys).astype(jnp.int32)
    offset = jax.random.randint(jax.random.fold_in(key, 12), (block_count, 1), 0, ZEROS).astype(jnp.int32)
    flips = jax.random.randint(jax.random.fold_in(key, 13), (block_count, TOK_DEV), 0, 2).astype(jnp.int32)
    computing = ranks < EXPERTS * CAP
    comp_id = (ranks // CAP).astype(jnp.int32)
    zero_second = (EXPERTS + (ranks + offset) % ZEROS).astype(jnp.int32)
    zero_first = (EXPERTS + (ranks + offset + ZEROS // 2) % ZEROS).astype(jnp.int32)
    first = jnp.where(computing, comp_id, zero_first).astype(jnp.int32)
    pick_one = jnp.where(flips == 1, zero_second, first).astype(jnp.int32)
    pick_two = jnp.where(flips == 1, first, zero_second).astype(jnp.int32)
    ids = jnp.stack([pick_one, pick_two], axis=-1).reshape(N_SECTION, TOKENS, TOPK)
    return (ids.astype(jnp.int32), ids < EXPERTS)


def draw_route_ids(key, part):
    ids, computing = route_plan(key)
    return ids


def draw_route_weights(key, part):
    ids, computing = route_plan(key)
    key = jax.random.fold_in(key, 7)
    uniform_draw = jax.random.uniform(key, (N_SECTION, TOKENS, TOPK), jnp.float32)
    comp_weight = 0.5 + 0.5 * uniform_draw
    zero_weight = jnp.exp(jnp.log(0.05) + uniform_draw * jnp.log(20.0))
    return jnp.clip(jnp.where(computing, comp_weight, zero_weight), 0.05, 1.0).astype(jnp.float32)


def block_scale(own_key, extent, cuts, low, high):
    def one(dim, parts):
        steps = jax.random.uniform(jax.random.fold_in(jax.random.fold_in(own_key, 6), dim), (parts,), jnp.float32, low / len(cuts), high / len(cuts))
        return jnp.repeat(jnp.exp(steps), extent[dim] // parts).reshape((-1,) + (1,) * (len(extent) - dim - 1))

    level = one(*cuts[0])
    for cut in cuts[1:]:
        level = level * one(*cut)
    return level


def gaussian(own_key, dims, spread, bound, pieces=(), kind=jnp.bfloat16):
    drawn = spread * jax.random.normal(own_key, dims, jnp.float32)
    if pieces:
        drawn = drawn * block_scale(own_key, dims, pieces, -0.22, 0.18)
    return jnp.clip(drawn, -bound, bound).astype(kind)


def setup_inputs(seed: int = 0, part: int = 0) -> dict:
    key_list = jax.random.split(jax.random.key(seed), 8)
    part_keys = jax.random.split(jax.random.fold_in(key_list[7], part), 8)
    blocks = gaussian(part_keys[0], (N_SECTION, TOKENS, D), 1.0, 6.0, ((0, 2), (1, 8)))
    norm_gain = jnp.clip(1.0 + 0.15 * jax.random.normal(key_list[1], (N_SECTION, D), jnp.float32), 0.25, 1.75).astype(jnp.bfloat16)
    w_gate = gaussian(key_list[2], (N_SECTION, D, EXPERTS * HID), D ** -0.5, 0.109375, ((0, 2), (2, 8)))
    w_up = gaussian(key_list[3], (N_SECTION, D, EXPERTS * HID), D ** -0.5, 0.109375, ((0, 2), (2, 8)))
    w_down = gaussian(key_list[4], (N_SECTION, EXPERTS * HID, D), HID ** -0.5, 0.15625, ((0, 2), (1, 8)))
    route_ids = draw_route_ids(jax.random.fold_in(jax.random.fold_in(key_list[7], part), 71), part)
    route_weights = draw_route_weights(jax.random.fold_in(jax.random.fold_in(key_list[7], part), 71), part)
    return dict(blocks=blocks, norm_gain=norm_gain, w_gate=w_gate, w_up=w_up, w_down=w_down, route_ids=route_ids, route_weights=route_weights)


def reference(blocks, norm_gain, w_gate, w_up, w_down, route_ids, route_weights):
    arrived = jnp.roll(blocks, 1, axis=0)
    slice_count = HID // HSLICE

    def one_section(section_args):
        block, section_gain, gate_full, up_full, down_full, section_ids, section_weights = section_args
        residual = block.astype(jnp.float32)
        inverse = lax.rsqrt(lax.optimization_barrier(jnp.mean(residual * residual, axis=-1, keepdims=True)) + 1e-06)
        normed = (residual * inverse * section_gain.astype(jnp.float32)).astype(jnp.bfloat16)
        token_rows = jnp.repeat(normed.reshape(N_EXPERT, TOK_DEV, D), TOPK, axis=1)
        pick_ids = section_ids.reshape(N_EXPERT, TOK_DEV * TOPK)
        pick_weights = section_weights.reshape(N_EXPERT, TOK_DEV * TOPK)
        zero_weight = lax.optimization_barrier(jnp.sum(jnp.where(section_ids >= EXPERTS, section_weights, 0.0), axis=1))
        start = residual + zero_weight[:, None] * normed.astype(jnp.float32)
        start = start.reshape(N_EXPERT, TOK_DEV, D)

        def fill(rows, target):
            return jnp.zeros((CAP + 1, D), jnp.bfloat16).at[target].set(rows)[:CAP]

        def one_expert(total, expert):
            member = pick_ids == expert
            slot_rank = (jnp.cumsum(member.astype(jnp.int32), axis=1) - 1).astype(jnp.int32)
            target = jnp.where(member, slot_rank, CAP).astype(jnp.int32)
            buffer = jax.vmap(fill)(token_rows, target).reshape(N_EXPERT * CAP, D)
            gate_cols = lax.dynamic_slice_in_dim(gate_full, (expert * HID).astype(jnp.int32), HID, 1)
            up_cols = lax.dynamic_slice_in_dim(up_full, (expert * HID).astype(jnp.int32), HID, 1)
            down_rows = lax.dynamic_slice_in_dim(down_full, (expert * HID).astype(jnp.int32), HID, 0)
            gate_act = jnp.dot(buffer, gate_cols, preferred_element_type=jnp.float32)
            up_act = jnp.dot(buffer, up_cols, preferred_element_type=jnp.float32)
            hidden = (jax.nn.silu(gate_act) * up_act).astype(jnp.bfloat16)
            hidden_split = hidden.astype(jnp.float32).reshape(N_EXPERT * CAP, slice_count, HSLICE)
            down_split = down_rows.astype(jnp.float32).reshape(slice_count, HSLICE, D)
            partial_value = jnp.einsum('rgk,gkd->grd', hidden_split, down_split)
            rounded = lax.optimization_barrier(partial_value.astype(jnp.bfloat16))
            expert_out = lax.optimization_barrier(jnp.sum(rounded.astype(jnp.float32), axis=0)).reshape(N_EXPERT, CAP, D)
            safe_rank = jnp.clip(slot_rank, 0, CAP - 1).astype(jnp.int32)
            taken = jnp.take_along_axis(expert_out, safe_rank[:, :, None], axis=1)
            scale = jnp.where(member, pick_weights, 0.0)
            added = (taken * scale[:, :, None]).reshape(N_EXPERT, TOK_DEV, TOPK, D)
            return (total + lax.optimization_barrier(jnp.sum(added, axis=2)), None)
        total, unused = lax.scan(one_expert, start, jnp.arange(EXPERTS, dtype=jnp.int32))
        return total.reshape(TOKENS, D).astype(jnp.bfloat16)
    return lax.map(one_section, (arrived, norm_gain, w_gate, w_up, w_down, route_ids, route_weights))
```

```python
import functools

import jax
import jax.numpy as jnp
from jax import lax
from jax.experimental import pallas as pl
from jax.experimental.pallas import tpu as pltpu
from jax.sharding import PartitionSpec as P

HID = 1536
CAP = 32
VMEM = pl.BlockSpec(memory_space=pltpu.VMEM)
HBM = pl.BlockSpec(memory_space=pltpu.HBM)
PARAMS = pltpu.CompilerParams(vmem_limit_bytes=24 * 1024 * 1024)


def after(value, *others):
    return lax.optimization_barrier((value, *others))[0]


def load_kernel(count, *refs):
    sources, targets, sems = refs[:count], refs[count:2 * count], refs[2 * count]
    copies = [
        pltpu.make_async_copy(a, b, sems.at[i]) for i, (a, b) in enumerate(zip(sources, targets))
    ]
    for copy in copies:
        copy.start()
    for copy in copies:
        copy.wait()


def loaded(*arrays):
    return pl.pallas_call(
        functools.partial(load_kernel, len(arrays)),
        out_shape=tuple(jax.ShapeDtypeStruct(a.shape, a.dtype) for a in arrays),
        in_specs=[HBM] * len(arrays),
        out_specs=(VMEM,) * len(arrays),
        scratch_shapes=[pltpu.SemaphoreType.DMA((len(arrays),))],
        compiler_params=PARAMS,
        cost_estimate=pl.CostEstimate(flops=0, bytes_accessed=6 * 1024 * 1024, transcendentals=0),
    )(*(pltpu.with_memory_space_constraint(a, pltpu.HBM) for a in arrays))


def slot_rows(ids, e):
    count = ids.shape[1]
    earlier = lax.broadcasted_iota(jnp.int32, (count, count), 0)
    later = lax.broadcasted_iota(jnp.int32, (count, count), 1)
    before = jnp.where(earlier < later, 1.0, 0.0).astype(jnp.bfloat16)
    slot = lax.broadcasted_iota(jnp.int32, (CAP, count), 0).astype(jnp.float32)
    hit = jnp.max(jnp.where(ids == e, 1.0, 0.0), axis=0, keepdims=True)
    hit = jnp.broadcast_to(hit, (CAP, count))
    rank = jnp.dot(hit.astype(jnp.bfloat16), before, preferred_element_type=jnp.float32)
    return jnp.where(rank == slot, hit, 0.0)


def pick_kernel(experts, ids_ref, block_ref, out_ref):
    for e in range(experts):
        table = slot_rows(ids_ref[...], e).astype(jnp.bfloat16)
        rows = jnp.dot(table, block_ref[...], preferred_element_type=jnp.float32)
        out_ref[e * CAP:(e + 1) * CAP, :] = rows.astype(jnp.bfloat16)


def picked_rows(experts, ids_t, block):
    return pl.pallas_call(
        functools.partial(pick_kernel, experts),
        out_shape=jax.ShapeDtypeStruct((experts * CAP, block.shape[1]), jnp.bfloat16),
        in_specs=[VMEM, VMEM],
        out_specs=VMEM,
        compiler_params=PARAMS,
        cost_estimate=pl.CostEstimate(
            flops=2 * experts * CAP * block.size, bytes_accessed=block.size, transcendentals=0
        ),
    )(ids_t, block)


def mlp_kernel(near_ref, far_ref, gain_ref, gate_ref, up_ref, down_ref, near_out, far_out):
    count = near_ref.shape[0]
    rows = jnp.concatenate([near_ref[...], far_ref[...]], axis=0).astype(jnp.float32)
    inverse = lax.rsqrt(jnp.mean(rows * rows, axis=-1, keepdims=True) + 1e-06)
    normed = (rows * inverse * gain_ref[...].astype(jnp.float32)).astype(jnp.bfloat16)
    across = (((1,), (1,)), ((), ()))
    gate = lax.dot_general(normed, gate_ref[...], across, preferred_element_type=jnp.float32)
    up = lax.dot_general(normed, up_ref[...], across, preferred_element_type=jnp.float32)
    hidden = (gate / (1.0 + jnp.exp(-gate)) * up).astype(jnp.bfloat16)
    partial = jnp.dot(hidden, down_ref[...], preferred_element_type=jnp.float32)
    partial = partial.astype(jnp.bfloat16)
    near_out[...] = partial[:count]
    far_out[...] = partial[count:]


def mlp(near, far, gain, gate_t, up_t, down):
    rows = 2 * near.shape[0]
    width, hidden = down.shape[1], down.shape[0]
    out = jax.ShapeDtypeStruct(near.shape, jnp.bfloat16)
    return pl.pallas_call(
        mlp_kernel,
        out_shape=(out, out),
        in_specs=[VMEM] * 6,
        out_specs=(VMEM, VMEM),
        compiler_params=PARAMS,
        cost_estimate=pl.CostEstimate(
            flops=6 * rows * width * hidden, bytes_accessed=6 * width * hidden, transcendentals=0
        ),
    )(near, far, gain, gate_t, up_t, down)


def parts_of(value):
    terms = []
    for _ in range(3):
        terms.append(value.astype(jnp.bfloat16))
        value = value - terms[-1].astype(jnp.float32)
    return terms


def base_kernel(experts, gain_ref, ids_ref, weights_ref, *refs):
    block_refs, out_ref, table_ref = refs[:-2], refs[-2], refs[-1]
    ids, weights = ids_ref[...], weights_ref[...]
    count = ids.shape[1]
    zero = jnp.sum(jnp.where(ids >= experts, weights, 0.0), axis=0, keepdims=True)
    same = lax.broadcasted_iota(jnp.int32, (count, count), 0) == lax.broadcasted_iota(
        jnp.int32, (count, count), 1
    )
    zero = jnp.sum(jnp.where(same, zero, 0.0), axis=1, keepdims=True)
    start = 0
    for ref in block_refs:
        end = start + ref.shape[0]
        rows = ref[...].astype(jnp.float32)
        inverse = lax.rsqrt(jnp.mean(rows * rows, axis=-1, keepdims=True) + 1e-06)
        normed = (rows * inverse * gain_ref[...].astype(jnp.float32)).astype(jnp.bfloat16)
        out_ref[start:end] = rows + zero[start:end] * normed.astype(jnp.float32)
        start = end
    tables = []
    for e in range(experts):
        weight = jnp.sum(jnp.where(ids == e, weights, 0.0), axis=0, keepdims=True)
        tables.append(slot_rows(ids, e) * weight)
    terms = parts_of(jnp.concatenate(tables, axis=0).T)
    table_ref[...] = jnp.concatenate(terms + terms[:2], axis=1)


def based(experts, blocks, gain, ids_t, weights_t):
    count, width = ids_t.shape[1], blocks[0].shape[1]
    return pl.pallas_call(
        functools.partial(base_kernel, experts),
        out_shape=(
            jax.ShapeDtypeStruct((count, width), jnp.float32),
            jax.ShapeDtypeStruct((count, 5 * experts * CAP), jnp.bfloat16),
        ),
        in_specs=[VMEM] * (3 + len(blocks)),
        out_specs=(VMEM, VMEM),
        compiler_params=PARAMS,
        cost_estimate=pl.CostEstimate(
            flops=8 * count * width, bytes_accessed=6 * count * width, transcendentals=0
        ),
    )(gain, ids_t, weights_t, *blocks)


def end_kernel(columns, base_ref, table_ref, *refs):
    back_refs, out_ref = refs[:-1], refs[-1]
    here = pl.ds(pl.multiple_of(pl.program_id(0) * columns, columns), columns)
    total = back_refs[0][:, here].astype(jnp.float32)
    for ref in back_refs[1:]:
        total = total + ref[:, here].astype(jnp.float32)
    high, low, _ = parts_of(total)
    rows = jnp.concatenate([high, high, high, low, low], axis=0)
    added = jnp.dot(table_ref[...], rows, preferred_element_type=jnp.float32)
    out_ref[...] = (base_ref[:, here] + added).astype(jnp.bfloat16)


def ended(base, table, backs):
    count, width = base.shape
    steps = 3
    columns = width // steps
    return pl.pallas_call(
        functools.partial(end_kernel, columns),
        out_shape=jax.ShapeDtypeStruct((count, width), jnp.bfloat16),
        grid=(steps,),
        in_specs=[VMEM] * (2 + len(backs)),
        out_specs=pl.BlockSpec((count, columns), lambda i: (0, i)),
        compiler_params=PARAMS,
        cost_estimate=pl.CostEstimate(
            flops=2 * count * width * table.shape[0], bytes_accessed=6 * count * width,
            transcendentals=0,
        ),
    )(base, table, *backs)


def early_kernel(left_ref, right_ref, out_ref):
    out_ref[...] = left_ref[...].astype(jnp.float32) + right_ref[...].astype(jnp.float32)


def summed_early(left, right):
    return pl.pallas_call(
        early_kernel,
        out_shape=jax.ShapeDtypeStruct(left.shape, jnp.float32),
        in_specs=[VMEM, VMEM],
        out_specs=VMEM,
        compiler_params=PARAMS,
        cost_estimate=pl.CostEstimate(
            flops=left.size, bytes_accessed=128 * left.size, transcendentals=0
        ),
    )(left, right)


def local(blocks, norm_gain, w_gate, w_up, w_down, route_ids, route_weights):
    slice_width = w_gate.shape[2]
    slice_count = HID // slice_width
    sections = lax.axis_size("section")
    devices = lax.axis_size("expert")
    experts = devices // slice_count
    same_slice = [[e * slice_count + k for e in range(experts)] for k in range(slice_count)]
    places = slice_count // 2
    token_count, width = blocks.shape[1:]

    def moved(value, sections_on, flip, side=0):
        pairs = []
        for s in range(sections):
            for d in range(devices):
                target = d ^ (2 * flip + side)
                pairs.append((s * devices + d, (s + sections_on) % sections * devices + target))
        return lax.ppermute(value, ("section", "expert"), pairs)

    next_ids = moved(route_ids, -1, 0)[0]
    block, = loaded(blocks[0])
    picked = picked_rows(experts, jnp.swapaxes(next_ids, 0, 1), block)
    if experts > 1:
        picked = lax.all_to_all(
            picked.reshape(experts, CAP, width), "expert", split_axis=0, concat_axis=0,
            tiled=True, axis_index_groups=same_slice,
        ).reshape(experts * CAP, width)
    gate_t, up_t, down, gain = loaded(
        after(jnp.swapaxes(w_gate[0], 0, 1), picked), jnp.swapaxes(w_up[0], 0, 1), w_down[0], norm_gain
    )

    near, far = {}, {}
    near[2] = moved(picked, 1, 2)
    near[0] = moved(picked, 1, 0)
    far[0] = moved(picked, 1, 0, 1)
    far[2] = moved(after(near[2], near[0], gain), 0, 0, 1)
    near[3] = moved(after(near[2], far[0]), 0, 1)
    near[1] = moved(after(near[0], near[2]), 0, 1)
    far[3] = moved(far[2], 0, 1)
    far[1] = moved(near[1], 0, 0, 1)
    pieces = 2
    size = token_count // pieces
    arrived = [
        moved(after(blocks[0, i * size:(i + 1) * size], near[0], far[0], near[2]), 1, 0)
        for i in range(pieces)
    ]
    base, table = based(
        experts, arrived, gain, jnp.swapaxes(route_ids[0], 0, 1),
        jnp.swapaxes(route_weights[0], 0, 1),
    )

    own, other = {}, {}
    for k in (2, 3, 1, 0):
        first = {2: (gain,), 3: (other.get(2),), 1: (own.get(3),), 0: (other.get(3), base)}[k]
        own[k], sent = mlp(after(near[k], *first), far[k], gain, gate_t, up_t, down)
        other[k] = moved(sent, 0, 0, 1)
    both = {
        k: (own[k].astype(jnp.float32) + other[k].astype(jnp.float32)).astype(jnp.bfloat16)
        for k in (2, 3, 1)
    }
    early = summed_early(own[0], moved(both[2], 0, 2))
    backs = [
        early, moved(both[3], 0, 3), moved(after(both[1], early), 0, 1), other[0],
    ]
    if experts > 1:
        summed = sum(back.astype(jnp.float32) for back in backs).reshape(experts, CAP, width)
        summed = lax.all_to_all(
            summed.astype(jnp.bfloat16), "expert", split_axis=0, concat_axis=0, tiled=True,
            axis_index_groups=same_slice,
        )
        backs = [summed.reshape(experts * CAP, width)]
    return ended(base, table, backs)[None]


def solution(mesh):
    placed = (
        P("section", ("dp", "expert"), None),
        P("section", None),
        P("section", None, "expert"),
        P("section", None, "expert"),
        P("section", "expert", None),
        P("section", ("dp", "expert"), None),
        P("section", ("dp", "expert"), None),
    )
    return jax.shard_map(
        local,
        mesh=mesh,
        in_specs=placed,
        out_specs=P("section", ("dp", "expert"), None),
        check_vma=False,
    )
```

```python
import functools

import jax
import jax.numpy as jnp
from jax import lax
from jax.experimental import pallas as pl
from jax.experimental.pallas import tpu as pltpu
from jax.sharding import PartitionSpec as P

HID = 1536
CAP = 32
VMEM = pl.BlockSpec(memory_space=pltpu.VMEM)
HBM = pl.BlockSpec(memory_space=pltpu.HBM)
PARAMS = pltpu.CompilerParams(vmem_limit_bytes=24 * 1024 * 1024)


def after(value, *others):
    return lax.optimization_barrier((value, *others))[0]


def load_kernel(count, *refs):
    sources, targets, sems = refs[:count], refs[count:2 * count], refs[2 * count]
    copies = [
        pltpu.make_async_copy(a, b, sems.at[i]) for i, (a, b) in enumerate(zip(sources, targets))
    ]
    for copy in copies:
        copy.start()
    for copy in copies:
        copy.wait()


def loaded(*arrays):
    return pl.pallas_call(
        functools.partial(load_kernel, len(arrays)),
        out_shape=tuple(jax.ShapeDtypeStruct(a.shape, a.dtype) for a in arrays),
        in_specs=[HBM] * len(arrays),
        out_specs=(VMEM,) * len(arrays),
        scratch_shapes=[pltpu.SemaphoreType.DMA((len(arrays),))],
        compiler_params=PARAMS,
        cost_estimate=pl.CostEstimate(flops=0, bytes_accessed=6 * 1024 * 1024, transcendentals=0),
    )(*(pltpu.with_memory_space_constraint(a, pltpu.HBM) for a in arrays))


def slot_rows(ids, e):
    count = ids.shape[1]
    earlier = lax.broadcasted_iota(jnp.int32, (count, count), 0)
    later = lax.broadcasted_iota(jnp.int32, (count, count), 1)
    before = jnp.where(earlier < later, 1.0, 0.0).astype(jnp.bfloat16)
    slot = lax.broadcasted_iota(jnp.int32, (CAP, count), 0).astype(jnp.float32)
    hit = jnp.max(jnp.where(ids == e, 1.0, 0.0), axis=0, keepdims=True)
    hit = jnp.broadcast_to(hit, (CAP, count))
    rank = jnp.dot(hit.astype(jnp.bfloat16), before, preferred_element_type=jnp.float32)
    return jnp.where(rank == slot, hit, 0.0)


def pick_kernel(experts, ids_ref, block_ref, out_ref):
    for e in range(experts):
        table = slot_rows(ids_ref[...], e).astype(jnp.bfloat16)
        rows = jnp.dot(table, block_ref[...], preferred_element_type=jnp.float32)
        out_ref[e * CAP:(e + 1) * CAP, :] = rows.astype(jnp.bfloat16)


def picked_rows(experts, ids_t, block):
    return pl.pallas_call(
        functools.partial(pick_kernel, experts),
        out_shape=jax.ShapeDtypeStruct((experts * CAP, block.shape[1]), jnp.bfloat16),
        in_specs=[VMEM, VMEM],
        out_specs=VMEM,
        compiler_params=PARAMS,
        cost_estimate=pl.CostEstimate(
            flops=2 * experts * CAP * block.size, bytes_accessed=block.size, transcendentals=0
        ),
    )(ids_t, block)


def mlp_kernel(near_ref, far_ref, gain_ref, gate_ref, up_ref, down_ref, near_out, far_out):
    count = near_ref.shape[0]
    rows = jnp.concatenate([near_ref[...], far_ref[...]], axis=0).astype(jnp.float32)
    inverse = lax.rsqrt(jnp.mean(rows * rows, axis=-1, keepdims=True) + 1e-06)
    normed = (rows * inverse * gain_ref[...].astype(jnp.float32)).astype(jnp.bfloat16)
    across = (((1,), (1,)), ((), ()))
    gate = lax.dot_general(normed, gate_ref[...], across, preferred_element_type=jnp.float32)
    up = lax.dot_general(normed, up_ref[...], across, preferred_element_type=jnp.float32)
    hidden = (gate / (1.0 + jnp.exp(-gate)) * up).astype(jnp.bfloat16)
    partial = jnp.dot(hidden, down_ref[...], preferred_element_type=jnp.float32)
    partial = partial.astype(jnp.bfloat16)
    near_out[...] = partial[:count]
    far_out[...] = partial[count:]


def mlp(near, far, gain, gate_t, up_t, down):
    rows = 2 * near.shape[0]
    width, hidden = down.shape[1], down.shape[0]
    out = jax.ShapeDtypeStruct(near.shape, jnp.bfloat16)
    return pl.pallas_call(
        mlp_kernel,
        out_shape=(out, out),
        in_specs=[VMEM] * 6,
        out_specs=(VMEM, VMEM),
        compiler_params=PARAMS,
        cost_estimate=pl.CostEstimate(
            flops=6 * rows * width * hidden, bytes_accessed=6 * width * hidden, transcendentals=0
        ),
    )(near, far, gain, gate_t, up_t, down)


def parts_of(value):
    terms = []
    for _ in range(3):
        terms.append(value.astype(jnp.bfloat16))
        value = value - terms[-1].astype(jnp.float32)
    return terms


def base_kernel(experts, gain_ref, ids_ref, weights_ref, *refs):
    block_refs, out_ref, table_ref = refs[:-2], refs[-2], refs[-1]
    ids, weights = ids_ref[...], weights_ref[...]
    count = ids.shape[1]
    zero = jnp.sum(jnp.where(ids >= experts, weights, 0.0), axis=0, keepdims=True)
    same = lax.broadcasted_iota(jnp.int32, (count, count), 0) == lax.broadcasted_iota(
        jnp.int32, (count, count), 1
    )
    zero = jnp.sum(jnp.where(same, zero, 0.0), axis=1, keepdims=True)
    start = 0
    for ref in block_refs:
        end = start + ref.shape[0]
        rows = ref[...].astype(jnp.float32)
        inverse = lax.rsqrt(jnp.mean(rows * rows, axis=-1, keepdims=True) + 1e-06)
        normed = (rows * inverse * gain_ref[...].astype(jnp.float32)).astype(jnp.bfloat16)
        out_ref[start:end] = rows + zero[start:end] * normed.astype(jnp.float32)
        start = end
    tables = []
    for e in range(experts):
        weight = jnp.sum(jnp.where(ids == e, weights, 0.0), axis=0, keepdims=True)
        tables.append(slot_rows(ids, e) * weight)
    terms = parts_of(jnp.concatenate(tables, axis=0).T)
    table_ref[...] = jnp.concatenate(terms + terms[:2], axis=1)


def based(experts, blocks, gain, ids_t, weights_t):
    count, width = ids_t.shape[1], blocks[0].shape[1]
    return pl.pallas_call(
        functools.partial(base_kernel, experts),
        out_shape=(
            jax.ShapeDtypeStruct((count, width), jnp.float32),
            jax.ShapeDtypeStruct((count, 5 * experts * CAP), jnp.bfloat16),
        ),
        in_specs=[VMEM] * (3 + len(blocks)),
        out_specs=(VMEM, VMEM),
        compiler_params=PARAMS,
        cost_estimate=pl.CostEstimate(
            flops=8 * count * width, bytes_accessed=6 * count * width, transcendentals=0
        ),
    )(gain, ids_t, weights_t, *blocks)


def end_kernel(columns, base_ref, table_ref, *refs):
    back_refs, out_ref = refs[:-1], refs[-1]
    here = pl.ds(pl.multiple_of(pl.program_id(0) * columns, columns), columns)
    total = back_refs[0][:, here].astype(jnp.float32)
    for ref in back_refs[1:]:
        total = total + ref[:, here].astype(jnp.float32)
    high, low, _ = parts_of(total)
    rows = jnp.concatenate([high, high, high, low, low], axis=0)
    added = jnp.dot(table_ref[...], rows, preferred_element_type=jnp.float32)
    out_ref[...] = (base_ref[:, here] + added).astype(jnp.bfloat16)


def ended(base, table, backs):
    count, width = base.shape
    steps = 3
    columns = width // steps
    return pl.pallas_call(
        functools.partial(end_kernel, columns),
        out_shape=jax.ShapeDtypeStruct((count, width), jnp.bfloat16),
        grid=(steps,),
        in_specs=[VMEM] * (2 + len(backs)),
        out_specs=pl.BlockSpec((count, columns), lambda i: (0, i)),
        compiler_params=PARAMS,
        cost_estimate=pl.CostEstimate(
            flops=2 * count * width * table.shape[0], bytes_accessed=6 * count * width,
            transcendentals=0,
        ),
    )(base, table, *backs)


def early_kernel(left_ref, right_ref, out_ref):
    out_ref[...] = left_ref[...].astype(jnp.float32) + right_ref[...].astype(jnp.float32)


def summed_early(left, right):
    return pl.pallas_call(
        early_kernel,
        out_shape=jax.ShapeDtypeStruct(left.shape, jnp.float32),
        in_specs=[VMEM, VMEM],
        out_specs=VMEM,
        compiler_params=PARAMS,
        cost_estimate=pl.CostEstimate(
            flops=left.size, bytes_accessed=128 * left.size, transcendentals=0
        ),
    )(left, right)


def local(blocks, norm_gain, w_gate, w_up, w_down, route_ids, route_weights):
    slice_width = w_gate.shape[2]
    slice_count = HID // slice_width
    sections = lax.axis_size("section")
    devices = lax.axis_size("expert")
    experts = devices // slice_count
    same_slice = [[e * slice_count + k for e in range(experts)] for k in range(slice_count)]
    places = slice_count // 2
    token_count, width = blocks.shape[1:]

    def moved(value, sections_on, flip, side=0):
        pairs = []
        for s in range(sections):
            for d in range(devices):
                target = d ^ (2 * flip + side)
                pairs.append((s * devices + d, (s + sections_on) % sections * devices + target))
        return lax.ppermute(value, ("section", "expert"), pairs)

    next_ids = moved(route_ids, -1, 0)[0]
    block, = loaded(blocks[0])
    picked = picked_rows(experts, jnp.swapaxes(next_ids, 0, 1), block)
    if experts > 1:
        picked = lax.all_to_all(
            picked.reshape(experts, CAP, width), "expert", split_axis=0, concat_axis=0,
            tiled=True, axis_index_groups=same_slice,
        ).reshape(experts * CAP, width)
    gate_t, up_t, down, gain = loaded(
        after(jnp.swapaxes(w_gate[0], 0, 1), picked), jnp.swapaxes(w_up[0], 0, 1), w_down[0], norm_gain
    )

    near, far = {}, {}
    near[2] = moved(picked, 1, 2)
    near[0] = moved(picked, 1, 0)
    far[0] = moved(picked, 1, 0, 1)
    far[2] = moved(after(near[2], near[0], gain), 0, 0, 1)
    near[1] = moved(near[0], 0, 1)
    near[3] = moved(after(near[2], far[0]), 0, 1)
    far[3] = moved(far[2], 0, 1)
    far[1] = moved(near[1], 0, 0, 1)
    pieces = 2
    size = token_count // pieces
    arrived = [
        moved(after(blocks[0, i * size:(i + 1) * size], near[0], far[0], near[2]), 1, 0)
        for i in range(pieces)
    ]
    base, table = based(
        experts, arrived, gain, jnp.swapaxes(route_ids[0], 0, 1),
        jnp.swapaxes(route_weights[0], 0, 1),
    )

    own, other = {}, {}
    for k in (2, 3, 1, 0):
        first = {2: (gain,), 3: (other.get(2), arrived[0]), 1: (own.get(3),), 0: (other.get(3), base)}[k]
        own[k], sent = mlp(after(near[k], *first), far[k], gain, gate_t, up_t, down)
        other[k] = moved(sent, 0, 0, 1)
    both = {
        k: (own[k].astype(jnp.float32) + other[k].astype(jnp.float32)).astype(jnp.bfloat16)
        for k in (2, 3, 1)
    }
    early = summed_early(own[0], moved(both[2], 0, 2))
    backs = [
        early, moved(both[3], 0, 3), moved(after(both[1], early), 0, 1), other[0],
    ]
    if experts > 1:
        summed = sum(back.astype(jnp.float32) for back in backs).reshape(experts, CAP, width)
        summed = lax.all_to_all(
            summed.astype(jnp.bfloat16), "expert", split_axis=0, concat_axis=0, tiled=True,
            axis_index_groups=same_slice,
        )
        backs = [summed.reshape(experts * CAP, width)]
    return ended(base, table, backs)[None]


def solution(mesh):
    placed = (
        P("section", ("dp", "expert"), None),
        P("section", None),
        P("section", None, "expert"),
        P("section", None, "expert"),
        P("section", "expert", None),
        P("section", ("dp", "expert"), None),
        P("section", ("dp", "expert"), None),
    )
    return jax.shard_map(
        local,
        mesh=mesh,
        in_specs=placed,
        out_specs=P("section", ("dp", "expert"), None),
        check_vma=False,
    )
```

```python
import functools

import jax
import jax.numpy as jnp
from jax import lax
from jax.experimental import pallas as pl
from jax.experimental.pallas import tpu as pltpu
from jax.sharding import PartitionSpec as P

HID = 1536
CAP = 32
VMEM = pl.BlockSpec(memory_space=pltpu.VMEM)
HBM = pl.BlockSpec(memory_space=pltpu.HBM)
PARAMS = pltpu.CompilerParams(vmem_limit_bytes=24 * 1024 * 1024)


def after(value, *others):
    return lax.optimization_barrier((value, *others))[0]


def load_kernel(count, *refs):
    sources, targets, sems = refs[:count], refs[count:2 * count], refs[2 * count]
    copies = [
        pltpu.make_async_copy(a, b, sems.at[i]) for i, (a, b) in enumerate(zip(sources, targets))
    ]
    for copy in copies:
        copy.start()
    for copy in copies:
        copy.wait()


def loaded(*arrays):
    return pl.pallas_call(
        functools.partial(load_kernel, len(arrays)),
        out_shape=tuple(jax.ShapeDtypeStruct(a.shape, a.dtype) for a in arrays),
        in_specs=[HBM] * len(arrays),
        out_specs=(VMEM,) * len(arrays),
        scratch_shapes=[pltpu.SemaphoreType.DMA((len(arrays),))],
        compiler_params=PARAMS,
        cost_estimate=pl.CostEstimate(flops=0, bytes_accessed=6 * 1024 * 1024, transcendentals=0),
    )(*(pltpu.with_memory_space_constraint(a, pltpu.HBM) for a in arrays))


def slot_rows(ids, e):
    count = ids.shape[1]
    earlier = lax.broadcasted_iota(jnp.int32, (count, count), 0)
    later = lax.broadcasted_iota(jnp.int32, (count, count), 1)
    before = jnp.where(earlier < later, 1.0, 0.0).astype(jnp.bfloat16)
    slot = lax.broadcasted_iota(jnp.int32, (CAP, count), 0).astype(jnp.float32)
    hit = jnp.max(jnp.where(ids == e, 1.0, 0.0), axis=0, keepdims=True)
    hit = jnp.broadcast_to(hit, (CAP, count))
    rank = jnp.dot(hit.astype(jnp.bfloat16), before, preferred_element_type=jnp.float32)
    return jnp.where(rank == slot, hit, 0.0)


def pick_kernel(experts, ids_ref, block_ref, out_ref):
    for e in range(experts):
        table = slot_rows(ids_ref[...], e).astype(jnp.bfloat16)
        rows = jnp.dot(table, block_ref[...], preferred_element_type=jnp.float32)
        out_ref[e * CAP:(e + 1) * CAP, :] = rows.astype(jnp.bfloat16)


def picked_rows(experts, ids_t, block):
    return pl.pallas_call(
        functools.partial(pick_kernel, experts),
        out_shape=jax.ShapeDtypeStruct((experts * CAP, block.shape[1]), jnp.bfloat16),
        in_specs=[VMEM, VMEM],
        out_specs=VMEM,
        compiler_params=PARAMS,
        cost_estimate=pl.CostEstimate(
            flops=2 * experts * CAP * block.size, bytes_accessed=block.size, transcendentals=0
        ),
    )(ids_t, block)


def mlp_kernel(near_ref, far_ref, gain_ref, gate_ref, up_ref, down_ref, near_out, far_out):
    count = near_ref.shape[0]
    rows = jnp.concatenate([near_ref[...], far_ref[...]], axis=0).astype(jnp.float32)
    inverse = lax.rsqrt(jnp.mean(rows * rows, axis=-1, keepdims=True) + 1e-06)
    normed = (rows * inverse * gain_ref[...].astype(jnp.float32)).astype(jnp.bfloat16)
    across = (((1,), (1,)), ((), ()))
    gate = lax.dot_general(normed, gate_ref[...], across, preferred_element_type=jnp.float32)
    up = lax.dot_general(normed, up_ref[...], across, preferred_element_type=jnp.float32)
    hidden = (gate / (1.0 + jnp.exp(-gate)) * up).astype(jnp.bfloat16)
    partial = jnp.dot(hidden, down_ref[...], preferred_element_type=jnp.float32)
    partial = partial.astype(jnp.bfloat16)
    near_out[...] = partial[:count]
    far_out[...] = partial[count:]


def mlp(near, far, gain, gate_t, up_t, down):
    rows = 2 * near.shape[0]
    width, hidden = down.shape[1], down.shape[0]
    out = jax.ShapeDtypeStruct(near.shape, jnp.bfloat16)
    return pl.pallas_call(
        mlp_kernel,
        out_shape=(out, out),
        in_specs=[VMEM] * 6,
        out_specs=(VMEM, VMEM),
        compiler_params=PARAMS,
        cost_estimate=pl.CostEstimate(
            flops=6 * rows * width * hidden, bytes_accessed=6 * width * hidden, transcendentals=0
        ),
    )(near, far, gain, gate_t, up_t, down)


def parts_of(value):
    terms = []
    for _ in range(3):
        terms.append(value.astype(jnp.bfloat16))
        value = value - terms[-1].astype(jnp.float32)
    return terms


def base_kernel(experts, gain_ref, ids_ref, weights_ref, *refs):
    block_refs, out_ref, table_ref = refs[:-2], refs[-2], refs[-1]
    ids, weights = ids_ref[...], weights_ref[...]
    count = ids.shape[1]
    zero = jnp.sum(jnp.where(ids >= experts, weights, 0.0), axis=0, keepdims=True)
    same = lax.broadcasted_iota(jnp.int32, (count, count), 0) == lax.broadcasted_iota(
        jnp.int32, (count, count), 1
    )
    zero = jnp.sum(jnp.where(same, zero, 0.0), axis=1, keepdims=True)
    start = 0
    for ref in block_refs:
        end = start + ref.shape[0]
        rows = ref[...].astype(jnp.float32)
        inverse = lax.rsqrt(jnp.mean(rows * rows, axis=-1, keepdims=True) + 1e-06)
        normed = (rows * inverse * gain_ref[...].astype(jnp.float32)).astype(jnp.bfloat16)
        out_ref[start:end] = rows + zero[start:end] * normed.astype(jnp.float32)
        start = end
    tables = []
    for e in range(experts):
        weight = jnp.sum(jnp.where(ids == e, weights, 0.0), axis=0, keepdims=True)
        tables.append(slot_rows(ids, e) * weight)
    terms = parts_of(jnp.concatenate(tables, axis=0).T)
    table_ref[...] = jnp.concatenate(terms + terms[:2], axis=1)


def based(experts, blocks, gain, ids_t, weights_t):
    count, width = ids_t.shape[1], blocks[0].shape[1]
    return pl.pallas_call(
        functools.partial(base_kernel, experts),
        out_shape=(
            jax.ShapeDtypeStruct((count, width), jnp.float32),
            jax.ShapeDtypeStruct((count, 5 * experts * CAP), jnp.bfloat16),
        ),
        in_specs=[VMEM] * (3 + len(blocks)),
        out_specs=(VMEM, VMEM),
        compiler_params=PARAMS,
        cost_estimate=pl.CostEstimate(
            flops=8 * count * width, bytes_accessed=6 * count * width, transcendentals=0
        ),
    )(gain, ids_t, weights_t, *blocks)


def end_kernel(columns, base_ref, table_ref, *refs):
    back_refs, out_ref = refs[:-1], refs[-1]
    here = pl.ds(pl.multiple_of(pl.program_id(0) * columns, columns), columns)
    total = back_refs[0][:, here].astype(jnp.float32)
    for ref in back_refs[1:]:
        total = total + ref[:, here].astype(jnp.float32)
    high, low, _ = parts_of(total)
    rows = jnp.concatenate([high, high, high, low, low], axis=0)
    added = jnp.dot(table_ref[...], rows, preferred_element_type=jnp.float32)
    out_ref[...] = (base_ref[:, here] + added).astype(jnp.bfloat16)


def ended(base, table, backs):
    count, width = base.shape
    steps = 3
    columns = width // steps
    return pl.pallas_call(
        functools.partial(end_kernel, columns),
        out_shape=jax.ShapeDtypeStruct((count, width), jnp.bfloat16),
        grid=(steps,),
        in_specs=[VMEM] * (2 + len(backs)),
        out_specs=pl.BlockSpec((count, columns), lambda i: (0, i)),
        compiler_params=PARAMS,
        cost_estimate=pl.CostEstimate(
            flops=2 * count * width * table.shape[0], bytes_accessed=6 * count * width,
            transcendentals=0,
        ),
    )(base, table, *backs)


def early_kernel(left_ref, right_ref, out_ref):
    out_ref[...] = left_ref[...].astype(jnp.float32) + right_ref[...].astype(jnp.float32)


def summed_early(left, right):
    return pl.pallas_call(
        early_kernel,
        out_shape=jax.ShapeDtypeStruct(left.shape, jnp.float32),
        in_specs=[VMEM, VMEM],
        out_specs=VMEM,
        compiler_params=PARAMS,
        cost_estimate=pl.CostEstimate(
            flops=left.size, bytes_accessed=128 * left.size, transcendentals=0
        ),
    )(left, right)


def local(blocks, norm_gain, w_gate, w_up, w_down, route_ids, route_weights):
    slice_width = w_gate.shape[2]
    slice_count = HID // slice_width
    sections = lax.axis_size("section")
    devices = lax.axis_size("expert")
    experts = devices // slice_count
    same_slice = [[e * slice_count + k for e in range(experts)] for k in range(slice_count)]
    places = slice_count // 2
    token_count, width = blocks.shape[1:]

    def moved(value, sections_on, flip, side=0):
        pairs = []
        for s in range(sections):
            for d in range(devices):
                target = d ^ (2 * flip + side)
                pairs.append((s * devices + d, (s + sections_on) % sections * devices + target))
        return lax.ppermute(value, ("section", "expert"), pairs)

    next_ids = moved(route_ids, -1, 0)[0]
    block, = loaded(blocks[0])
    picked = picked_rows(experts, jnp.swapaxes(next_ids, 0, 1), block)
    if experts > 1:
        picked = lax.all_to_all(
            picked.reshape(experts, CAP, width), "expert", split_axis=0, concat_axis=0,
            tiled=True, axis_index_groups=same_slice,
        ).reshape(experts * CAP, width)
    gate_t, up_t, down, gain = loaded(
        after(jnp.swapaxes(w_gate[0], 0, 1), picked), jnp.swapaxes(w_up[0], 0, 1), w_down[0], norm_gain
    )

    near, far = {}, {}
    near[2] = moved(picked, 1, 2)
    near[0] = moved(picked, 1, 0)
    far[0] = moved(picked, 1, 0, 1)
    far[2] = moved(after(near[2], near[0], gain), 0, 0, 1)
    near[1] = moved(near[0], 0, 1)
    near[3] = moved(after(near[2], far[0]), 0, 1)
    far[3] = moved(far[2], 0, 1)
    far[1] = moved(near[1], 0, 0, 1)
    pieces = 2
    size = token_count // pieces
    arrived = [
        moved(after(blocks[0, i * size:(i + 1) * size], near[0], far[0], near[2]), 1, 0)
        for i in range(pieces)
    ]
    base, table = based(
        experts, arrived, gain, jnp.swapaxes(route_ids[0], 0, 1),
        jnp.swapaxes(route_weights[0], 0, 1),
    )

    own, other = {}, {}
    for k in (2, 3, 1, 0):
        first = {2: (gain,), 3: (other.get(2), arrived[0]), 1: (own.get(3),), 0: (own.get(3),)}[k]
        own[k], sent = mlp(after(near[k], *first), far[k], gain, gate_t, up_t, down)
        other[k] = moved(sent, 0, 0, 1)
    both = {
        k: (own[k].astype(jnp.float32) + other[k].astype(jnp.float32)).astype(jnp.bfloat16)
        for k in (2, 3, 1)
    }
    early = summed_early(own[0], moved(both[2], 0, 2))
    backs = [
        early, moved(both[3], 0, 3), moved(after(both[1], base), 0, 1), other[0],
    ]
    if experts > 1:
        summed = sum(back.astype(jnp.float32) for back in backs).reshape(experts, CAP, width)
        summed = lax.all_to_all(
            summed.astype(jnp.bfloat16), "expert", split_axis=0, concat_axis=0, tiled=True,
            axis_index_groups=same_slice,
        )
        backs = [summed.reshape(experts * CAP, width)]
    return ended(base, table, backs)[None]


def solution(mesh):
    placed = (
        P("section", ("dp", "expert"), None),
        P("section", None),
        P("section", None, "expert"),
        P("section", None, "expert"),
        P("section", "expert", None),
        P("section", ("dp", "expert"), None),
        P("section", ("dp", "expert"), None),
    )
    return jax.shard_map(
        local,
        mesh=mesh,
        in_specs=placed,
        out_specs=P("section", ("dp", "expert"), None),
        check_vma=False,
    )
```

```python
import functools

import jax
import jax.numpy as jnp
from jax import lax
from jax.experimental import pallas as pl
from jax.experimental.pallas import tpu as pltpu
from jax.sharding import PartitionSpec as P

HID = 1536
CAP = 32
VMEM = pl.BlockSpec(memory_space=pltpu.VMEM)
HBM = pl.BlockSpec(memory_space=pltpu.HBM)
PARAMS = pltpu.CompilerParams(vmem_limit_bytes=24 * 1024 * 1024)


def after(value, *others):
    return lax.optimization_barrier((value, *others))[0]


def load_kernel(count, *refs):
    sources, targets, sems = refs[:count], refs[count:2 * count], refs[2 * count]
    copies = [
        pltpu.make_async_copy(a, b, sems.at[i]) for i, (a, b) in enumerate(zip(sources, targets))
    ]
    for copy in copies:
        copy.start()
    for copy in copies:
        copy.wait()


def loaded(*arrays):
    return pl.pallas_call(
        functools.partial(load_kernel, len(arrays)),
        out_shape=tuple(jax.ShapeDtypeStruct(a.shape, a.dtype) for a in arrays),
        in_specs=[HBM] * len(arrays),
        out_specs=(VMEM,) * len(arrays),
        scratch_shapes=[pltpu.SemaphoreType.DMA((len(arrays),))],
        compiler_params=PARAMS,
        cost_estimate=pl.CostEstimate(flops=0, bytes_accessed=6 * 1024 * 1024, transcendentals=0),
    )(*(pltpu.with_memory_space_constraint(a, pltpu.HBM) for a in arrays))


def slot_rows(ids, e):
    count = ids.shape[1]
    earlier = lax.broadcasted_iota(jnp.int32, (count, count), 0)
    later = lax.broadcasted_iota(jnp.int32, (count, count), 1)
    before = jnp.where(earlier < later, 1.0, 0.0).astype(jnp.bfloat16)
    slot = lax.broadcasted_iota(jnp.int32, (CAP, count), 0).astype(jnp.float32)
    hit = jnp.max(jnp.where(ids == e, 1.0, 0.0), axis=0, keepdims=True)
    hit = jnp.broadcast_to(hit, (CAP, count))
    rank = jnp.dot(hit.astype(jnp.bfloat16), before, preferred_element_type=jnp.float32)
    return jnp.where(rank == slot, hit, 0.0)


def pick_kernel(experts, ids_ref, block_ref, out_ref):
    for e in range(experts):
        table = slot_rows(ids_ref[...], e).astype(jnp.bfloat16)
        rows = jnp.dot(table, block_ref[...], preferred_element_type=jnp.float32)
        out_ref[e * CAP:(e + 1) * CAP, :] = rows.astype(jnp.bfloat16)


def picked_rows(experts, ids_t, block):
    return pl.pallas_call(
        functools.partial(pick_kernel, experts),
        out_shape=jax.ShapeDtypeStruct((experts * CAP, block.shape[1]), jnp.bfloat16),
        in_specs=[VMEM, VMEM],
        out_specs=VMEM,
        compiler_params=PARAMS,
        cost_estimate=pl.CostEstimate(
            flops=2 * experts * CAP * block.size, bytes_accessed=block.size, transcendentals=0
        ),
    )(ids_t, block)


def mlp_kernel(near_ref, far_ref, gain_ref, gate_ref, up_ref, down_ref, near_out, far_out):
    count = near_ref.shape[0]
    rows = jnp.concatenate([near_ref[...], far_ref[...]], axis=0).astype(jnp.float32)
    inverse = lax.rsqrt(jnp.mean(rows * rows, axis=-1, keepdims=True) + 1e-06)
    normed = (rows * inverse * gain_ref[...].astype(jnp.float32)).astype(jnp.bfloat16)
    across = (((1,), (1,)), ((), ()))
    gate = lax.dot_general(normed, gate_ref[...], across, preferred_element_type=jnp.float32)
    up = lax.dot_general(normed, up_ref[...], across, preferred_element_type=jnp.float32)
    hidden = (gate / (1.0 + jnp.exp(-gate)) * up).astype(jnp.bfloat16)
    partial = jnp.dot(hidden, down_ref[...], preferred_element_type=jnp.float32)
    partial = partial.astype(jnp.bfloat16)
    near_out[...] = partial[:count]
    far_out[...] = partial[count:]


def mlp(near, far, gain, gate_t, up_t, down):
    rows = 2 * near.shape[0]
    width, hidden = down.shape[1], down.shape[0]
    out = jax.ShapeDtypeStruct(near.shape, jnp.bfloat16)
    return pl.pallas_call(
        mlp_kernel,
        out_shape=(out, out),
        in_specs=[VMEM] * 6,
        out_specs=(VMEM, VMEM),
        compiler_params=PARAMS,
        cost_estimate=pl.CostEstimate(
            flops=6 * rows * width * hidden, bytes_accessed=6 * width * hidden, transcendentals=0
        ),
    )(near, far, gain, gate_t, up_t, down)


def parts_of(value):
    terms = []
    for _ in range(3):
        terms.append(value.astype(jnp.bfloat16))
        value = value - terms[-1].astype(jnp.float32)
    return terms


def base_kernel(experts, gain_ref, ids_ref, weights_ref, *refs):
    block_refs, (out_ref, table_ref, pick_ref) = refs[:-3], refs[-3:]
    ids, weights = ids_ref[...], weights_ref[...]
    count = ids.shape[1]
    zero = jnp.sum(jnp.where(ids >= experts, weights, 0.0), axis=0, keepdims=True)
    same = lax.broadcasted_iota(jnp.int32, (count, count), 0) == lax.broadcasted_iota(
        jnp.int32, (count, count), 1
    )
    zero = jnp.sum(jnp.where(same, zero, 0.0), axis=1, keepdims=True)
    start = 0
    for ref in block_refs:
        end = start + ref.shape[0]
        rows = ref[...].astype(jnp.float32)
        inverse = lax.rsqrt(jnp.mean(rows * rows, axis=-1, keepdims=True) + 1e-06)
        normed = (rows * inverse * gain_ref[...].astype(jnp.float32)).astype(jnp.bfloat16)
        out_ref[start:end] = rows + zero[start:end] * normed.astype(jnp.float32)
        start = end
    tables = []
    for e in range(experts):
        weight = jnp.sum(jnp.where(ids == e, weights, 0.0), axis=0, keepdims=True)
        slots = slot_rows(ids, e)
        tables.append(slots * weight)
        start, total = 0, 0.0
        for ref in block_refs:
            end = start + ref.shape[0]
            part = slots[:, start:end].astype(jnp.bfloat16)
            total += jnp.dot(part, ref[...], preferred_element_type=jnp.float32)
            start = end
        pick_ref[e * CAP:(e + 1) * CAP, :] = total.astype(jnp.bfloat16)
    terms = parts_of(jnp.concatenate(tables, axis=0).T)
    table_ref[...] = jnp.concatenate(terms + terms[:2], axis=1)


def based(experts, blocks, gain, ids_t, weights_t):
    count, width = ids_t.shape[1], blocks[0].shape[1]
    return pl.pallas_call(
        functools.partial(base_kernel, experts),
        out_shape=(
            jax.ShapeDtypeStruct((count, width), jnp.float32),
            jax.ShapeDtypeStruct((count, 5 * experts * CAP), jnp.bfloat16),
            jax.ShapeDtypeStruct((experts * CAP, width), jnp.bfloat16),
        ),
        in_specs=[VMEM] * (3 + len(blocks)),
        out_specs=(VMEM, VMEM, VMEM),
        compiler_params=PARAMS,
        cost_estimate=pl.CostEstimate(
            flops=8 * count * width, bytes_accessed=6 * count * width, transcendentals=0
        ),
    )(gain, ids_t, weights_t, *blocks)


def end_kernel(columns, base_ref, table_ref, *refs):
    back_refs, out_ref = refs[:-1], refs[-1]
    here = pl.ds(pl.multiple_of(pl.program_id(0) * columns, columns), columns)
    total = back_refs[0][:, here].astype(jnp.float32)
    for ref in back_refs[1:]:
        total = total + ref[:, here].astype(jnp.float32)
    high, low, _ = parts_of(total)
    rows = jnp.concatenate([high, high, high, low, low], axis=0)
    added = jnp.dot(table_ref[...], rows, preferred_element_type=jnp.float32)
    out_ref[...] = (base_ref[:, here] + added).astype(jnp.bfloat16)


def ended(base, table, backs):
    count, width = base.shape
    steps = 3
    columns = width // steps
    return pl.pallas_call(
        functools.partial(end_kernel, columns),
        out_shape=jax.ShapeDtypeStruct((count, width), jnp.bfloat16),
        grid=(steps,),
        in_specs=[VMEM] * (2 + len(backs)),
        out_specs=pl.BlockSpec((count, columns), lambda i: (0, i)),
        compiler_params=PARAMS,
        cost_estimate=pl.CostEstimate(
            flops=2 * count * width * table.shape[0], bytes_accessed=6 * count * width,
            transcendentals=0,
        ),
    )(base, table, *backs)


def early_kernel(left_ref, right_ref, out_ref):
    out_ref[...] = left_ref[...].astype(jnp.float32) + right_ref[...].astype(jnp.float32)


def summed_early(left, right):
    return pl.pallas_call(
        early_kernel,
        out_shape=jax.ShapeDtypeStruct(left.shape, jnp.float32),
        in_specs=[VMEM, VMEM],
        out_specs=VMEM,
        compiler_params=PARAMS,
        cost_estimate=pl.CostEstimate(
            flops=left.size, bytes_accessed=128 * left.size, transcendentals=0
        ),
    )(left, right)


def local(blocks, norm_gain, w_gate, w_up, w_down, route_ids, route_weights):
    slice_width = w_gate.shape[2]
    slice_count = HID // slice_width
    sections = lax.axis_size("section")
    devices = lax.axis_size("expert")
    experts = devices // slice_count
    same_slice = [[e * slice_count + k for e in range(experts)] for k in range(slice_count)]
    places = slice_count // 2
    token_count, width = blocks.shape[1:]

    def moved(value, sections_on, flip, side=0):
        pairs = []
        for s in range(sections):
            for d in range(devices):
                target = d ^ (2 * flip + side)
                pairs.append((s * devices + d, (s + sections_on) % sections * devices + target))
        return lax.ppermute(value, ("section", "expert"), pairs)

    def exchanged(rows):
        rows = rows.reshape(experts, CAP, width)
        return lax.all_to_all(
            rows, "expert", split_axis=0, concat_axis=0, tiled=True, axis_index_groups=same_slice
        ).reshape(experts * CAP, width)

    next_ids = moved(route_ids, -1, 0)[0]
    block, = loaded(blocks[0])
    picked = picked_rows(experts, jnp.swapaxes(next_ids, 0, 1), block)
    if experts > 1:
        picked = exchanged(picked)
    gate_t, up_t, down, gain = loaded(
        after(jnp.swapaxes(w_gate[0], 0, 1), picked), jnp.swapaxes(w_up[0], 0, 1), w_down[0], norm_gain
    )

    near, far = {}, {}
    near[2] = moved(picked, 1, 2)
    near[1] = moved(picked, 1, 1)
    far[0] = moved(picked, 1, 0, 1)
    far[2] = moved(after(near[2], gain), 0, 0, 1)
    far[1] = moved(near[1], 0, 0, 1)
    near[3] = moved(after(near[2], far[0], near[1]), 0, 1)
    far[3] = moved(far[2], 0, 1)
    pieces = 2
    size = token_count // pieces
    arrived = [
        moved(after(blocks[0, i * size:(i + 1) * size], near[1], far[0], near[2]), 1, 0)
        for i in range(pieces)
    ]
    base, table, near[0] = based(
        experts, arrived, gain, jnp.swapaxes(route_ids[0], 0, 1),
        jnp.swapaxes(route_weights[0], 0, 1),
    )

    if experts > 1:
        near[0] = exchanged(near[0])
    own, other = {}, {}
    for k in (2, 3, 1, 0):
        first = {2: (gain,), 3: (other.get(2), arrived[0], far[1]), 1: (own.get(3),), 0: (own.get(1),)}[k]
        own[k], sent = mlp(after(near[k], *first), far[k], gain, gate_t, up_t, down)
        other[k] = moved(sent, 0, 0, 1)
    both = {
        k: (own[k].astype(jnp.float32) + other[k].astype(jnp.float32)).astype(jnp.bfloat16)
        for k in (2, 3, 1)
    }
    early = summed_early(own[0], moved(both[2], 0, 2))
    backs = [
        early, moved(both[3], 0, 3), moved(after(both[1], early), 0, 1), other[0],
    ]
    if experts > 1:
        backs = [exchanged(sum(back.astype(jnp.float32) for back in backs).astype(jnp.bfloat16))]
    return ended(base, table, backs)[None]


def solution(mesh):
    placed = (
        P("section", ("dp", "expert"), None),
        P("section", None),
        P("section", None, "expert"),
        P("section", None, "expert"),
        P("section", "expert", None),
        P("section", ("dp", "expert"), None),
        P("section", ("dp", "expert"), None),
    )
    return jax.shard_map(
        local,
        mesh=mesh,
        in_specs=placed,
        out_specs=P("section", ("dp", "expert"), None),
        check_vma=False,
    )
```

```python
import functools

import jax
import jax.numpy as jnp
from jax import lax
from jax.experimental import pallas as pl
from jax.experimental.pallas import tpu as pltpu
from jax.sharding import PartitionSpec as P

HID = 1536
CAP = 32
VMEM = pl.BlockSpec(memory_space=pltpu.VMEM)
HBM = pl.BlockSpec(memory_space=pltpu.HBM)
PARAMS = pltpu.CompilerParams(vmem_limit_bytes=24 * 1024 * 1024)


def after(value, *others):
    return lax.optimization_barrier((value, *others))[0]


def load_kernel(count, *refs):
    sources, targets, sems = refs[:count], refs[count:2 * count], refs[2 * count]
    copies = [
        pltpu.make_async_copy(a, b, sems.at[i]) for i, (a, b) in enumerate(zip(sources, targets))
    ]
    for copy in copies:
        copy.start()
    for copy in copies:
        copy.wait()


def loaded(*arrays):
    return pl.pallas_call(
        functools.partial(load_kernel, len(arrays)),
        out_shape=tuple(jax.ShapeDtypeStruct(a.shape, a.dtype) for a in arrays),
        in_specs=[HBM] * len(arrays),
        out_specs=(VMEM,) * len(arrays),
        scratch_shapes=[pltpu.SemaphoreType.DMA((len(arrays),))],
        compiler_params=PARAMS,
        cost_estimate=pl.CostEstimate(flops=0, bytes_accessed=6 * 1024 * 1024, transcendentals=0),
    )(*(pltpu.with_memory_space_constraint(a, pltpu.HBM) for a in arrays))


def slot_rows(ids, e):
    count = ids.shape[1]
    earlier = lax.broadcasted_iota(jnp.int32, (count, count), 0)
    later = lax.broadcasted_iota(jnp.int32, (count, count), 1)
    before = jnp.where(earlier < later, 1.0, 0.0).astype(jnp.bfloat16)
    slot = lax.broadcasted_iota(jnp.int32, (CAP, count), 0).astype(jnp.float32)
    hit = jnp.max(jnp.where(ids == e, 1.0, 0.0), axis=0, keepdims=True)
    hit = jnp.broadcast_to(hit, (CAP, count))
    rank = jnp.dot(hit.astype(jnp.bfloat16), before, preferred_element_type=jnp.float32)
    return jnp.where(rank == slot, hit, 0.0)


def pick_kernel(experts, ids_ref, block_ref, out_ref):
    for e in range(experts):
        table = slot_rows(ids_ref[...], e).astype(jnp.bfloat16)
        rows = jnp.dot(table, block_ref[...], preferred_element_type=jnp.float32)
        out_ref[e * CAP:(e + 1) * CAP, :] = rows.astype(jnp.bfloat16)


def picked_rows(experts, ids_t, block):
    return pl.pallas_call(
        functools.partial(pick_kernel, experts),
        out_shape=jax.ShapeDtypeStruct((experts * CAP, block.shape[1]), jnp.bfloat16),
        in_specs=[VMEM, VMEM],
        out_specs=VMEM,
        compiler_params=PARAMS,
        cost_estimate=pl.CostEstimate(
            flops=2 * experts * CAP * block.size, bytes_accessed=block.size, transcendentals=0
        ),
    )(ids_t, block)


def mlp_kernel(near_ref, far_ref, gain_ref, gate_ref, up_ref, down_ref, near_out, far_out):
    count = near_ref.shape[0]
    rows = jnp.concatenate([near_ref[...], far_ref[...]], axis=0).astype(jnp.float32)
    inverse = lax.rsqrt(jnp.mean(rows * rows, axis=-1, keepdims=True) + 1e-06)
    normed = (rows * inverse * gain_ref[...].astype(jnp.float32)).astype(jnp.bfloat16)
    across = (((1,), (1,)), ((), ()))
    gate = lax.dot_general(normed, gate_ref[...], across, preferred_element_type=jnp.float32)
    up = lax.dot_general(normed, up_ref[...], across, preferred_element_type=jnp.float32)
    hidden = (gate / (1.0 + jnp.exp(-gate)) * up).astype(jnp.bfloat16)
    partial = jnp.dot(hidden, down_ref[...], preferred_element_type=jnp.float32)
    partial = partial.astype(jnp.bfloat16)
    near_out[...] = partial[:count]
    far_out[...] = partial[count:]


def mlp(near, far, gain, gate_t, up_t, down):
    rows = 2 * near.shape[0]
    width, hidden = down.shape[1], down.shape[0]
    out = jax.ShapeDtypeStruct(near.shape, jnp.bfloat16)
    return pl.pallas_call(
        mlp_kernel,
        out_shape=(out, out),
        in_specs=[VMEM] * 6,
        out_specs=(VMEM, VMEM),
        compiler_params=PARAMS,
        cost_estimate=pl.CostEstimate(
            flops=6 * rows * width * hidden, bytes_accessed=6 * width * hidden, transcendentals=0
        ),
    )(near, far, gain, gate_t, up_t, down)


def parts_of(value):
    terms = []
    for _ in range(3):
        terms.append(value.astype(jnp.bfloat16))
        value = value - terms[-1].astype(jnp.float32)
    return terms


def base_kernel(experts, gain_ref, ids_ref, weights_ref, *refs):
    block_refs, (out_ref, table_ref, pick_ref) = refs[:-3], refs[-3:]
    ids, weights = ids_ref[...], weights_ref[...]
    count = ids.shape[1]
    zero = jnp.sum(jnp.where(ids >= experts, weights, 0.0), axis=0, keepdims=True)
    same = lax.broadcasted_iota(jnp.int32, (count, count), 0) == lax.broadcasted_iota(
        jnp.int32, (count, count), 1
    )
    zero = jnp.sum(jnp.where(same, zero, 0.0), axis=1, keepdims=True)
    start = 0
    for ref in block_refs:
        end = start + ref.shape[0]
        rows = ref[...].astype(jnp.float32)
        inverse = lax.rsqrt(jnp.mean(rows * rows, axis=-1, keepdims=True) + 1e-06)
        normed = (rows * inverse * gain_ref[...].astype(jnp.float32)).astype(jnp.bfloat16)
        out_ref[start:end] = rows + zero[start:end] * normed.astype(jnp.float32)
        start = end
    tables = []
    for e in range(experts):
        weight = jnp.sum(jnp.where(ids == e, weights, 0.0), axis=0, keepdims=True)
        slots = slot_rows(ids, e)
        tables.append(slots * weight)
        start, total = 0, 0.0
        for ref in block_refs:
            end = start + ref.shape[0]
            part = slots[:, start:end].astype(jnp.bfloat16)
            total += jnp.dot(part, ref[...], preferred_element_type=jnp.float32)
            start = end
        pick_ref[e * CAP:(e + 1) * CAP, :] = total.astype(jnp.bfloat16)
    terms = parts_of(jnp.concatenate(tables, axis=0).T)
    table_ref[...] = jnp.concatenate(terms + terms[:2], axis=1)


def based(experts, blocks, gain, ids_t, weights_t):
    count, width = ids_t.shape[1], blocks[0].shape[1]
    return pl.pallas_call(
        functools.partial(base_kernel, experts),
        out_shape=(
            jax.ShapeDtypeStruct((count, width), jnp.float32),
            jax.ShapeDtypeStruct((count, 5 * experts * CAP), jnp.bfloat16),
            jax.ShapeDtypeStruct((experts * CAP, width), jnp.bfloat16),
        ),
        in_specs=[VMEM] * (3 + len(blocks)),
        out_specs=(VMEM, VMEM, VMEM),
        compiler_params=PARAMS,
        cost_estimate=pl.CostEstimate(
            flops=8 * count * width, bytes_accessed=6 * count * width, transcendentals=0
        ),
    )(gain, ids_t, weights_t, *blocks)


def end_kernel(columns, base_ref, table_ref, *refs):
    back_refs, out_ref = refs[:-1], refs[-1]
    here = pl.ds(pl.multiple_of(pl.program_id(0) * columns, columns), columns)
    total = back_refs[0][:, here].astype(jnp.float32)
    for ref in back_refs[1:]:
        total = total + ref[:, here].astype(jnp.float32)
    high, low, _ = parts_of(total)
    rows = jnp.concatenate([high, high, high, low, low], axis=0)
    added = jnp.dot(table_ref[...], rows, preferred_element_type=jnp.float32)
    out_ref[...] = (base_ref[:, here] + added).astype(jnp.bfloat16)


def ended(base, table, backs):
    count, width = base.shape
    steps = 3
    columns = width // steps
    return pl.pallas_call(
        functools.partial(end_kernel, columns),
        out_shape=jax.ShapeDtypeStruct((count, width), jnp.bfloat16),
        grid=(steps,),
        in_specs=[VMEM] * (2 + len(backs)),
        out_specs=pl.BlockSpec((count, columns), lambda i: (0, i)),
        compiler_params=PARAMS,
        cost_estimate=pl.CostEstimate(
            flops=2 * count * width * table.shape[0], bytes_accessed=6 * count * width,
            transcendentals=0,
        ),
    )(base, table, *backs)


def early_kernel(left_ref, right_ref, out_ref):
    out_ref[...] = left_ref[...].astype(jnp.float32) + right_ref[...].astype(jnp.float32)


def summed_early(left, right):
    return pl.pallas_call(
        early_kernel,
        out_shape=jax.ShapeDtypeStruct(left.shape, jnp.float32),
        in_specs=[VMEM, VMEM],
        out_specs=VMEM,
        compiler_params=PARAMS,
        cost_estimate=pl.CostEstimate(
            flops=left.size, bytes_accessed=128 * left.size, transcendentals=0
        ),
    )(left, right)


def local(blocks, norm_gain, w_gate, w_up, w_down, route_ids, route_weights):
    slice_width = w_gate.shape[2]
    slice_count = HID // slice_width
    sections = lax.axis_size("section")
    devices = lax.axis_size("expert")
    experts = devices // slice_count
    same_slice = [[e * slice_count + k for e in range(experts)] for k in range(slice_count)]
    places = slice_count // 2
    token_count, width = blocks.shape[1:]

    def moved(value, sections_on, flip, side=0):
        pairs = []
        for s in range(sections):
            for d in range(devices):
                target = d ^ (2 * flip + side)
                pairs.append((s * devices + d, (s + sections_on) % sections * devices + target))
        return lax.ppermute(value, ("section", "expert"), pairs)

    def exchanged(rows):
        rows = rows.reshape(experts, CAP, width)
        return lax.all_to_all(
            rows, "expert", split_axis=0, concat_axis=0, tiled=True, axis_index_groups=same_slice
        ).reshape(experts * CAP, width)

    next_ids = moved(route_ids, -1, 0)[0]
    block, = loaded(blocks[0])
    picked = picked_rows(experts, jnp.swapaxes(next_ids, 0, 1), block)
    if experts > 1:
        picked = exchanged(picked)
    gate_t, up_t, down, gain = loaded(
        after(jnp.swapaxes(w_gate[0], 0, 1), picked), jnp.swapaxes(w_up[0], 0, 1), w_down[0], norm_gain
    )

    near, far = {}, {}
    far[0] = moved(picked, 1, 0, 1)
    near[2] = moved(picked, 1, 2)
    far[2] = moved(after(near[2], far[0], gain), 0, 0, 1)
    near[3] = moved(near[2], 0, 1)
    far[3] = moved(far[2], 0, 1)
    near[1] = moved(picked, 1, 1)
    pieces = 2
    size = token_count // pieces
    arrived = [
        moved(after(blocks[0, i * size:(i + 1) * size], near[1], near[2]), 1, 0)
        for i in range(pieces)
    ]
    base, table, near[0] = based(
        experts, arrived, gain, jnp.swapaxes(route_ids[0], 0, 1),
        jnp.swapaxes(route_weights[0], 0, 1),
    )

    if experts > 1:
        near[0] = exchanged(near[0])
    own, other = {}, {}
    for k in (2, 3, 1, 0):
        first = {2: (near[3],), 3: (other.get(2), arrived[0]), 1: (own.get(3),), 0: (own.get(1),)}[k]
        if k == 3:
            far[1] = moved(after(near[1], own[2]), 0, 0, 1)
        own[k], sent = mlp(after(near[k], *first), far[k], gain, gate_t, up_t, down)
        other[k] = moved(sent, 0, 0, 1)
    both = {
        k: (own[k].astype(jnp.float32) + other[k].astype(jnp.float32)).astype(jnp.bfloat16)
        for k in (2, 3, 1)
    }
    early = summed_early(own[0], moved(both[2], 0, 2))
    backs = [
        early, moved(both[3], 0, 3), moved(after(both[1], early), 0, 1), other[0],
    ]
    if experts > 1:
        backs = [exchanged(sum(back.astype(jnp.float32) for back in backs).astype(jnp.bfloat16))]
    return ended(base, table, backs)[None]


def solution(mesh):
    placed = (
        P("section", ("dp", "expert"), None),
        P("section", None),
        P("section", None, "expert"),
        P("section", None, "expert"),
        P("section", "expert", None),
        P("section", ("dp", "expert"), None),
        P("section", ("dp", "expert"), None),
    )
    return jax.shard_map(
        local,
        mesh=mesh,
        in_specs=placed,
        out_specs=P("section", ("dp", "expert"), None),
        check_vma=False,
    )
```

```python
import functools

import jax
import jax.numpy as jnp
from jax import lax
from jax.experimental import pallas as pl
from jax.experimental.pallas import tpu as pltpu
from jax.sharding import PartitionSpec as P

HID = 1536
CAP = 32
VMEM = pl.BlockSpec(memory_space=pltpu.VMEM)
HBM = pl.BlockSpec(memory_space=pltpu.HBM)
PARAMS = pltpu.CompilerParams(vmem_limit_bytes=24 * 1024 * 1024)


def after(value, *others):
    return lax.optimization_barrier((value, *others))[0]


def load_kernel(count, *refs):
    sources, targets, sems = refs[:count], refs[count:2 * count], refs[2 * count]
    copies = [
        pltpu.make_async_copy(a, b, sems.at[i]) for i, (a, b) in enumerate(zip(sources, targets))
    ]
    for copy in copies:
        copy.start()
    for copy in copies:
        copy.wait()


def loaded(*arrays):
    return pl.pallas_call(
        functools.partial(load_kernel, len(arrays)),
        out_shape=tuple(jax.ShapeDtypeStruct(a.shape, a.dtype) for a in arrays),
        in_specs=[HBM] * len(arrays),
        out_specs=(VMEM,) * len(arrays),
        scratch_shapes=[pltpu.SemaphoreType.DMA((len(arrays),))],
        compiler_params=PARAMS,
        cost_estimate=pl.CostEstimate(flops=0, bytes_accessed=6 * 1024 * 1024, transcendentals=0),
    )(*(pltpu.with_memory_space_constraint(a, pltpu.HBM) for a in arrays))


def slot_rows(ids, e):
    count = ids.shape[1]
    earlier = lax.broadcasted_iota(jnp.int32, (count, count), 0)
    later = lax.broadcasted_iota(jnp.int32, (count, count), 1)
    before = jnp.where(earlier < later, 1.0, 0.0).astype(jnp.bfloat16)
    slot = lax.broadcasted_iota(jnp.int32, (CAP, count), 0).astype(jnp.float32)
    hit = jnp.max(jnp.where(ids == e, 1.0, 0.0), axis=0, keepdims=True)
    hit = jnp.broadcast_to(hit, (CAP, count))
    rank = jnp.dot(hit.astype(jnp.bfloat16), before, preferred_element_type=jnp.float32)
    return jnp.where(rank == slot, hit, 0.0)


def pick_kernel(experts, ids_ref, block_ref, out_ref):
    for e in range(experts):
        table = slot_rows(ids_ref[...], e).astype(jnp.bfloat16)
        rows = jnp.dot(table, block_ref[...], preferred_element_type=jnp.float32)
        out_ref[e * CAP:(e + 1) * CAP, :] = rows.astype(jnp.bfloat16)


def picked_rows(experts, ids_t, block):
    return pl.pallas_call(
        functools.partial(pick_kernel, experts),
        out_shape=jax.ShapeDtypeStruct((experts * CAP, block.shape[1]), jnp.bfloat16),
        in_specs=[VMEM, VMEM],
        out_specs=VMEM,
        compiler_params=PARAMS,
        cost_estimate=pl.CostEstimate(
            flops=2 * experts * CAP * block.size, bytes_accessed=block.size, transcendentals=0
        ),
    )(ids_t, block)


def mlp_kernel(near_ref, far_ref, gain_ref, gate_ref, up_ref, down_ref, near_out, far_out):
    count = near_ref.shape[0]
    rows = jnp.concatenate([near_ref[...], far_ref[...]], axis=0).astype(jnp.float32)
    inverse = lax.rsqrt(jnp.mean(rows * rows, axis=-1, keepdims=True) + 1e-06)
    normed = (rows * inverse * gain_ref[...].astype(jnp.float32)).astype(jnp.bfloat16)
    across = (((1,), (1,)), ((), ()))
    gate = lax.dot_general(normed, gate_ref[...], across, preferred_element_type=jnp.float32)
    up = lax.dot_general(normed, up_ref[...], across, preferred_element_type=jnp.float32)
    hidden = (gate / (1.0 + jnp.exp(-gate)) * up).astype(jnp.bfloat16)
    partial = jnp.dot(hidden, down_ref[...], preferred_element_type=jnp.float32)
    partial = partial.astype(jnp.bfloat16)
    near_out[...] = partial[:count]
    far_out[...] = partial[count:]


def mlp(near, far, gain, gate_t, up_t, down):
    rows = 2 * near.shape[0]
    width, hidden = down.shape[1], down.shape[0]
    out = jax.ShapeDtypeStruct(near.shape, jnp.bfloat16)
    return pl.pallas_call(
        mlp_kernel,
        out_shape=(out, out),
        in_specs=[VMEM] * 6,
        out_specs=(VMEM, VMEM),
        compiler_params=PARAMS,
        cost_estimate=pl.CostEstimate(
            flops=6 * rows * width * hidden, bytes_accessed=6 * width * hidden, transcendentals=0
        ),
    )(near, far, gain, gate_t, up_t, down)


def parts_of(value):
    terms = []
    for _ in range(3):
        terms.append(value.astype(jnp.bfloat16))
        value = value - terms[-1].astype(jnp.float32)
    return terms


def base_kernel(experts, gain_ref, ids_ref, weights_ref, *refs):
    block_refs, (out_ref, table_ref, pick_ref) = refs[:-3], refs[-3:]
    ids, weights = ids_ref[...], weights_ref[...]
    count = ids.shape[1]
    zero = jnp.sum(jnp.where(ids >= experts, weights, 0.0), axis=0, keepdims=True)
    same = lax.broadcasted_iota(jnp.int32, (count, count), 0) == lax.broadcasted_iota(
        jnp.int32, (count, count), 1
    )
    zero = jnp.sum(jnp.where(same, zero, 0.0), axis=1, keepdims=True)
    start = 0
    for ref in block_refs:
        end = start + ref.shape[0]
        rows = ref[...].astype(jnp.float32)
        inverse = lax.rsqrt(jnp.mean(rows * rows, axis=-1, keepdims=True) + 1e-06)
        normed = (rows * inverse * gain_ref[...].astype(jnp.float32)).astype(jnp.bfloat16)
        out_ref[start:end] = rows + zero[start:end] * normed.astype(jnp.float32)
        start = end
    tables = []
    for e in range(experts):
        weight = jnp.sum(jnp.where(ids == e, weights, 0.0), axis=0, keepdims=True)
        slots = slot_rows(ids, e)
        tables.append(slots * weight)
        start, total = 0, 0.0
        for ref in block_refs:
            end = start + ref.shape[0]
            part = slots[:, start:end].astype(jnp.bfloat16)
            total += jnp.dot(part, ref[...], preferred_element_type=jnp.float32)
            start = end
        pick_ref[e * CAP:(e + 1) * CAP, :] = total.astype(jnp.bfloat16)
    terms = parts_of(jnp.concatenate(tables, axis=0).T)
    table_ref[...] = jnp.concatenate(terms + terms[:2], axis=1)


def based(experts, blocks, gain, ids_t, weights_t):
    count, width = ids_t.shape[1], blocks[0].shape[1]
    return pl.pallas_call(
        functools.partial(base_kernel, experts),
        out_shape=(
            jax.ShapeDtypeStruct((count, width), jnp.float32),
            jax.ShapeDtypeStruct((count, 5 * experts * CAP), jnp.bfloat16),
            jax.ShapeDtypeStruct((experts * CAP, width), jnp.bfloat16),
        ),
        in_specs=[VMEM] * (3 + len(blocks)),
        out_specs=(VMEM, VMEM, VMEM),
        compiler_params=PARAMS,
        cost_estimate=pl.CostEstimate(
            flops=8 * count * width, bytes_accessed=6 * count * width, transcendentals=0
        ),
    )(gain, ids_t, weights_t, *blocks)


def end_kernel(columns, base_ref, table_ref, *refs):
    back_refs, out_ref = refs[:-1], refs[-1]
    here = pl.ds(pl.multiple_of(pl.program_id(0) * columns, columns), columns)
    total = back_refs[0][:, here].astype(jnp.float32)
    for ref in back_refs[1:]:
        total = total + ref[:, here].astype(jnp.float32)
    high, low, _ = parts_of(total)
    rows = jnp.concatenate([high, high, high, low, low], axis=0)
    added = jnp.dot(table_ref[...], rows, preferred_element_type=jnp.float32)
    out_ref[...] = (base_ref[:, here] + added).astype(jnp.bfloat16)


def ended(base, table, backs):
    count, width = base.shape
    steps = 3
    columns = width // steps
    return pl.pallas_call(
        functools.partial(end_kernel, columns),
        out_shape=jax.ShapeDtypeStruct((count, width), jnp.bfloat16),
        grid=(steps,),
        in_specs=[VMEM] * (2 + len(backs)),
        out_specs=pl.BlockSpec((count, columns), lambda i: (0, i)),
        compiler_params=PARAMS,
        cost_estimate=pl.CostEstimate(
            flops=2 * count * width * table.shape[0], bytes_accessed=6 * count * width,
            transcendentals=0,
        ),
    )(base, table, *backs)


def early_kernel(left_ref, right_ref, out_ref):
    out_ref[...] = left_ref[...].astype(jnp.float32) + right_ref[...].astype(jnp.float32)


def summed_early(left, right):
    return pl.pallas_call(
        early_kernel,
        out_shape=jax.ShapeDtypeStruct(left.shape, jnp.float32),
        in_specs=[VMEM, VMEM],
        out_specs=VMEM,
        compiler_params=PARAMS,
        cost_estimate=pl.CostEstimate(
            flops=left.size, bytes_accessed=128 * left.size, transcendentals=0
        ),
    )(left, right)


def local(blocks, norm_gain, w_gate, w_up, w_down, route_ids, route_weights):
    slice_width = w_gate.shape[2]
    slice_count = HID // slice_width
    sections = lax.axis_size("section")
    devices = lax.axis_size("expert")
    experts = devices // slice_count
    same_slice = [[e * slice_count + k for e in range(experts)] for k in range(slice_count)]
    places = slice_count // 2
    token_count, width = blocks.shape[1:]

    def moved(value, sections_on, flip, side=0):
        pairs = []
        for s in range(sections):
            for d in range(devices):
                target = d ^ (2 * flip + side)
                pairs.append((s * devices + d, (s + sections_on) % sections * devices + target))
        return lax.ppermute(value, ("section", "expert"), pairs)

    def exchanged(rows):
        rows = rows.reshape(experts, CAP, width)
        return lax.all_to_all(
            rows, "expert", split_axis=0, concat_axis=0, tiled=True, axis_index_groups=same_slice
        ).reshape(experts * CAP, width)

    next_ids = moved(route_ids, -1, 0)[0]
    block, = loaded(blocks[0])
    picked = picked_rows(experts, jnp.swapaxes(next_ids, 0, 1), block)
    if experts > 1:
        picked = exchanged(picked)
    gate_t, up_t, down, gain = loaded(
        after(jnp.swapaxes(w_gate[0], 0, 1), picked), jnp.swapaxes(w_up[0], 0, 1), w_down[0], norm_gain
    )

    near, far = {}, {}
    near[2] = moved(picked, 1, 2)
    far[0] = moved(picked, 1, 0, 1)
    far[2] = moved(after(near[2], far[0], gain), 0, 0, 1)
    near[3] = moved(near[2], 0, 1)
    far[3] = moved(far[2], 0, 1)
    near[1] = moved(after(picked, near[2]), 1, 1)
    pieces = 2
    size = token_count // pieces
    arrived = [
        moved(after(blocks[0, i * size:(i + 1) * size], far[0], near[2]), 1, 0)
        for i in range(pieces)
    ]
    base, table, near[0] = based(
        experts, arrived, gain, jnp.swapaxes(route_ids[0], 0, 1),
        jnp.swapaxes(route_weights[0], 0, 1),
    )

    if experts > 1:
        near[0] = exchanged(near[0])
    own, other = {}, {}
    for k in (2, 3, 1, 0):
        first = {2: (near[3],), 3: (other.get(2), arrived[0]), 1: (own.get(3),), 0: (own.get(1),)}[k]
        if k == 3:
            far[1] = moved(after(near[1], own[2]), 0, 0, 1)
        own[k], sent = mlp(after(near[k], *first), far[k], gain, gate_t, up_t, down)
        other[k] = moved(sent, 0, 0, 1)
    both = {
        k: (own[k].astype(jnp.float32) + other[k].astype(jnp.float32)).astype(jnp.bfloat16)
        for k in (2, 3, 1)
    }
    early = summed_early(own[0], moved(both[2], 0, 2))
    backs = [
        early, moved(both[3], 0, 3), moved(after(both[1], early), 0, 1), other[0],
    ]
    if experts > 1:
        backs = [exchanged(sum(back.astype(jnp.float32) for back in backs).astype(jnp.bfloat16))]
    return ended(base, table, backs)[None]


def solution(mesh):
    placed = (
        P("section", ("dp", "expert"), None),
        P("section", None),
        P("section", None, "expert"),
        P("section", None, "expert"),
        P("section", "expert", None),
        P("section", ("dp", "expert"), None),
        P("section", ("dp", "expert"), None),
    )
    return jax.shard_map(
        local,
        mesh=mesh,
        in_specs=placed,
        out_specs=P("section", ("dp", "expert"), None),
        check_vma=False,
    )
```

```python
import functools

import jax
import jax.numpy as jnp
from jax import lax
from jax.experimental import pallas as pl
from jax.experimental.pallas import tpu as pltpu
from jax.sharding import PartitionSpec as P

HID = 1536
CAP = 32
VMEM = pl.BlockSpec(memory_space=pltpu.VMEM)
HBM = pl.BlockSpec(memory_space=pltpu.HBM)
PARAMS = pltpu.CompilerParams(vmem_limit_bytes=24 * 1024 * 1024)


def after(value, *others):
    return lax.optimization_barrier((value, *others))[0]


def load_kernel(count, *refs):
    sources, targets, sems = refs[:count], refs[count:2 * count], refs[2 * count]
    copies = [
        pltpu.make_async_copy(a, b, sems.at[i]) for i, (a, b) in enumerate(zip(sources, targets))
    ]
    for copy in copies:
        copy.start()
    for copy in copies:
        copy.wait()


def loaded(*arrays):
    return pl.pallas_call(
        functools.partial(load_kernel, len(arrays)),
        out_shape=tuple(jax.ShapeDtypeStruct(a.shape, a.dtype) for a in arrays),
        in_specs=[HBM] * len(arrays),
        out_specs=(VMEM,) * len(arrays),
        scratch_shapes=[pltpu.SemaphoreType.DMA((len(arrays),))],
        compiler_params=PARAMS,
        cost_estimate=pl.CostEstimate(flops=0, bytes_accessed=6 * 1024 * 1024, transcendentals=0),
    )(*(pltpu.with_memory_space_constraint(a, pltpu.HBM) for a in arrays))


def slot_rows(ids, e):
    count = ids.shape[1]
    earlier = lax.broadcasted_iota(jnp.int32, (count, count), 0)
    later = lax.broadcasted_iota(jnp.int32, (count, count), 1)
    before = jnp.where(earlier < later, 1.0, 0.0).astype(jnp.bfloat16)
    slot = lax.broadcasted_iota(jnp.int32, (CAP, count), 0).astype(jnp.float32)
    hit = jnp.max(jnp.where(ids == e, 1.0, 0.0), axis=0, keepdims=True)
    hit = jnp.broadcast_to(hit, (CAP, count))
    rank = jnp.dot(hit.astype(jnp.bfloat16), before, preferred_element_type=jnp.float32)
    return jnp.where(rank == slot, hit, 0.0)


def pick_kernel(experts, ids_ref, block_ref, out_ref):
    for e in range(experts):
        table = slot_rows(ids_ref[...], e).astype(jnp.bfloat16)
        rows = jnp.dot(table, block_ref[...], preferred_element_type=jnp.float32)
        out_ref[e * CAP:(e + 1) * CAP, :] = rows.astype(jnp.bfloat16)


def picked_rows(experts, ids_t, block):
    return pl.pallas_call(
        functools.partial(pick_kernel, experts),
        out_shape=jax.ShapeDtypeStruct((experts * CAP, block.shape[1]), jnp.bfloat16),
        in_specs=[VMEM, VMEM],
        out_specs=VMEM,
        compiler_params=PARAMS,
        cost_estimate=pl.CostEstimate(
            flops=2 * experts * CAP * block.size, bytes_accessed=block.size, transcendentals=0
        ),
    )(ids_t, block)


def mlp_kernel(near_ref, far_ref, gain_ref, gate_ref, up_ref, down_ref, near_out, far_out):
    count = near_ref.shape[0]
    rows = jnp.concatenate([near_ref[...], far_ref[...]], axis=0).astype(jnp.float32)
    inverse = lax.rsqrt(jnp.mean(rows * rows, axis=-1, keepdims=True) + 1e-06)
    normed = (rows * inverse * gain_ref[...].astype(jnp.float32)).astype(jnp.bfloat16)
    across = (((1,), (1,)), ((), ()))
    gate = lax.dot_general(normed, gate_ref[...], across, preferred_element_type=jnp.float32)
    up = lax.dot_general(normed, up_ref[...], across, preferred_element_type=jnp.float32)
    hidden = (gate / (1.0 + jnp.exp(-gate)) * up).astype(jnp.bfloat16)
    partial = jnp.dot(hidden, down_ref[...], preferred_element_type=jnp.float32)
    partial = partial.astype(jnp.bfloat16)
    near_out[...] = partial[:count]
    far_out[...] = partial[count:]


def mlp(near, far, gain, gate_t, up_t, down):
    rows = 2 * near.shape[0]
    width, hidden = down.shape[1], down.shape[0]
    out = jax.ShapeDtypeStruct(near.shape, jnp.bfloat16)
    return pl.pallas_call(
        mlp_kernel,
        out_shape=(out, out),
        in_specs=[VMEM] * 6,
        out_specs=(VMEM, VMEM),
        compiler_params=PARAMS,
        cost_estimate=pl.CostEstimate(
            flops=6 * rows * width * hidden, bytes_accessed=6 * width * hidden, transcendentals=0
        ),
    )(near, far, gain, gate_t, up_t, down)


def parts_of(value):
    terms = []
    for _ in range(3):
        terms.append(value.astype(jnp.bfloat16))
        value = value - terms[-1].astype(jnp.float32)
    return terms


def base_kernel(experts, gain_ref, ids_ref, weights_ref, *refs):
    block_refs, (out_ref, table_ref, pick_ref) = refs[:-3], refs[-3:]
    ids, weights = ids_ref[...], weights_ref[...]
    count = ids.shape[1]
    zero = jnp.sum(jnp.where(ids >= experts, weights, 0.0), axis=0, keepdims=True)
    same = lax.broadcasted_iota(jnp.int32, (count, count), 0) == lax.broadcasted_iota(
        jnp.int32, (count, count), 1
    )
    zero = jnp.sum(jnp.where(same, zero, 0.0), axis=1, keepdims=True)
    start = 0
    for ref in block_refs:
        end = start + ref.shape[0]
        rows = ref[...].astype(jnp.float32)
        inverse = lax.rsqrt(jnp.mean(rows * rows, axis=-1, keepdims=True) + 1e-06)
        normed = (rows * inverse * gain_ref[...].astype(jnp.float32)).astype(jnp.bfloat16)
        out_ref[start:end] = rows + zero[start:end] * normed.astype(jnp.float32)
        start = end
    tables = []
    for e in range(experts):
        weight = jnp.sum(jnp.where(ids == e, weights, 0.0), axis=0, keepdims=True)
        slots = slot_rows(ids, e)
        tables.append(slots * weight)
        start, total = 0, 0.0
        for ref in block_refs:
            end = start + ref.shape[0]
            part = slots[:, start:end].astype(jnp.bfloat16)
            total += jnp.dot(part, ref[...], preferred_element_type=jnp.float32)
            start = end
        pick_ref[e * CAP:(e + 1) * CAP, :] = total.astype(jnp.bfloat16)
    terms = parts_of(jnp.concatenate(tables, axis=0).T)
    table_ref[...] = jnp.concatenate(terms + terms[:2], axis=1)


def based(experts, blocks, gain, ids_t, weights_t):
    count, width = ids_t.shape[1], blocks[0].shape[1]
    return pl.pallas_call(
        functools.partial(base_kernel, experts),
        out_shape=(
            jax.ShapeDtypeStruct((count, width), jnp.float32),
            jax.ShapeDtypeStruct((count, 5 * experts * CAP), jnp.bfloat16),
            jax.ShapeDtypeStruct((experts * CAP, width), jnp.bfloat16),
        ),
        in_specs=[VMEM] * (3 + len(blocks)),
        out_specs=(VMEM, VMEM, VMEM),
        compiler_params=PARAMS,
        cost_estimate=pl.CostEstimate(
            flops=8 * count * width, bytes_accessed=6 * count * width, transcendentals=0
        ),
    )(gain, ids_t, weights_t, *blocks)


def end_kernel(columns, base_ref, table_ref, *refs):
    back_refs, out_ref = refs[:-1], refs[-1]
    here = pl.ds(pl.multiple_of(pl.program_id(0) * columns, columns), columns)
    total = back_refs[0][:, here].astype(jnp.float32)
    for ref in back_refs[1:]:
        total = total + ref[:, here].astype(jnp.float32)
    high, low, _ = parts_of(total)
    rows = jnp.concatenate([high, high, high, low, low], axis=0)
    added = jnp.dot(table_ref[...], rows, preferred_element_type=jnp.float32)
    out_ref[...] = (base_ref[:, here] + added).astype(jnp.bfloat16)


def ended(base, table, backs):
    count, width = base.shape
    steps = 3
    columns = width // steps
    return pl.pallas_call(
        functools.partial(end_kernel, columns),
        out_shape=jax.ShapeDtypeStruct((count, width), jnp.bfloat16),
        grid=(steps,),
        in_specs=[VMEM] * (2 + len(backs)),
        out_specs=pl.BlockSpec((count, columns), lambda i: (0, i)),
        compiler_params=PARAMS,
        cost_estimate=pl.CostEstimate(
            flops=2 * count * width * table.shape[0], bytes_accessed=6 * count * width,
            transcendentals=0,
        ),
    )(base, table, *backs)


def early_kernel(left_ref, right_ref, out_ref):
    out_ref[...] = left_ref[...].astype(jnp.float32) + right_ref[...].astype(jnp.float32)


def summed_early(left, right):
    return pl.pallas_call(
        early_kernel,
        out_shape=jax.ShapeDtypeStruct(left.shape, jnp.float32),
        in_specs=[VMEM, VMEM],
        out_specs=VMEM,
        compiler_params=PARAMS,
        cost_estimate=pl.CostEstimate(
            flops=left.size, bytes_accessed=128 * left.size, transcendentals=0
        ),
    )(left, right)


def local(blocks, norm_gain, w_gate, w_up, w_down, route_ids, route_weights):
    slice_width = w_gate.shape[2]
    slice_count = HID // slice_width
    sections = lax.axis_size("section")
    devices = lax.axis_size("expert")
    experts = devices // slice_count
    same_slice = [[e * slice_count + k for e in range(experts)] for k in range(slice_count)]
    places = slice_count // 2
    token_count, width = blocks.shape[1:]

    def moved(value, sections_on, flip, side=0):
        pairs = []
        for s in range(sections):
            for d in range(devices):
                target = d ^ (2 * flip + side)
                pairs.append((s * devices + d, (s + sections_on) % sections * devices + target))
        return lax.ppermute(value, ("section", "expert"), pairs)

    def exchanged(rows):
        rows = rows.reshape(experts, CAP, width)
        return lax.all_to_all(
            rows, "expert", split_axis=0, concat_axis=0, tiled=True, axis_index_groups=same_slice
        ).reshape(experts * CAP, width)

    next_ids = moved(route_ids, -1, 0)[0]
    block, = loaded(blocks[0])
    picked = picked_rows(experts, jnp.swapaxes(next_ids, 0, 1), block)
    if experts > 1:
        picked = exchanged(picked)
    gate_t, up_t, down, gain = loaded(
        after(jnp.swapaxes(w_gate[0], 0, 1), picked), jnp.swapaxes(w_up[0], 0, 1), w_down[0], norm_gain
    )

    near, far = {}, {}
    near[2] = moved(picked, 1, 2)
    far[0] = moved(picked, 1, 0, 1)
    far[2] = moved(after(near[2], gain), 0, 0, 1)
    near[3] = moved(near[2], 0, 1)
    far[3] = moved(far[2], 0, 1)
    near[1] = moved(after(picked, near[2]), 1, 1)
    cuts = [CAP * 3 // 2]
    arrived = [
        moved(after(piece, far[0], near[2]), 1, 0)
        for piece in jnp.split(blocks[0], cuts)
    ]
    base, table, near[0] = based(
        experts, arrived, gain, jnp.swapaxes(route_ids[0], 0, 1),
        jnp.swapaxes(route_weights[0], 0, 1),
    )

    if experts > 1:
        near[0] = exchanged(near[0])
    own, other = {}, {}
    for k in (2, 3, 1, 0):
        first = {2: (near[3],), 3: (other.get(2), arrived[0]), 1: (own.get(3),), 0: (own.get(1),)}[k]
        if k == 3:
            far[1] = moved(after(near[1], own[2]), 0, 0, 1)
        own[k], sent = mlp(after(near[k], *first), far[k], gain, gate_t, up_t, down)
        other[k] = moved(sent, 0, 0, 1)
    both = {
        k: (own[k].astype(jnp.float32) + other[k].astype(jnp.float32)).astype(jnp.bfloat16)
        for k in (2, 3, 1)
    }
    early = summed_early(own[0], moved(both[2], 0, 2))
    backs = [
        early, moved(both[3], 0, 3), moved(after(both[1], early), 0, 1), other[0],
    ]
    if experts > 1:
        backs = [exchanged(sum(back.astype(jnp.float32) for back in backs).astype(jnp.bfloat16))]
    return ended(base, table, backs)[None]


def solution(mesh):
    placed = (
        P("section", ("dp", "expert"), None),
        P("section", None),
        P("section", None, "expert"),
        P("section", None, "expert"),
        P("section", "expert", None),
        P("section", ("dp", "expert"), None),
        P("section", ("dp", "expert"), None),
    )
    return jax.shard_map(
        local,
        mesh=mesh,
        in_specs=placed,
        out_specs=P("section", ("dp", "expert"), None),
        check_vma=False,
    )
```

```python
import functools

import jax
import jax.numpy as jnp
from jax import lax
from jax.experimental import pallas as pl
from jax.experimental.pallas import tpu as pltpu
from jax.sharding import PartitionSpec as P

HID = 1536
CAP = 32
VMEM = pl.BlockSpec(memory_space=pltpu.VMEM)
HBM = pl.BlockSpec(memory_space=pltpu.HBM)
PARAMS = pltpu.CompilerParams(vmem_limit_bytes=24 * 1024 * 1024)


def after(value, *others):
    return lax.optimization_barrier((value, *others))[0]


def parity():
    return lax.rem(lax.axis_index("expert"), 2)


def half_of(ref, which):
    half = ref.shape[1] // 2
    return ref.at[:, pl.ds(pl.multiple_of(which * half, half), half)]


def part_of(ref, which, parts):
    rows = ref.shape[0] // parts
    return ref.at[pl.ds(pl.multiple_of(which * rows, rows), rows)]


def load_kernel(kinds, *refs):
    count = len(kinds)
    sources, targets, sems = refs[:count], refs[count:2 * count], refs[2 * count]
    copies = []
    for i, (kind, source, target) in enumerate(zip(kinds, sources, targets)):
        if kind == "own":
            source = half_of(source, parity())
        if kind == "sent":
            source = half_of(source, 1 - parity())
            source = part_of(source, lax.axis_index("dp"), source.shape[0] // target.shape[0])
        copies.append(pltpu.make_async_copy(source, target, sems.at[i]))
    for copy in copies:
        copy.start()
    for copy in copies:
        copy.wait()


def loaded(arrays, kinds):
    shapes = []
    for a, kind in zip(arrays, kinds):
        rows, columns = a.shape
        rows = rows // lax.axis_size("dp") if kind == "sent" else rows
        shapes.append((rows, columns if kind == "whole" else columns // 2))
    return pl.pallas_call(
        functools.partial(load_kernel, kinds),
        out_shape=tuple(jax.ShapeDtypeStruct(s, a.dtype) for s, a in zip(shapes, arrays)),
        in_specs=[HBM] * len(arrays),
        out_specs=(VMEM,) * len(arrays),
        scratch_shapes=[pltpu.SemaphoreType.DMA((len(arrays),))],
        compiler_params=PARAMS,
        cost_estimate=pl.CostEstimate(
            flops=0, bytes_accessed=4 * sum(r * c for r, c in shapes), transcendentals=0
        ),
    )(*(pltpu.with_memory_space_constraint(a, pltpu.HBM) for a in arrays))


def gather_kernel(own_ref, other_ref, out_ref, sems):
    core = lax.axis_index("dp")
    copies = [
        pltpu.make_async_copy(own_ref, part_of(out_ref, core, 2), sems.at[0]),
        pltpu.make_async_copy(other_ref, part_of(out_ref, 1 - core, 2), sems.at[1]),
    ]
    for copy in copies:
        copy.start()
    for copy in copies:
        copy.wait()


def gathered(own, other):
    rows, columns = own.shape
    return pl.pallas_call(
        gather_kernel,
        out_shape=jax.ShapeDtypeStruct((2 * rows, columns), own.dtype),
        in_specs=[VMEM, VMEM],
        out_specs=VMEM,
        scratch_shapes=[pltpu.SemaphoreType.DMA((2,))],
        compiler_params=PARAMS,
        cost_estimate=pl.CostEstimate(
            flops=0, bytes_accessed=8 * rows * columns, transcendentals=0
        ),
    )(own, other)


def slot_rows(ids, e):
    count = ids.shape[1]
    earlier = lax.broadcasted_iota(jnp.int32, (count, count), 0)
    later = lax.broadcasted_iota(jnp.int32, (count, count), 1)
    before = jnp.where(earlier < later, 1.0, 0.0).astype(jnp.bfloat16)
    slot = lax.broadcasted_iota(jnp.int32, (CAP, count), 0).astype(jnp.float32)
    hit = jnp.max(jnp.where(ids == e, 1.0, 0.0), axis=0, keepdims=True)
    hit = jnp.broadcast_to(hit, (CAP, count))
    rank = jnp.dot(hit.astype(jnp.bfloat16), before, preferred_element_type=jnp.float32)
    return jnp.where(rank == slot, hit, 0.0)


def pick_kernel(experts, ids_ref, block_ref, out_ref):
    for e in range(experts):
        table = slot_rows(ids_ref[...], e).astype(jnp.bfloat16)
        rows = jnp.dot(table, block_ref[...], preferred_element_type=jnp.float32)
        out_ref[e * CAP:(e + 1) * CAP, :] = rows.astype(jnp.bfloat16)


def picked_rows(experts, ids_t, block):
    return pl.pallas_call(
        functools.partial(pick_kernel, experts),
        out_shape=jax.ShapeDtypeStruct((experts * CAP, block.shape[1]), jnp.bfloat16),
        in_specs=[VMEM, VMEM],
        out_specs=VMEM,
        compiler_params=PARAMS,
        cost_estimate=pl.CostEstimate(
            flops=2 * experts * CAP * block.size, bytes_accessed=block.size, transcendentals=0
        ),
    )(ids_t, block)


def hidden_kernel(near_ref, far_ref, gain_ref, gate_ref, up_ref, out_ref):
    rows = jnp.concatenate([near_ref[...], far_ref[...]], axis=0).astype(jnp.float32)
    inverse = lax.rsqrt(jnp.mean(rows * rows, axis=-1, keepdims=True) + 1e-06)
    normed = (rows * inverse * gain_ref[...].astype(jnp.float32)).astype(jnp.bfloat16)
    across = (((1,), (1,)), ((), ()))
    gate = lax.dot_general(normed, gate_ref[...], across, preferred_element_type=jnp.float32)
    up = lax.dot_general(normed, up_ref[...], across, preferred_element_type=jnp.float32)
    out_ref[...] = (gate / (1.0 + jnp.exp(-gate)) * up).astype(jnp.bfloat16)


def hidden_of(near, far, gain, gate_t, up_t):
    rows, (hidden, width) = 2 * near.shape[0], gate_t.shape
    return pl.pallas_call(
        hidden_kernel,
        out_shape=jax.ShapeDtypeStruct((rows, hidden), jnp.bfloat16),
        in_specs=[VMEM] * 5,
        out_specs=VMEM,
        compiler_params=PARAMS,
        cost_estimate=pl.CostEstimate(
            flops=4 * rows * width * hidden, bytes_accessed=4 * width * hidden, transcendentals=0
        ),
    )(near, far, gain, gate_t, up_t)


def down_kernel(own_ref, other_ref, own_down_ref, other_down_ref, out_ref):
    count = own_ref.shape[0] // 2
    other = jnp.concatenate([other_ref[count:], other_ref[:count]], axis=0)
    total = jnp.dot(own_ref[...], own_down_ref[...], preferred_element_type=jnp.float32)
    total += jnp.dot(other, other_down_ref[...], preferred_element_type=jnp.float32)
    out_ref[...] = total.astype(jnp.bfloat16)


def down_of(own, other, own_down, other_down):
    rows, (hidden, half) = own.shape[0], own_down.shape
    return pl.pallas_call(
        down_kernel,
        out_shape=jax.ShapeDtypeStruct((rows, half), jnp.bfloat16),
        in_specs=[VMEM] * 4,
        out_specs=VMEM,
        compiler_params=PARAMS,
        cost_estimate=pl.CostEstimate(
            flops=4 * rows * half * hidden, bytes_accessed=4 * half * hidden, transcendentals=0
        ),
    )(own, other, own_down, other_down)


def join_kernel(*refs):
    back_refs, near_ref, far_ref = refs[:-2], refs[-2], refs[-1]
    total = back_refs[0][...].astype(jnp.float32)
    for ref in back_refs[1:]:
        total = total + ref[...].astype(jnp.float32)
    count = near_ref.shape[0]
    near_ref[...] = total[:count]
    far_ref[...] = total[count:].astype(jnp.bfloat16)


def joined(backs):
    rows, half = backs[0].shape
    return pl.pallas_call(
        join_kernel,
        out_shape=(
            jax.ShapeDtypeStruct((rows // 2, half), jnp.float32),
            jax.ShapeDtypeStruct((rows // 2, half), jnp.bfloat16),
        ),
        in_specs=[VMEM] * len(backs),
        out_specs=(VMEM, VMEM),
        compiler_params=PARAMS,
        cost_estimate=pl.CostEstimate(
            flops=4 * rows * half, bytes_accessed=8 * rows * half, transcendentals=0
        ),
    )(*backs)


def parts_of(value):
    terms = []
    for _ in range(3):
        terms.append(value.astype(jnp.bfloat16))
        value = value - terms[-1].astype(jnp.float32)
    return terms


def base_kernel(experts, gain_ref, ids_ref, weights_ref, *refs):
    block_refs, (out_ref, table_ref, pick_ref) = refs[:-3], refs[-3:]
    ids, weights = ids_ref[...], weights_ref[...]
    count = ids.shape[1]
    zero = jnp.sum(jnp.where(ids >= experts, weights, 0.0), axis=0, keepdims=True)
    same = lax.broadcasted_iota(jnp.int32, (count, count), 0) == lax.broadcasted_iota(
        jnp.int32, (count, count), 1
    )
    zero = jnp.sum(jnp.where(same, zero, 0.0), axis=1, keepdims=True)
    start = 0
    for ref in block_refs:
        end = start + ref.shape[0]
        rows = ref[...].astype(jnp.float32)
        inverse = lax.rsqrt(jnp.mean(rows * rows, axis=-1, keepdims=True) + 1e-06)
        normed = (rows * inverse * gain_ref[...].astype(jnp.float32)).astype(jnp.bfloat16)
        out_ref[start:end] = rows + zero[start:end] * normed.astype(jnp.float32)
        start = end
    tables = []
    for e in range(experts):
        weight = jnp.sum(jnp.where(ids == e, weights, 0.0), axis=0, keepdims=True)
        slots = slot_rows(ids, e)
        tables.append(slots * weight)
        start, total = 0, 0.0
        for ref in block_refs:
            end = start + ref.shape[0]
            part = slots[:, start:end].astype(jnp.bfloat16)
            total += jnp.dot(part, ref[...], preferred_element_type=jnp.float32)
            start = end
        pick_ref[e * CAP:(e + 1) * CAP, :] = total.astype(jnp.bfloat16)
    terms = parts_of(jnp.concatenate(tables, axis=0).T)
    table_ref[...] = jnp.concatenate(terms + terms[:2], axis=1)


def based(experts, blocks, gain, ids_t, weights_t):
    count, width = ids_t.shape[1], blocks[0].shape[1]
    return pl.pallas_call(
        functools.partial(base_kernel, experts),
        out_shape=(
            jax.ShapeDtypeStruct((count, width), jnp.float32),
            jax.ShapeDtypeStruct((count, 5 * experts * CAP), jnp.bfloat16),
            jax.ShapeDtypeStruct((experts * CAP, width), jnp.bfloat16),
        ),
        in_specs=[VMEM] * (3 + len(blocks)),
        out_specs=(VMEM, VMEM, VMEM),
        compiler_params=PARAMS,
        cost_estimate=pl.CostEstimate(
            flops=8 * count * width, bytes_accessed=6 * count * width, transcendentals=0
        ),
    )(gain, ids_t, weights_t, *blocks)


def end_kernel(steps, ordered, base_ref, table_ref, near_ref, other_ref, out_ref):
    step = pl.program_id(0)
    columns = out_ref.shape[1]
    here = pl.ds(pl.multiple_of(step * columns, columns), columns)
    within = pl.ds(pl.multiple_of(lax.rem(step, steps // 2) * columns, columns), columns)
    first = 0 if ordered else parity()
    near = near_ref[:, within].astype(jnp.float32)
    other = other_ref[:, within].astype(jnp.float32)
    total = jnp.where(lax.div(step, steps // 2) == first, near, other)
    high, low, _ = parts_of(total)
    rows = jnp.concatenate([high, high, high, low, low], axis=0)
    added = jnp.dot(table_ref[...], rows, preferred_element_type=jnp.float32)
    out_ref[...] = (base_ref[:, here] + added).astype(jnp.bfloat16)


def ended(base, table, near, other, ordered):
    count, width = base.shape
    steps = 4
    columns = width // steps
    return pl.pallas_call(
        functools.partial(end_kernel, steps, ordered),
        out_shape=jax.ShapeDtypeStruct((count, width), jnp.bfloat16),
        grid=(steps,),
        in_specs=[VMEM] * 4,
        out_specs=pl.BlockSpec((count, columns), lambda i: (0, i)),
        compiler_params=PARAMS,
        cost_estimate=pl.CostEstimate(
            flops=2 * count * width * table.shape[0], bytes_accessed=6 * count * width,
            transcendentals=0,
        ),
    )(base, table, near, other)


def early_kernel(left_ref, right_ref, out_ref):
    out_ref[...] = left_ref[...].astype(jnp.float32) + right_ref[...].astype(jnp.float32)


def summed_early(left, right):
    return pl.pallas_call(
        early_kernel,
        out_shape=jax.ShapeDtypeStruct(left.shape, jnp.float32),
        in_specs=[VMEM, VMEM],
        out_specs=VMEM,
        compiler_params=PARAMS,
        cost_estimate=pl.CostEstimate(
            flops=left.size, bytes_accessed=128 * left.size, transcendentals=0
        ),
    )(left, right)


def local(blocks, norm_gain, w_gate, w_up, w_down, route_ids, route_weights):
    slice_width = w_gate.shape[2]
    slice_count = HID // slice_width
    sections = lax.axis_size("section")
    devices = lax.axis_size("expert")
    experts = devices // slice_count
    same_slice = [[e * slice_count + k for e in range(experts)] for k in range(slice_count)]
    places = slice_count // 2
    token_count, width = blocks.shape[1:]

    def moved(value, sections_on, flip, side=0):
        pairs = []
        for s in range(sections):
            for d in range(devices):
                target = d ^ (2 * flip + side)
                pairs.append((s * devices + d, (s + sections_on) % sections * devices + target))
        return lax.ppermute(value, ("section", "expert"), pairs)

    def exchanged(rows):
        rows = rows.reshape(experts, CAP, width)
        return lax.all_to_all(
            rows, "expert", split_axis=0, concat_axis=0, tiled=True, axis_index_groups=same_slice
        ).reshape(experts * CAP, width)

    next_ids = moved(route_ids, -1, 0)[0]
    block, down_sent = loaded((blocks[0], w_down[0]), ("whole", "sent"))
    picked = picked_rows(experts, jnp.swapaxes(next_ids, 0, 1), block)
    if experts > 1:
        picked = exchanged(picked)
    own_down, gate_t, up_t, gain = loaded(
        (
            after(w_down[0], picked), jnp.swapaxes(w_gate[0], 0, 1), jnp.swapaxes(w_up[0], 0, 1),
            norm_gain,
        ),
        ("own", "whole", "whole", "whole"),
    )
    other_down = moved(after(down_sent, picked), 0, 0, 1)
    if lax.axis_size("dp") == 2:
        other_down = gathered(other_down, lax.ppermute(other_down, "dp", [(0, 1), (1, 0)]))

    near, far = {}, {}
    near[2] = moved(picked, 1, 2)
    far[0] = moved(picked, 1, 0, 1)
    far[2] = moved(after(near[2], gain), 0, 0, 1)
    near[3] = moved(near[2], 0, 1)
    far[3] = moved(far[2], 0, 1)
    near[1] = moved(after(picked, far[2]), 1, 1)
    cuts = [CAP * 3 // 2]
    arrived = [
        moved(after(piece, far[0], near[2]), 1, 0)
        for piece in jnp.split(blocks[0], cuts)
    ]
    base, table, near[0] = based(
        experts, arrived, gain, jnp.swapaxes(route_ids[0], 0, 1),
        jnp.swapaxes(route_weights[0], 0, 1),
    )

    if experts > 1:
        near[0] = exchanged(near[0])
    hidden, part, back = {}, {}, {}
    for k in (2, 3, 1, 0):
        first = {
            2: (near[3],), 3: (part.get(2), arrived[0]), 1: (hidden.get(3),), 0: (hidden.get(1), back.get(2))
        }[k]
        if k == 3:
            far[1] = moved(after(near[1], part[2]), 0, 0, 1)
        hidden[k] = hidden_of(after(near[k], *first), far[k], gain, gate_t, up_t)
        part[k] = down_of(hidden[k], moved(hidden[k], 0, 0, 1), own_down, other_down)
        back[k] = moved(part[k], 0, k) if k else part[k]
    early = summed_early(back[0], back[2])
    own, others = joined([early, back[3], back[1]])
    others = moved(others, 0, 0, 1)
    if experts > 1:
        own = own.astype(jnp.bfloat16)
        left = parity() == 0
        summed = [jnp.where(left, own, others), jnp.where(left, others, own)]
        summed = exchanged(jnp.concatenate(summed, axis=1))
        own, others = summed[:, :width // 2], summed[:, width // 2:]
    return ended(base, table, own, others, experts > 1)[None]


def solution(mesh):
    placed = (
        P("section", ("dp", "expert"), None),
        P("section", None),
        P("section", None, "expert"),
        P("section", None, "expert"),
        P("section", "expert", None),
        P("section", ("dp", "expert"), None),
        P("section", ("dp", "expert"), None),
    )
    return jax.shard_map(
        local,
        mesh=mesh,
        in_specs=placed,
        out_specs=P("section", ("dp", "expert"), None),
        check_vma=False,
    )
```

```python
import functools

import jax
import jax.numpy as jnp
from jax import lax
from jax.experimental import pallas as pl
from jax.experimental.pallas import tpu as pltpu
from jax.sharding import PartitionSpec as P

HID = 1536
CAP = 32
VMEM = pl.BlockSpec(memory_space=pltpu.VMEM)
HBM = pl.BlockSpec(memory_space=pltpu.HBM)
PARAMS = pltpu.CompilerParams(vmem_limit_bytes=24 * 1024 * 1024)


def after(value, *others):
    return lax.optimization_barrier((value, *others))[0]


def parity():
    return lax.rem(lax.axis_index("expert"), 2)


def half_of(ref, which):
    half = ref.shape[1] // 2
    return ref.at[:, pl.ds(pl.multiple_of(which * half, half), half)]


def part_of(ref, which, parts):
    rows = ref.shape[0] // parts
    return ref.at[pl.ds(pl.multiple_of(which * rows, rows), rows)]


def load_kernel(kinds, *refs):
    count = len(kinds)
    sources, targets, sems = refs[:count], refs[count:2 * count], refs[2 * count]
    copies = []
    for i, (kind, source, target) in enumerate(zip(kinds, sources, targets)):
        if kind == "own":
            source = half_of(source, parity())
        if kind == "sent":
            source = half_of(source, 1 - parity())
            source = part_of(source, lax.axis_index("dp"), source.shape[0] // target.shape[0])
        copies.append(pltpu.make_async_copy(source, target, sems.at[i]))
    for copy in copies:
        copy.start()
    for copy in copies:
        copy.wait()


def loaded(arrays, kinds):
    shapes = []
    for a, kind in zip(arrays, kinds):
        rows, columns = a.shape
        rows = rows // lax.axis_size("dp") if kind == "sent" else rows
        shapes.append((rows, columns if kind == "whole" else columns // 2))
    return pl.pallas_call(
        functools.partial(load_kernel, kinds),
        out_shape=tuple(jax.ShapeDtypeStruct(s, a.dtype) for s, a in zip(shapes, arrays)),
        in_specs=[HBM] * len(arrays),
        out_specs=(VMEM,) * len(arrays),
        scratch_shapes=[pltpu.SemaphoreType.DMA((len(arrays),))],
        compiler_params=PARAMS,
        cost_estimate=pl.CostEstimate(
            flops=0, bytes_accessed=4 * sum(r * c for r, c in shapes), transcendentals=0
        ),
    )(*(pltpu.with_memory_space_constraint(a, pltpu.HBM) for a in arrays))


def gather_kernel(own_ref, other_ref, out_ref, sems):
    core = lax.axis_index("dp")
    copies = [
        pltpu.make_async_copy(own_ref, part_of(out_ref, core, 2), sems.at[0]),
        pltpu.make_async_copy(other_ref, part_of(out_ref, 1 - core, 2), sems.at[1]),
    ]
    for copy in copies:
        copy.start()
    for copy in copies:
        copy.wait()


def gathered(own, other):
    rows, columns = own.shape
    return pl.pallas_call(
        gather_kernel,
        out_shape=jax.ShapeDtypeStruct((2 * rows, columns), own.dtype),
        in_specs=[VMEM, VMEM],
        out_specs=VMEM,
        scratch_shapes=[pltpu.SemaphoreType.DMA((2,))],
        compiler_params=PARAMS,
        cost_estimate=pl.CostEstimate(
            flops=0, bytes_accessed=8 * rows * columns, transcendentals=0
        ),
    )(own, other)


def slot_rows(ids, e):
    count = ids.shape[1]
    earlier = lax.broadcasted_iota(jnp.int32, (count, count), 0)
    later = lax.broadcasted_iota(jnp.int32, (count, count), 1)
    before = jnp.where(earlier < later, 1.0, 0.0).astype(jnp.bfloat16)
    slot = lax.broadcasted_iota(jnp.int32, (CAP, count), 0).astype(jnp.float32)
    hit = jnp.max(jnp.where(ids == e, 1.0, 0.0), axis=0, keepdims=True)
    hit = jnp.broadcast_to(hit, (CAP, count))
    rank = jnp.dot(hit.astype(jnp.bfloat16), before, preferred_element_type=jnp.float32)
    return jnp.where(rank == slot, hit, 0.0)


def pick_kernel(experts, ids_ref, block_ref, out_ref):
    for e in range(experts):
        table = slot_rows(ids_ref[...], e).astype(jnp.bfloat16)
        rows = jnp.dot(table, block_ref[...], preferred_element_type=jnp.float32)
        out_ref[e * CAP:(e + 1) * CAP, :] = rows.astype(jnp.bfloat16)


def picked_rows(experts, ids_t, block):
    return pl.pallas_call(
        functools.partial(pick_kernel, experts),
        out_shape=jax.ShapeDtypeStruct((experts * CAP, block.shape[1]), jnp.bfloat16),
        in_specs=[VMEM, VMEM],
        out_specs=VMEM,
        compiler_params=PARAMS,
        cost_estimate=pl.CostEstimate(
            flops=2 * experts * CAP * block.size, bytes_accessed=block.size, transcendentals=0
        ),
    )(ids_t, block)


def hidden_kernel(near_ref, far_ref, gain_ref, gate_ref, up_ref, out_ref):
    rows = jnp.concatenate([near_ref[...], far_ref[...]], axis=0).astype(jnp.float32)
    inverse = lax.rsqrt(jnp.mean(rows * rows, axis=-1, keepdims=True) + 1e-06)
    normed = (rows * inverse * gain_ref[...].astype(jnp.float32)).astype(jnp.bfloat16)
    across = (((1,), (1,)), ((), ()))
    gate = lax.dot_general(normed, gate_ref[...], across, preferred_element_type=jnp.float32)
    up = lax.dot_general(normed, up_ref[...], across, preferred_element_type=jnp.float32)
    out_ref[...] = (gate / (1.0 + jnp.exp(-gate)) * up).astype(jnp.bfloat16)


def hidden_of(near, far, gain, gate_t, up_t):
    rows, (hidden, width) = 2 * near.shape[0], gate_t.shape
    return pl.pallas_call(
        hidden_kernel,
        out_shape=jax.ShapeDtypeStruct((rows, hidden), jnp.bfloat16),
        in_specs=[VMEM] * 5,
        out_specs=VMEM,
        compiler_params=PARAMS,
        cost_estimate=pl.CostEstimate(
            flops=4 * rows * width * hidden, bytes_accessed=4 * width * hidden, transcendentals=0
        ),
    )(near, far, gain, gate_t, up_t)


def down_kernel(own_ref, other_ref, own_down_ref, other_down_ref, out_ref):
    count = own_ref.shape[0] // 2
    other = jnp.concatenate([other_ref[count:], other_ref[:count]], axis=0)
    total = jnp.dot(own_ref[...], own_down_ref[...], preferred_element_type=jnp.float32)
    total += jnp.dot(other, other_down_ref[...], preferred_element_type=jnp.float32)
    out_ref[...] = total.astype(jnp.bfloat16)


def down_of(own, other, own_down, other_down):
    rows, (hidden, half) = own.shape[0], own_down.shape
    return pl.pallas_call(
        down_kernel,
        out_shape=jax.ShapeDtypeStruct((rows, half), jnp.bfloat16),
        in_specs=[VMEM] * 4,
        out_specs=VMEM,
        compiler_params=PARAMS,
        cost_estimate=pl.CostEstimate(
            flops=4 * rows * half * hidden, bytes_accessed=4 * half * hidden, transcendentals=0
        ),
    )(own, other, own_down, other_down)


def join_kernel(*refs):
    back_refs, near_ref, far_ref = refs[:-2], refs[-2], refs[-1]
    total = back_refs[0][...].astype(jnp.float32)
    for ref in back_refs[1:]:
        total = total + ref[...].astype(jnp.float32)
    count = near_ref.shape[0]
    near_ref[...] = total[:count]
    far_ref[...] = total[count:].astype(jnp.bfloat16)


def joined(backs):
    rows, half = backs[0].shape
    return pl.pallas_call(
        join_kernel,
        out_shape=(
            jax.ShapeDtypeStruct((rows // 2, half), jnp.float32),
            jax.ShapeDtypeStruct((rows // 2, half), jnp.bfloat16),
        ),
        in_specs=[VMEM] * len(backs),
        out_specs=(VMEM, VMEM),
        compiler_params=PARAMS,
        cost_estimate=pl.CostEstimate(
            flops=4 * rows * half, bytes_accessed=8 * rows * half, transcendentals=0
        ),
    )(*backs)


def parts_of(value):
    terms = []
    for _ in range(3):
        terms.append(value.astype(jnp.bfloat16))
        value = value - terms[-1].astype(jnp.float32)
    return terms


def base_kernel(experts, gain_ref, ids_ref, weights_ref, *refs):
    block_refs, (out_ref, table_ref, pick_ref) = refs[:-3], refs[-3:]
    ids, weights = ids_ref[...], weights_ref[...]
    count = ids.shape[1]
    zero = jnp.sum(jnp.where(ids >= experts, weights, 0.0), axis=0, keepdims=True)
    same = lax.broadcasted_iota(jnp.int32, (count, count), 0) == lax.broadcasted_iota(
        jnp.int32, (count, count), 1
    )
    zero = jnp.sum(jnp.where(same, zero, 0.0), axis=1, keepdims=True)
    start = 0
    for ref in block_refs:
        end = start + ref.shape[0]
        rows = ref[...].astype(jnp.float32)
        inverse = lax.rsqrt(jnp.mean(rows * rows, axis=-1, keepdims=True) + 1e-06)
        normed = (rows * inverse * gain_ref[...].astype(jnp.float32)).astype(jnp.bfloat16)
        out_ref[start:end] = rows + zero[start:end] * normed.astype(jnp.float32)
        start = end
    tables = []
    for e in range(experts):
        weight = jnp.sum(jnp.where(ids == e, weights, 0.0), axis=0, keepdims=True)
        slots = slot_rows(ids, e)
        tables.append(slots * weight)
        start, total = 0, 0.0
        for ref in block_refs:
            end = start + ref.shape[0]
            part = slots[:, start:end].astype(jnp.bfloat16)
            total += jnp.dot(part, ref[...], preferred_element_type=jnp.float32)
            start = end
        pick_ref[e * CAP:(e + 1) * CAP, :] = total.astype(jnp.bfloat16)
    terms = parts_of(jnp.concatenate(tables, axis=0).T)
    table_ref[...] = jnp.concatenate(terms + terms[:2], axis=1)


def based(experts, blocks, gain, ids_t, weights_t):
    count, width = ids_t.shape[1], blocks[0].shape[1]
    return pl.pallas_call(
        functools.partial(base_kernel, experts),
        out_shape=(
            jax.ShapeDtypeStruct((count, width), jnp.float32),
            jax.ShapeDtypeStruct((count, 5 * experts * CAP), jnp.bfloat16),
            jax.ShapeDtypeStruct((experts * CAP, width), jnp.bfloat16),
        ),
        in_specs=[VMEM] * (3 + len(blocks)),
        out_specs=(VMEM, VMEM, VMEM),
        compiler_params=PARAMS,
        cost_estimate=pl.CostEstimate(
            flops=8 * count * width, bytes_accessed=6 * count * width, transcendentals=0
        ),
    )(gain, ids_t, weights_t, *blocks)


def end_kernel(steps, ordered, base_ref, table_ref, near_ref, other_ref, out_ref):
    step = pl.program_id(0)
    columns = out_ref.shape[1]
    here = pl.ds(pl.multiple_of(step * columns, columns), columns)
    within = pl.ds(pl.multiple_of(lax.rem(step, steps // 2) * columns, columns), columns)
    first = 0 if ordered else parity()
    near = near_ref[:, within].astype(jnp.float32)
    other = other_ref[:, within].astype(jnp.float32)
    total = jnp.where(lax.div(step, steps // 2) == first, near, other)
    high, low, _ = parts_of(total)
    rows = jnp.concatenate([high, high, high, low, low], axis=0)
    added = jnp.dot(table_ref[...], rows, preferred_element_type=jnp.float32)
    out_ref[...] = (base_ref[:, here] + added).astype(jnp.bfloat16)


def ended(base, table, near, other, ordered):
    count, width = base.shape
    steps = 4
    columns = width // steps
    return pl.pallas_call(
        functools.partial(end_kernel, steps, ordered),
        out_shape=jax.ShapeDtypeStruct((count, width), jnp.bfloat16),
        grid=(steps,),
        in_specs=[VMEM] * 4,
        out_specs=pl.BlockSpec((count, columns), lambda i: (0, i)),
        compiler_params=PARAMS,
        cost_estimate=pl.CostEstimate(
            flops=2 * count * width * table.shape[0], bytes_accessed=6 * count * width,
            transcendentals=0,
        ),
    )(base, table, near, other)


def early_kernel(left_ref, right_ref, out_ref):
    out_ref[...] = left_ref[...].astype(jnp.float32) + right_ref[...].astype(jnp.float32)


def summed_early(left, right):
    return pl.pallas_call(
        early_kernel,
        out_shape=jax.ShapeDtypeStruct(left.shape, jnp.float32),
        in_specs=[VMEM, VMEM],
        out_specs=VMEM,
        compiler_params=PARAMS,
        cost_estimate=pl.CostEstimate(
            flops=left.size, bytes_accessed=128 * left.size, transcendentals=0
        ),
    )(left, right)


def local(blocks, norm_gain, w_gate, w_up, w_down, route_ids, route_weights):
    slice_width = w_gate.shape[2]
    slice_count = HID // slice_width
    sections = lax.axis_size("section")
    devices = lax.axis_size("expert")
    experts = devices // slice_count
    same_slice = [[e * slice_count + k for e in range(experts)] for k in range(slice_count)]
    places = slice_count // 2
    token_count, width = blocks.shape[1:]

    def moved(value, sections_on, flip, side=0):
        pairs = []
        for s in range(sections):
            for d in range(devices):
                target = d ^ (2 * flip + side)
                pairs.append((s * devices + d, (s + sections_on) % sections * devices + target))
        return lax.ppermute(value, ("section", "expert"), pairs)

    def exchanged(rows):
        rows = rows.reshape(experts, CAP, width)
        return lax.all_to_all(
            rows, "expert", split_axis=0, concat_axis=0, tiled=True, axis_index_groups=same_slice
        ).reshape(experts * CAP, width)

    next_ids = moved(route_ids, -1, 0)[0]
    block, down_sent = loaded((blocks[0], w_down[0]), ("whole", "sent"))
    picked = picked_rows(experts, jnp.swapaxes(next_ids, 0, 1), block)
    if experts > 1:
        picked = exchanged(picked)
    own_down, gate_t, up_t, gain = loaded(
        (
            after(w_down[0], picked), jnp.swapaxes(w_gate[0], 0, 1), jnp.swapaxes(w_up[0], 0, 1),
            norm_gain,
        ),
        ("own", "whole", "whole", "whole"),
    )
    other_down = moved(after(down_sent, picked), 0, 0, 1)
    if lax.axis_size("dp") == 2:
        other_down = gathered(other_down, lax.ppermute(other_down, "dp", [(0, 1), (1, 0)]))

    near, far = {}, {}
    near[2] = moved(picked, 1, 2)
    far[0] = moved(picked, 1, 0, 1)
    far[2] = moved(after(near[2], gain), 0, 0, 1)
    near[3] = moved(near[2], 0, 1)
    far[3] = moved(far[2], 0, 1)
    near[1] = moved(after(picked, near[2]), 1, 1)
    cuts = [CAP * 3 // 2]
    arrived = [
        moved(after(piece, far[0], near[2]), 1, 0)
        for piece in jnp.split(blocks[0], cuts)
    ]
    base, table, near[0] = based(
        experts, arrived, gain, jnp.swapaxes(route_ids[0], 0, 1),
        jnp.swapaxes(route_weights[0], 0, 1),
    )

    if experts > 1:
        near[0] = exchanged(near[0])
    hidden, part, back = {}, {}, {}
    for k in (2, 3, 1, 0):
        first = {
            2: (near[3],), 3: (part.get(2), arrived[0]), 1: (hidden.get(3),), 0: (hidden.get(1), back.get(2))
        }[k]
        if k == 3:
            far[1] = moved(after(near[1], part[2]), 0, 0, 1)
        hidden[k] = hidden_of(after(near[k], *first), far[k], gain, gate_t, up_t)
        crossed = moved(hidden[k], 0, 0, 1)
        if k == 2:
            crossed = after(crossed, far[3])
        part[k] = down_of(hidden[k], crossed, own_down, other_down)
        back[k] = moved(part[k], 0, k) if k else part[k]
    early = summed_early(back[0], back[2])
    own, others = joined([early, back[3], back[1]])
    others = moved(others, 0, 0, 1)
    if experts > 1:
        own = own.astype(jnp.bfloat16)
        left = parity() == 0
        summed = [jnp.where(left, own, others), jnp.where(left, others, own)]
        summed = exchanged(jnp.concatenate(summed, axis=1))
        own, others = summed[:, :width // 2], summed[:, width // 2:]
    return ended(base, table, own, others, experts > 1)[None]


def solution(mesh):
    placed = (
        P("section", ("dp", "expert"), None),
        P("section", None),
        P("section", None, "expert"),
        P("section", None, "expert"),
        P("section", "expert", None),
        P("section", ("dp", "expert"), None),
        P("section", ("dp", "expert"), None),
    )
    return jax.shard_map(
        local,
        mesh=mesh,
        in_specs=placed,
        out_specs=P("section", ("dp", "expert"), None),
        check_vma=False,
    )
```

```python
import functools

import jax
import jax.numpy as jnp
from jax import lax
from jax.experimental import pallas as pl
from jax.experimental.pallas import tpu as pltpu
from jax.sharding import PartitionSpec as P

HID = 1536
CAP = 32
VMEM = pl.BlockSpec(memory_space=pltpu.VMEM)
HBM = pl.BlockSpec(memory_space=pltpu.HBM)
PARAMS = pltpu.CompilerParams(vmem_limit_bytes=24 * 1024 * 1024)


def after(value, *others):
    return lax.optimization_barrier((value, *others))[0]


def parity():
    return lax.rem(lax.axis_index("expert"), 2)


def half_of(ref, which):
    half = ref.shape[1] // 2
    return ref.at[:, pl.ds(pl.multiple_of(which * half, half), half)]


def part_of(ref, which, parts):
    rows = ref.shape[0] // parts
    return ref.at[pl.ds(pl.multiple_of(which * rows, rows), rows)]


def load_kernel(kinds, *refs):
    count = len(kinds)
    sources, targets, sems = refs[:count], refs[count:2 * count], refs[2 * count]
    copies = []
    for i, (kind, source, target) in enumerate(zip(kinds, sources, targets)):
        if kind == "own":
            source = half_of(source, parity())
        if kind == "sent":
            source = half_of(source, 1 - parity())
            source = part_of(source, lax.axis_index("dp"), source.shape[0] // target.shape[0])
        copies.append(pltpu.make_async_copy(source, target, sems.at[i]))
    for copy in copies:
        copy.start()
    for copy in copies:
        copy.wait()


def loaded(arrays, kinds):
    shapes = []
    for a, kind in zip(arrays, kinds):
        rows, columns = a.shape
        rows = rows // lax.axis_size("dp") if kind == "sent" else rows
        shapes.append((rows, columns if kind == "whole" else columns // 2))
    return pl.pallas_call(
        functools.partial(load_kernel, kinds),
        out_shape=tuple(jax.ShapeDtypeStruct(s, a.dtype) for s, a in zip(shapes, arrays)),
        in_specs=[HBM] * len(arrays),
        out_specs=(VMEM,) * len(arrays),
        scratch_shapes=[pltpu.SemaphoreType.DMA((len(arrays),))],
        compiler_params=PARAMS,
        cost_estimate=pl.CostEstimate(
            flops=0, bytes_accessed=4 * sum(r * c for r, c in shapes), transcendentals=0
        ),
    )(*(pltpu.with_memory_space_constraint(a, pltpu.HBM) for a in arrays))


def gather_kernel(own_ref, other_ref, out_ref, sems):
    core = lax.axis_index("dp")
    copies = [
        pltpu.make_async_copy(own_ref, part_of(out_ref, core, 2), sems.at[0]),
        pltpu.make_async_copy(other_ref, part_of(out_ref, 1 - core, 2), sems.at[1]),
    ]
    for copy in copies:
        copy.start()
    for copy in copies:
        copy.wait()


def gathered(own, other):
    rows, columns = own.shape
    return pl.pallas_call(
        gather_kernel,
        out_shape=jax.ShapeDtypeStruct((2 * rows, columns), own.dtype),
        in_specs=[VMEM, VMEM],
        out_specs=VMEM,
        scratch_shapes=[pltpu.SemaphoreType.DMA((2,))],
        compiler_params=PARAMS,
        cost_estimate=pl.CostEstimate(
            flops=0, bytes_accessed=8 * rows * columns, transcendentals=0
        ),
    )(own, other)


def slot_rows(ids, e):
    count = ids.shape[1]
    earlier = lax.broadcasted_iota(jnp.int32, (count, count), 0)
    later = lax.broadcasted_iota(jnp.int32, (count, count), 1)
    before = jnp.where(earlier < later, 1.0, 0.0).astype(jnp.bfloat16)
    slot = lax.broadcasted_iota(jnp.int32, (CAP, count), 0).astype(jnp.float32)
    hit = jnp.max(jnp.where(ids == e, 1.0, 0.0), axis=0, keepdims=True)
    hit = jnp.broadcast_to(hit, (CAP, count))
    rank = jnp.dot(hit.astype(jnp.bfloat16), before, preferred_element_type=jnp.float32)
    return jnp.where(rank == slot, hit, 0.0)


def pick_kernel(experts, ids_ref, block_ref, out_ref):
    for e in range(experts):
        table = slot_rows(ids_ref[...], e).astype(jnp.bfloat16)
        rows = jnp.dot(table, block_ref[...], preferred_element_type=jnp.float32)
        out_ref[e * CAP:(e + 1) * CAP, :] = rows.astype(jnp.bfloat16)


def picked_rows(experts, ids_t, block):
    return pl.pallas_call(
        functools.partial(pick_kernel, experts),
        out_shape=jax.ShapeDtypeStruct((experts * CAP, block.shape[1]), jnp.bfloat16),
        in_specs=[VMEM, VMEM],
        out_specs=VMEM,
        compiler_params=PARAMS,
        cost_estimate=pl.CostEstimate(
            flops=2 * experts * CAP * block.size, bytes_accessed=block.size, transcendentals=0
        ),
    )(ids_t, block)


def hidden_kernel(near_ref, far_ref, gain_ref, gate_ref, up_ref, out_ref):
    rows = jnp.concatenate([near_ref[...], far_ref[...]], axis=0).astype(jnp.float32)
    inverse = lax.rsqrt(jnp.mean(rows * rows, axis=-1, keepdims=True) + 1e-06)
    normed = (rows * inverse * gain_ref[...].astype(jnp.float32)).astype(jnp.bfloat16)
    across = (((1,), (1,)), ((), ()))
    gate = lax.dot_general(normed, gate_ref[...], across, preferred_element_type=jnp.float32)
    up = lax.dot_general(normed, up_ref[...], across, preferred_element_type=jnp.float32)
    out_ref[...] = (gate / (1.0 + jnp.exp(-gate)) * up).astype(jnp.bfloat16)


def hidden_of(near, far, gain, gate_t, up_t):
    rows, (hidden, width) = 2 * near.shape[0], gate_t.shape
    return pl.pallas_call(
        hidden_kernel,
        out_shape=jax.ShapeDtypeStruct((rows, hidden), jnp.bfloat16),
        in_specs=[VMEM] * 5,
        out_specs=VMEM,
        compiler_params=PARAMS,
        cost_estimate=pl.CostEstimate(
            flops=4 * rows * width * hidden, bytes_accessed=4 * width * hidden, transcendentals=0
        ),
    )(near, far, gain, gate_t, up_t)


def down_kernel(own_ref, other_ref, own_down_ref, other_down_ref, out_ref):
    count = own_ref.shape[0] // 2
    other = jnp.concatenate([other_ref[count:], other_ref[:count]], axis=0)
    total = jnp.dot(own_ref[...], own_down_ref[...], preferred_element_type=jnp.float32)
    total += jnp.dot(other, other_down_ref[...], preferred_element_type=jnp.float32)
    out_ref[...] = total.astype(jnp.bfloat16)


def down_of(own, other, own_down, other_down):
    rows, (hidden, half) = own.shape[0], own_down.shape
    return pl.pallas_call(
        down_kernel,
        out_shape=jax.ShapeDtypeStruct((rows, half), jnp.bfloat16),
        in_specs=[VMEM] * 4,
        out_specs=VMEM,
        compiler_params=PARAMS,
        cost_estimate=pl.CostEstimate(
            flops=4 * rows * half * hidden, bytes_accessed=4 * half * hidden, transcendentals=0
        ),
    )(own, other, own_down, other_down)


def join_kernel(*refs):
    back_refs, near_ref, far_ref = refs[:-2], refs[-2], refs[-1]
    total = back_refs[0][...].astype(jnp.float32)
    for ref in back_refs[1:]:
        total = total + ref[...].astype(jnp.float32)
    count = near_ref.shape[0]
    near_ref[...] = total[:count]
    far_ref[...] = total[count:].astype(jnp.bfloat16)


def joined(backs):
    rows, half = backs[0].shape
    return pl.pallas_call(
        join_kernel,
        out_shape=(
            jax.ShapeDtypeStruct((rows // 2, half), jnp.float32),
            jax.ShapeDtypeStruct((rows // 2, half), jnp.bfloat16),
        ),
        in_specs=[VMEM] * len(backs),
        out_specs=(VMEM, VMEM),
        compiler_params=PARAMS,
        cost_estimate=pl.CostEstimate(
            flops=4 * rows * half, bytes_accessed=8 * rows * half, transcendentals=0
        ),
    )(*backs)


def parts_of(value):
    terms = []
    for _ in range(3):
        terms.append(value.astype(jnp.bfloat16))
        value = value - terms[-1].astype(jnp.float32)
    return terms


def base_kernel(experts, gain_ref, ids_ref, weights_ref, *refs):
    block_refs, (out_ref, table_ref, pick_ref) = refs[:-3], refs[-3:]
    ids, weights = ids_ref[...], weights_ref[...]
    count = ids.shape[1]
    zero = jnp.sum(jnp.where(ids >= experts, weights, 0.0), axis=0, keepdims=True)
    same = lax.broadcasted_iota(jnp.int32, (count, count), 0) == lax.broadcasted_iota(
        jnp.int32, (count, count), 1
    )
    zero = jnp.sum(jnp.where(same, zero, 0.0), axis=1, keepdims=True)
    start = 0
    for ref in block_refs:
        end = start + ref.shape[0]
        rows = ref[...].astype(jnp.float32)
        inverse = lax.rsqrt(jnp.mean(rows * rows, axis=-1, keepdims=True) + 1e-06)
        normed = (rows * inverse * gain_ref[...].astype(jnp.float32)).astype(jnp.bfloat16)
        out_ref[start:end] = rows + zero[start:end] * normed.astype(jnp.float32)
        start = end
    tables = []
    for e in range(experts):
        weight = jnp.sum(jnp.where(ids == e, weights, 0.0), axis=0, keepdims=True)
        slots = slot_rows(ids, e)
        tables.append(slots * weight)
        start, total = 0, 0.0
        for ref in block_refs:
            end = start + ref.shape[0]
            part = slots[:, start:end].astype(jnp.bfloat16)
            total += jnp.dot(part, ref[...], preferred_element_type=jnp.float32)
            start = end
        pick_ref[e * CAP:(e + 1) * CAP, :] = total.astype(jnp.bfloat16)
    terms = parts_of(jnp.concatenate(tables, axis=0).T)
    table_ref[...] = jnp.concatenate(terms + terms[:2], axis=1)


def based(experts, blocks, gain, ids_t, weights_t):
    count, width = ids_t.shape[1], blocks[0].shape[1]
    return pl.pallas_call(
        functools.partial(base_kernel, experts),
        out_shape=(
            jax.ShapeDtypeStruct((count, width), jnp.float32),
            jax.ShapeDtypeStruct((count, 5 * experts * CAP), jnp.bfloat16),
            jax.ShapeDtypeStruct((experts * CAP, width), jnp.bfloat16),
        ),
        in_specs=[VMEM] * (3 + len(blocks)),
        out_specs=(VMEM, VMEM, VMEM),
        compiler_params=PARAMS,
        cost_estimate=pl.CostEstimate(
            flops=8 * count * width, bytes_accessed=6 * count * width, transcendentals=0
        ),
    )(gain, ids_t, weights_t, *blocks)


def end_kernel(steps, which, base_ref, table_ref, rows_ref, *refs):
    out_ref, done, sems = refs[-3:]
    half = rows_ref.shape[1]
    columns = half // steps
    if which is None:
        which = parity()
    elif which < 0:
        which = 1 - parity()
    copies = []
    for step in range(steps):
        within = slice(step * columns, (step + 1) * columns)
        here = pl.ds(pl.multiple_of(which * half + step * columns, columns), columns)
        high, low, _ = parts_of(rows_ref[:, within].astype(jnp.float32))
        rows = jnp.concatenate([high, high, high, low, low], axis=0)
        added = jnp.dot(table_ref[...], rows, preferred_element_type=jnp.float32)
        done[:, within] = (base_ref[:, here] + added).astype(jnp.bfloat16)
        copies.append(pltpu.make_async_copy(done.at[:, within], out_ref.at[:, here], sems.at[step]))
        copies[-1].start()
    for copy in copies:
        copy.wait()


def ended(base, table, rows, which, out=None):
    count, width = base.shape
    half = rows.shape[1]
    steps = 3
    return pl.pallas_call(
        functools.partial(end_kernel, steps, which),
        out_shape=jax.ShapeDtypeStruct((count, width), jnp.bfloat16),
        in_specs=[VMEM] * 3 + ([] if out is None else [HBM]),
        out_specs=HBM,
        scratch_shapes=[pltpu.VMEM((count, half), jnp.bfloat16), pltpu.SemaphoreType.DMA((steps,))],
        input_output_aliases={} if out is None else {3: 0},
        compiler_params=PARAMS,
        cost_estimate=pl.CostEstimate(
            flops=2 * count * half * table.shape[1], bytes_accessed=6 * count * half,
            transcendentals=0,
        ),
    )(base, table, rows, *(() if out is None else (out,)))


def early_kernel(left_ref, right_ref, out_ref):
    out_ref[...] = left_ref[...].astype(jnp.float32) + right_ref[...].astype(jnp.float32)


def summed_early(left, right):
    return pl.pallas_call(
        early_kernel,
        out_shape=jax.ShapeDtypeStruct(left.shape, jnp.float32),
        in_specs=[VMEM, VMEM],
        out_specs=VMEM,
        compiler_params=PARAMS,
        cost_estimate=pl.CostEstimate(
            flops=left.size, bytes_accessed=128 * left.size, transcendentals=0
        ),
    )(left, right)


def local(blocks, norm_gain, w_gate, w_up, w_down, route_ids, route_weights):
    slice_width = w_gate.shape[2]
    slice_count = HID // slice_width
    sections = lax.axis_size("section")
    devices = lax.axis_size("expert")
    experts = devices // slice_count
    same_slice = [[e * slice_count + k for e in range(experts)] for k in range(slice_count)]
    places = slice_count // 2
    token_count, width = blocks.shape[1:]

    def moved(value, sections_on, flip, side=0):
        pairs = []
        for s in range(sections):
            for d in range(devices):
                target = d ^ (2 * flip + side)
                pairs.append((s * devices + d, (s + sections_on) % sections * devices + target))
        return lax.ppermute(value, ("section", "expert"), pairs)

    def exchanged(rows):
        rows = rows.reshape(experts, CAP, width)
        return lax.all_to_all(
            rows, "expert", split_axis=0, concat_axis=0, tiled=True, axis_index_groups=same_slice
        ).reshape(experts * CAP, width)

    next_ids = moved(route_ids, -1, 0)[0]
    block, down_sent = loaded((blocks[0], w_down[0]), ("whole", "sent"))
    picked = picked_rows(experts, jnp.swapaxes(next_ids, 0, 1), block)
    if experts > 1:
        picked = exchanged(picked)
    own_down, gate_t, up_t, gain = loaded(
        (
            after(w_down[0], picked), jnp.swapaxes(w_gate[0], 0, 1), jnp.swapaxes(w_up[0], 0, 1),
            norm_gain,
        ),
        ("own", "whole", "whole", "whole"),
    )
    other_down = moved(after(down_sent, picked), 0, 0, 1)
    if lax.axis_size("dp") == 2:
        other_down = gathered(other_down, lax.ppermute(other_down, "dp", [(0, 1), (1, 0)]))

    near, far = {}, {}
    near[2] = moved(picked, 1, 2)
    far[0] = moved(picked, 1, 0, 1)
    far[2] = moved(after(near[2], gain), 0, 0, 1)
    near[3] = moved(near[2], 0, 1)
    far[3] = moved(far[2], 0, 1)
    near[1] = moved(after(picked, near[2]), 1, 1)
    cuts = [CAP * 3 // 2]
    arrived = [
        moved(after(piece, far[0], near[2]), 1, 0)
        for piece in jnp.split(blocks[0], cuts)
    ]
    base, table, near[0] = based(
        experts, arrived, gain, jnp.swapaxes(route_ids[0], 0, 1),
        jnp.swapaxes(route_weights[0], 0, 1),
    )

    if experts > 1:
        near[0] = exchanged(near[0])
    hidden, part, back = {}, {}, {}
    for k in (2, 3, 1, 0):
        first = {
            2: (near[3],), 3: (part.get(2),), 1: (hidden.get(3),), 0: (hidden.get(1),)
        }[k]
        if k == 3:
            far[1] = moved(after(near[1], part[2]), 0, 0, 1)
        hidden[k] = hidden_of(after(near[k], *first), far[k], gain, gate_t, up_t)
        crossed = moved(hidden[k], 0, 0, 1)
        if k == 2:
            crossed = after(crossed, far[3])
        part[k] = down_of(hidden[k], crossed, own_down, other_down)
    back[2] = moved(part[2], 0, 2)
    back[3] = moved(after(part[3], back[2], hidden[0]), 0, 3)
    back[1] = moved(part[1], 0, 1)
    back[0] = part[0]
    early = summed_early(back[0], back[2])
    own, others = joined([early, back[3], back[1]])
    others = moved(others, 0, 0, 1)
    if experts > 1:
        own = own.astype(jnp.bfloat16)
        left = parity() == 0
        summed = [jnp.where(left, own, others), jnp.where(left, others, own)]
        summed = exchanged(jnp.concatenate(summed, axis=1))
        out = ended(base, table, summed[:, :width // 2], 0)
        return ended(base, table, summed[:, width // 2:], 1, out)[None]
    out = ended(base, table, own, None)
    return ended(base, table, others, -1, out)[None]


def solution(mesh):
    placed = (
        P("section", ("dp", "expert"), None),
        P("section", None),
        P("section", None, "expert"),
        P("section", None, "expert"),
        P("section", "expert", None),
        P("section", ("dp", "expert"), None),
        P("section", ("dp", "expert"), None),
    )
    return jax.shard_map(
        local,
        mesh=mesh,
        in_specs=placed,
        out_specs=P("section", ("dp", "expert"), None),
        check_vma=False,
    )
```

```python
import functools

import jax
import jax.numpy as jnp
from jax import lax
from jax.experimental import pallas as pl
from jax.experimental.pallas import tpu as pltpu
from jax.sharding import PartitionSpec as P

HID = 1536
CAP = 32
VMEM = pl.BlockSpec(memory_space=pltpu.VMEM)
HBM = pl.BlockSpec(memory_space=pltpu.HBM)
PARAMS = pltpu.CompilerParams(vmem_limit_bytes=24 * 1024 * 1024)


def after(value, *others):
    return lax.optimization_barrier((value, *others))[0]


def parity():
    return lax.rem(lax.axis_index("expert"), 2)


def half_of(ref, which):
    half = ref.shape[1] // 2
    return ref.at[:, pl.ds(pl.multiple_of(which * half, half), half)]


def part_of(ref, which, parts):
    rows = ref.shape[0] // parts
    return ref.at[pl.ds(pl.multiple_of(which * rows, rows), rows)]


def load_kernel(kinds, *refs):
    count = len(kinds)
    sources, targets, sems = refs[:count], refs[count:2 * count], refs[2 * count]
    copies = []
    for i, (kind, source, target) in enumerate(zip(kinds, sources, targets)):
        if kind == "own":
            source = half_of(source, parity())
        if kind == "sent":
            source = half_of(source, 1 - parity())
            source = part_of(source, lax.axis_index("dp"), source.shape[0] // target.shape[0])
        copies.append(pltpu.make_async_copy(source, target, sems.at[i]))
    for copy in copies:
        copy.start()
    for copy in copies:
        copy.wait()


def loaded(arrays, kinds):
    shapes = []
    for a, kind in zip(arrays, kinds):
        rows, columns = a.shape
        rows = rows // lax.axis_size("dp") if kind == "sent" else rows
        shapes.append((rows, columns if kind == "whole" else columns // 2))
    return pl.pallas_call(
        functools.partial(load_kernel, kinds),
        out_shape=tuple(jax.ShapeDtypeStruct(s, a.dtype) for s, a in zip(shapes, arrays)),
        in_specs=[HBM] * len(arrays),
        out_specs=(VMEM,) * len(arrays),
        scratch_shapes=[pltpu.SemaphoreType.DMA((len(arrays),))],
        compiler_params=PARAMS,
        cost_estimate=pl.CostEstimate(
            flops=0, bytes_accessed=4 * sum(r * c for r, c in shapes), transcendentals=0
        ),
    )(*(pltpu.with_memory_space_constraint(a, pltpu.HBM) for a in arrays))


def gather_kernel(own_ref, other_ref, out_ref, sems):
    core = lax.axis_index("dp")
    copies = [
        pltpu.make_async_copy(own_ref, part_of(out_ref, core, 2), sems.at[0]),
        pltpu.make_async_copy(other_ref, part_of(out_ref, 1 - core, 2), sems.at[1]),
    ]
    for copy in copies:
        copy.start()
    for copy in copies:
        copy.wait()


def gathered(own, other):
    rows, columns = own.shape
    return pl.pallas_call(
        gather_kernel,
        out_shape=jax.ShapeDtypeStruct((2 * rows, columns), own.dtype),
        in_specs=[VMEM, VMEM],
        out_specs=VMEM,
        scratch_shapes=[pltpu.SemaphoreType.DMA((2,))],
        compiler_params=PARAMS,
        cost_estimate=pl.CostEstimate(
            flops=0, bytes_accessed=8 * rows * columns, transcendentals=0
        ),
    )(own, other)


def slot_rows(ids, e):
    count = ids.shape[1]
    earlier = lax.broadcasted_iota(jnp.int32, (count, count), 0)
    later = lax.broadcasted_iota(jnp.int32, (count, count), 1)
    before = jnp.where(earlier < later, 1.0, 0.0).astype(jnp.bfloat16)
    slot = lax.broadcasted_iota(jnp.int32, (CAP, count), 0).astype(jnp.float32)
    hit = jnp.max(jnp.where(ids == e, 1.0, 0.0), axis=0, keepdims=True)
    hit = jnp.broadcast_to(hit, (CAP, count))
    rank = jnp.dot(hit.astype(jnp.bfloat16), before, preferred_element_type=jnp.float32)
    return jnp.where(rank == slot, hit, 0.0)


def pick_kernel(experts, ids_ref, *refs):
    block_refs, out_ref = refs[:-1], refs[-1]
    for e in range(experts):
        table = slot_rows(ids_ref[...], e)
        start, rows = 0, 0.0
        for ref in block_refs:
            end = start + ref.shape[0]
            part = table[:, start:end].astype(jnp.bfloat16)
            rows += jnp.dot(part, ref[...], preferred_element_type=jnp.float32)
            start = end
        out_ref[e * CAP:(e + 1) * CAP, :] = rows.astype(jnp.bfloat16)


def picked_rows(experts, ids_t, *blocks):
    width, size = blocks[0].shape[1], sum(block.size for block in blocks)
    return pl.pallas_call(
        functools.partial(pick_kernel, experts),
        out_shape=jax.ShapeDtypeStruct((experts * CAP, width), jnp.bfloat16),
        in_specs=[VMEM] * (1 + len(blocks)),
        out_specs=VMEM,
        compiler_params=PARAMS,
        cost_estimate=pl.CostEstimate(
            flops=2 * experts * CAP * size, bytes_accessed=size, transcendentals=0
        ),
    )(ids_t, *blocks)


def hidden_kernel(near_ref, far_ref, gain_ref, gate_ref, up_ref, out_ref):
    rows = jnp.concatenate([near_ref[...], far_ref[...]], axis=0).astype(jnp.float32)
    inverse = lax.rsqrt(jnp.mean(rows * rows, axis=-1, keepdims=True) + 1e-06)
    normed = (rows * inverse * gain_ref[...].astype(jnp.float32)).astype(jnp.bfloat16)
    across = (((1,), (1,)), ((), ()))
    gate = lax.dot_general(normed, gate_ref[...], across, preferred_element_type=jnp.float32)
    up = lax.dot_general(normed, up_ref[...], across, preferred_element_type=jnp.float32)
    out_ref[...] = (gate / (1.0 + jnp.exp(-gate)) * up).astype(jnp.bfloat16)


def hidden_of(near, far, gain, gate_t, up_t):
    rows, (hidden, width) = 2 * near.shape[0], gate_t.shape
    return pl.pallas_call(
        hidden_kernel,
        out_shape=jax.ShapeDtypeStruct((rows, hidden), jnp.bfloat16),
        in_specs=[VMEM] * 5,
        out_specs=VMEM,
        compiler_params=PARAMS,
        cost_estimate=pl.CostEstimate(
            flops=4 * rows * width * hidden, bytes_accessed=4 * width * hidden, transcendentals=0
        ),
    )(near, far, gain, gate_t, up_t)


def down_kernel(own_ref, other_ref, own_down_ref, other_down_ref, out_ref):
    count = own_ref.shape[0] // 2
    other = jnp.concatenate([other_ref[count:], other_ref[:count]], axis=0)
    total = jnp.dot(own_ref[...], own_down_ref[...], preferred_element_type=jnp.float32)
    total += jnp.dot(other, other_down_ref[...], preferred_element_type=jnp.float32)
    out_ref[...] = total.astype(jnp.bfloat16)


def down_of(own, other, own_down, other_down):
    rows, (hidden, half) = own.shape[0], own_down.shape
    return pl.pallas_call(
        down_kernel,
        out_shape=jax.ShapeDtypeStruct((rows, half), jnp.bfloat16),
        in_specs=[VMEM] * 4,
        out_specs=VMEM,
        compiler_params=PARAMS,
        cost_estimate=pl.CostEstimate(
            flops=4 * rows * half * hidden, bytes_accessed=4 * half * hidden, transcendentals=0
        ),
    )(own, other, own_down, other_down)


def join_kernel(*refs):
    back_refs, near_ref, far_ref = refs[:-2], refs[-2], refs[-1]
    total = back_refs[0][...].astype(jnp.float32)
    for ref in back_refs[1:]:
        total = total + ref[...].astype(jnp.float32)
    count = near_ref.shape[0]
    near_ref[...] = total[:count]
    far_ref[...] = total[count:].astype(jnp.bfloat16)


def joined(backs):
    rows, half = backs[0].shape
    return pl.pallas_call(
        join_kernel,
        out_shape=(
            jax.ShapeDtypeStruct((rows // 2, half), jnp.float32),
            jax.ShapeDtypeStruct((rows // 2, half), jnp.bfloat16),
        ),
        in_specs=[VMEM] * len(backs),
        out_specs=(VMEM, VMEM),
        compiler_params=PARAMS,
        cost_estimate=pl.CostEstimate(
            flops=4 * rows * half, bytes_accessed=8 * rows * half, transcendentals=0
        ),
    )(*backs)


def parts_of(value):
    terms = []
    for _ in range(3):
        terms.append(value.astype(jnp.bfloat16))
        value = value - terms[-1].astype(jnp.float32)
    return terms


def base_kernel(experts, gain_ref, ids_ref, weights_ref, *refs):
    block_refs, (out_ref, table_ref) = refs[:-2], refs[-2:]
    ids, weights = ids_ref[...], weights_ref[...]
    count = ids.shape[1]
    zero = jnp.sum(jnp.where(ids >= experts, weights, 0.0), axis=0, keepdims=True)
    same = lax.broadcasted_iota(jnp.int32, (count, count), 0) == lax.broadcasted_iota(
        jnp.int32, (count, count), 1
    )
    zero = jnp.sum(jnp.where(same, zero, 0.0), axis=1, keepdims=True)
    start = 0
    for ref in block_refs:
        end = start + ref.shape[0]
        rows = ref[...].astype(jnp.float32)
        inverse = lax.rsqrt(jnp.mean(rows * rows, axis=-1, keepdims=True) + 1e-06)
        normed = (rows * inverse * gain_ref[...].astype(jnp.float32)).astype(jnp.bfloat16)
        out_ref[start:end] = rows + zero[start:end] * normed.astype(jnp.float32)
        start = end
    tables = []
    for e in range(experts):
        weight = jnp.sum(jnp.where(ids == e, weights, 0.0), axis=0, keepdims=True)
        tables.append(slot_rows(ids, e) * weight)
    terms = parts_of(jnp.concatenate(tables, axis=0).T)
    table_ref[...] = jnp.concatenate(terms + terms[:2], axis=1)


def based(experts, blocks, gain, ids_t, weights_t):
    count, width = ids_t.shape[1], blocks[0].shape[1]
    return pl.pallas_call(
        functools.partial(base_kernel, experts),
        out_shape=(
            jax.ShapeDtypeStruct((count, width), jnp.float32),
            jax.ShapeDtypeStruct((count, 5 * experts * CAP), jnp.bfloat16),
        ),
        in_specs=[VMEM] * (3 + len(blocks)),
        out_specs=(VMEM, VMEM),
        compiler_params=PARAMS,
        cost_estimate=pl.CostEstimate(
            flops=8 * count * width, bytes_accessed=6 * count * width, transcendentals=0
        ),
    )(gain, ids_t, weights_t, *blocks)


def end_kernel(steps, which, base_ref, table_ref, rows_ref, *refs):
    out_ref, done, sems = refs[-3:]
    half = rows_ref.shape[1]
    columns = half // steps
    if which is None:
        which = parity()
    elif which < 0:
        which = 1 - parity()
    copies = []
    for step in range(steps):
        within = slice(step * columns, (step + 1) * columns)
        here = pl.ds(pl.multiple_of(which * half + step * columns, columns), columns)
        high, low, _ = parts_of(rows_ref[:, within].astype(jnp.float32))
        rows = jnp.concatenate([high, high, high, low, low], axis=0)
        added = jnp.dot(table_ref[...], rows, preferred_element_type=jnp.float32)
        done[:, within] = (base_ref[:, here] + added).astype(jnp.bfloat16)
        copies.append(pltpu.make_async_copy(done.at[:, within], out_ref.at[:, here], sems.at[step]))
        copies[-1].start()
    for copy in copies:
        copy.wait()


def ended(base, table, rows, which, out=None):
    count, width = base.shape
    half = rows.shape[1]
    steps = 3
    return pl.pallas_call(
        functools.partial(end_kernel, steps, which),
        out_shape=jax.ShapeDtypeStruct((count, width), jnp.bfloat16),
        in_specs=[VMEM] * 3 + ([] if out is None else [HBM]),
        out_specs=HBM,
        scratch_shapes=[pltpu.VMEM((count, half), jnp.bfloat16), pltpu.SemaphoreType.DMA((steps,))],
        input_output_aliases={} if out is None else {3: 0},
        compiler_params=PARAMS,
        cost_estimate=pl.CostEstimate(
            flops=2 * count * half * table.shape[1], bytes_accessed=6 * count * half,
            transcendentals=0,
        ),
    )(base, table, rows, *(() if out is None else (out,)))


def early_kernel(left_ref, right_ref, out_ref):
    out_ref[...] = left_ref[...].astype(jnp.float32) + right_ref[...].astype(jnp.float32)


def summed_early(left, right):
    return pl.pallas_call(
        early_kernel,
        out_shape=jax.ShapeDtypeStruct(left.shape, jnp.float32),
        in_specs=[VMEM, VMEM],
        out_specs=VMEM,
        compiler_params=PARAMS,
        cost_estimate=pl.CostEstimate(
            flops=left.size, bytes_accessed=128 * left.size, transcendentals=0
        ),
    )(left, right)


def local(blocks, norm_gain, w_gate, w_up, w_down, route_ids, route_weights):
    slice_width = w_gate.shape[2]
    slice_count = HID // slice_width
    sections = lax.axis_size("section")
    devices = lax.axis_size("expert")
    experts = devices // slice_count
    same_slice = [[e * slice_count + k for e in range(experts)] for k in range(slice_count)]
    places = slice_count // 2
    token_count, width = blocks.shape[1:]

    def moved(value, sections_on, flip, side=0):
        pairs = []
        for s in range(sections):
            for d in range(devices):
                target = d ^ (2 * flip + side)
                pairs.append((s * devices + d, (s + sections_on) % sections * devices + target))
        return lax.ppermute(value, ("section", "expert"), pairs)

    def exchanged(rows):
        rows = rows.reshape(experts, CAP, width)
        return lax.all_to_all(
            rows, "expert", split_axis=0, concat_axis=0, tiled=True, axis_index_groups=same_slice
        ).reshape(experts * CAP, width)

    next_ids = moved(route_ids, -1, 0)[0]
    block, down_sent = loaded((blocks[0], w_down[0]), ("whole", "sent"))
    picked = picked_rows(experts, jnp.swapaxes(next_ids, 0, 1), block)
    if experts > 1:
        picked = exchanged(picked)
    own_down, gate_t, up_t, gain = loaded(
        (
            after(w_down[0], picked), jnp.swapaxes(w_gate[0], 0, 1), jnp.swapaxes(w_up[0], 0, 1),
            norm_gain,
        ),
        ("own", "whole", "whole", "whole"),
    )
    other_down = moved(after(down_sent, picked), 0, 0, 1)
    if lax.axis_size("dp") == 2:
        other_down = gathered(other_down, lax.ppermute(other_down, "dp", [(0, 1), (1, 0)]))

    near, far = {}, {}
    near[2] = moved(picked, 1, 2)
    far[0] = moved(picked, 1, 0, 1)
    far[2] = moved(after(near[2], gain), 0, 0, 1)
    near[3] = moved(near[2], 0, 1)
    far[3] = moved(far[2], 0, 1)
    near[1] = moved(after(picked, near[2]), 1, 1)
    cuts = [CAP * 3 // 2]
    arrived = [
        moved(after(piece, far[0], near[2]), 1, 0)
        for piece in jnp.split(blocks[0], cuts)
    ]
    ids_t = jnp.swapaxes(route_ids[0], 0, 1)
    near[0] = picked_rows(experts, ids_t, *arrived)
    base, table = based(experts, arrived, gain, ids_t, jnp.swapaxes(route_weights[0], 0, 1))

    if experts > 1:
        near[0] = exchanged(near[0])
    hidden, part, back = {}, {}, {}
    for k in (2, 3, 1, 0):
        first = {
            2: (near[3],), 3: (part.get(2), arrived[0]), 1: (hidden.get(3),), 0: (hidden.get(1), back.get(2))
        }[k]
        if k == 3:
            far[1] = moved(after(near[1], part[2]), 0, 0, 1)
        hidden[k] = hidden_of(after(near[k], *first), far[k], gain, gate_t, up_t)
        crossed = moved(hidden[k], 0, 0, 1)
        if k == 2:
            crossed = after(crossed, far[3])
        part[k] = down_of(hidden[k], crossed, own_down, other_down)
        back[k] = moved(part[k], 0, k) if k else part[k]
    early = summed_early(back[0], back[2])
    own, others = joined([early, back[3], back[1]])
    others = moved(others, 0, 0, 1)
    if experts > 1:
        own = own.astype(jnp.bfloat16)
        left = parity() == 0
        summed = [jnp.where(left, own, others), jnp.where(left, others, own)]
        summed = exchanged(jnp.concatenate(summed, axis=1))
        out = ended(base, table, summed[:, :width // 2], 0)
        return ended(base, table, summed[:, width // 2:], 1, out)[None]
    out = ended(base, table, own, None)
    return ended(base, table, others, -1, out)[None]


def solution(mesh):
    placed = (
        P("section", ("dp", "expert"), None),
        P("section", None),
        P("section", None, "expert"),
        P("section", None, "expert"),
        P("section", "expert", None),
        P("section", ("dp", "expert"), None),
        P("section", ("dp", "expert"), None),
    )
    return jax.shard_map(
        local,
        mesh=mesh,
        in_specs=placed,
        out_specs=P("section", ("dp", "expert"), None),
        check_vma=False,
    )
```

```python
import functools

import jax
import jax.numpy as jnp
from jax import lax
from jax.experimental import pallas as pl
from jax.experimental.pallas import tpu as pltpu
from jax.sharding import PartitionSpec as P

HID = 1536
CAP = 32
VMEM = pl.BlockSpec(memory_space=pltpu.VMEM)
HBM = pl.BlockSpec(memory_space=pltpu.HBM)
PARAMS = pltpu.CompilerParams(vmem_limit_bytes=24 * 1024 * 1024)


def after(value, *others):
    return lax.optimization_barrier((value, *others))[0]


def load_kernel(count, *refs):
    sources, targets, sems = refs[:count], refs[count:2 * count], refs[2 * count]
    copies = [
        pltpu.make_async_copy(a, b, sems.at[i]) for i, (a, b) in enumerate(zip(sources, targets))
    ]
    for copy in copies:
        copy.start()
    for copy in copies:
        copy.wait()


def loaded(*arrays):
    return pl.pallas_call(
        functools.partial(load_kernel, len(arrays)),
        out_shape=tuple(jax.ShapeDtypeStruct(a.shape, a.dtype) for a in arrays),
        in_specs=[HBM] * len(arrays),
        out_specs=(VMEM,) * len(arrays),
        scratch_shapes=[pltpu.SemaphoreType.DMA((len(arrays),))],
        compiler_params=PARAMS,
        cost_estimate=pl.CostEstimate(flops=0, bytes_accessed=6 * 1024 * 1024, transcendentals=0),
    )(*(pltpu.with_memory_space_constraint(a, pltpu.HBM) for a in arrays))


def slot_rows(ids, e):
    count = ids.shape[1]
    earlier = lax.broadcasted_iota(jnp.int32, (count, count), 0)
    later = lax.broadcasted_iota(jnp.int32, (count, count), 1)
    before = jnp.where(earlier < later, 1.0, 0.0).astype(jnp.bfloat16)
    slot = lax.broadcasted_iota(jnp.int32, (CAP, count), 0).astype(jnp.float32)
    hit = jnp.max(jnp.where(ids == e, 1.0, 0.0), axis=0, keepdims=True)
    hit = jnp.broadcast_to(hit, (CAP, count))
    rank = jnp.dot(hit.astype(jnp.bfloat16), before, preferred_element_type=jnp.float32)
    return jnp.where(rank == slot, hit, 0.0)


def pick_kernel(experts, ids_ref, block_ref, out_ref):
    for e in range(experts):
        table = slot_rows(ids_ref[...], e).astype(jnp.bfloat16)
        rows = jnp.dot(table, block_ref[...], preferred_element_type=jnp.float32)
        out_ref[e * CAP:(e + 1) * CAP, :] = rows.astype(jnp.bfloat16)


def picked_rows(experts, ids_t, block):
    return pl.pallas_call(
        functools.partial(pick_kernel, experts),
        out_shape=jax.ShapeDtypeStruct((experts * CAP, block.shape[1]), jnp.bfloat16),
        in_specs=[VMEM, VMEM],
        out_specs=VMEM,
        compiler_params=PARAMS,
        cost_estimate=pl.CostEstimate(
            flops=2 * experts * CAP * block.size, bytes_accessed=block.size, transcendentals=0
        ),
    )(ids_t, block)


def mlp_kernel(near_ref, far_ref, gain_ref, gate_ref, up_ref, down_ref, near_out, far_out):
    count = near_ref.shape[0]
    rows = jnp.concatenate([near_ref[...], far_ref[...]], axis=0).astype(jnp.float32)
    inverse = lax.rsqrt(jnp.mean(rows * rows, axis=-1, keepdims=True) + 1e-06)
    normed = (rows * inverse * gain_ref[...].astype(jnp.float32)).astype(jnp.bfloat16)
    across = (((1,), (1,)), ((), ()))
    gate = lax.dot_general(normed, gate_ref[...], across, preferred_element_type=jnp.float32)
    up = lax.dot_general(normed, up_ref[...], across, preferred_element_type=jnp.float32)
    hidden = (gate / (1.0 + jnp.exp(-gate)) * up).astype(jnp.bfloat16)
    partial = jnp.dot(hidden, down_ref[...], preferred_element_type=jnp.float32)
    partial = partial.astype(jnp.bfloat16)
    near_out[...] = partial[:count]
    far_out[...] = partial[count:]


def mlp(near, far, gain, gate_t, up_t, down):
    rows = 2 * near.shape[0]
    width, hidden = down.shape[1], down.shape[0]
    out = jax.ShapeDtypeStruct(near.shape, jnp.bfloat16)
    return pl.pallas_call(
        mlp_kernel,
        out_shape=(out, out),
        in_specs=[VMEM] * 6,
        out_specs=(VMEM, VMEM),
        compiler_params=PARAMS,
        cost_estimate=pl.CostEstimate(
            flops=6 * rows * width * hidden, bytes_accessed=6 * width * hidden, transcendentals=0
        ),
    )(near, far, gain, gate_t, up_t, down)


def parts_of(value):
    terms = []
    for _ in range(3):
        terms.append(value.astype(jnp.bfloat16))
        value = value - terms[-1].astype(jnp.float32)
    return terms


def base_kernel(experts, gain_ref, ids_ref, weights_ref, *refs):
    block_refs, (out_ref, table_ref, pick_ref) = refs[:-3], refs[-3:]
    ids, weights = ids_ref[...], weights_ref[...]
    count = ids.shape[1]
    zero = jnp.sum(jnp.where(ids >= experts, weights, 0.0), axis=0, keepdims=True)
    same = lax.broadcasted_iota(jnp.int32, (count, count), 0) == lax.broadcasted_iota(
        jnp.int32, (count, count), 1
    )
    zero = jnp.sum(jnp.where(same, zero, 0.0), axis=1, keepdims=True)
    start = 0
    for ref in block_refs:
        end = start + ref.shape[0]
        rows = ref[...].astype(jnp.float32)
        inverse = lax.rsqrt(jnp.mean(rows * rows, axis=-1, keepdims=True) + 1e-06)
        normed = (rows * inverse * gain_ref[...].astype(jnp.float32)).astype(jnp.bfloat16)
        out_ref[start:end] = rows + zero[start:end] * normed.astype(jnp.float32)
        start = end
    tables = []
    for e in range(experts):
        weight = jnp.sum(jnp.where(ids == e, weights, 0.0), axis=0, keepdims=True)
        slots = slot_rows(ids, e)
        tables.append(slots * weight)
        start, total = 0, 0.0
        for ref in block_refs:
            end = start + ref.shape[0]
            part = slots[:, start:end].astype(jnp.bfloat16)
            total += jnp.dot(part, ref[...], preferred_element_type=jnp.float32)
            start = end
        pick_ref[e * CAP:(e + 1) * CAP, :] = total.astype(jnp.bfloat16)
    terms = parts_of(jnp.concatenate(tables, axis=0).T)
    table_ref[...] = jnp.concatenate(terms + terms[:2], axis=1)


def based(experts, blocks, gain, ids_t, weights_t):
    count, width = ids_t.shape[1], blocks[0].shape[1]
    return pl.pallas_call(
        functools.partial(base_kernel, experts),
        out_shape=(
            jax.ShapeDtypeStruct((count, width), jnp.float32),
            jax.ShapeDtypeStruct((count, 5 * experts * CAP), jnp.bfloat16),
            jax.ShapeDtypeStruct((experts * CAP, width), jnp.bfloat16),
        ),
        in_specs=[VMEM] * (3 + len(blocks)),
        out_specs=(VMEM, VMEM, VMEM),
        compiler_params=PARAMS,
        cost_estimate=pl.CostEstimate(
            flops=8 * count * width, bytes_accessed=6 * count * width, transcendentals=0
        ),
    )(gain, ids_t, weights_t, *blocks)


def end_kernel(columns, base_ref, table_ref, *refs):
    back_refs, out_ref = refs[:-1], refs[-1]
    here = pl.ds(pl.multiple_of(pl.program_id(0) * columns, columns), columns)
    total = back_refs[0][:, here].astype(jnp.float32)
    for ref in back_refs[1:]:
        total = total + ref[:, here].astype(jnp.float32)
    high, low, _ = parts_of(total)
    rows = jnp.concatenate([high, high, high, low, low], axis=0)
    added = jnp.dot(table_ref[...], rows, preferred_element_type=jnp.float32)
    out_ref[...] = (base_ref[:, here] + added).astype(jnp.bfloat16)


def ended(base, table, backs):
    count, width = base.shape
    steps = 3
    columns = width // steps
    return pl.pallas_call(
        functools.partial(end_kernel, columns),
        out_shape=jax.ShapeDtypeStruct((count, width), jnp.bfloat16),
        grid=(steps,),
        in_specs=[VMEM] * (2 + len(backs)),
        out_specs=pl.BlockSpec((count, columns), lambda i: (0, i)),
        compiler_params=PARAMS,
        cost_estimate=pl.CostEstimate(
            flops=2 * count * width * table.shape[0], bytes_accessed=6 * count * width,
            transcendentals=0,
        ),
    )(base, table, *backs)


def early_kernel(left_ref, right_ref, out_ref):
    out_ref[...] = left_ref[...].astype(jnp.float32) + right_ref[...].astype(jnp.float32)


def summed_early(left, right):
    return pl.pallas_call(
        early_kernel,
        out_shape=jax.ShapeDtypeStruct(left.shape, jnp.float32),
        in_specs=[VMEM, VMEM],
        out_specs=VMEM,
        compiler_params=PARAMS,
        cost_estimate=pl.CostEstimate(
            flops=left.size, bytes_accessed=128 * left.size, transcendentals=0
        ),
    )(left, right)


def local(blocks, norm_gain, w_gate, w_up, w_down, route_ids, route_weights):
    slice_width = w_gate.shape[2]
    slice_count = HID // slice_width
    sections = lax.axis_size("section")
    devices = lax.axis_size("expert")
    experts = devices // slice_count
    same_slice = [[e * slice_count + k for e in range(experts)] for k in range(slice_count)]
    places = slice_count // 2
    token_count, width = blocks.shape[1:]

    def moved(value, sections_on, flip, side=0):
        pairs = []
        for s in range(sections):
            for d in range(devices):
                target = d ^ (2 * flip + side)
                pairs.append((s * devices + d, (s + sections_on) % sections * devices + target))
        return lax.ppermute(value, ("section", "expert"), pairs)

    def exchanged(rows):
        rows = rows.reshape(experts, CAP, width)
        return lax.all_to_all(
            rows, "expert", split_axis=0, concat_axis=0, tiled=True, axis_index_groups=same_slice
        ).reshape(experts * CAP, width)

    next_ids = moved(route_ids, -1, 0)[0]
    block, = loaded(blocks[0])
    picked = picked_rows(experts, jnp.swapaxes(next_ids, 0, 1), block)
    if experts > 1:
        picked = exchanged(picked)
    gate_t, up_t, down, gain = loaded(
        after(jnp.swapaxes(w_gate[0], 0, 1), picked), jnp.swapaxes(w_up[0], 0, 1), w_down[0], norm_gain
    )

    near, far = {}, {}
    near[2] = moved(picked, 1, 2)
    far[0] = moved(picked, 1, 0, 1)
    far[2] = moved(after(near[2], gain), 0, 0, 1)
    near[3] = moved(near[2], 0, 1)
    far[3] = moved(far[2], 0, 1)
    near[1] = moved(after(picked, near[2]), 1, 1)
    cuts = [CAP * 3 // 2]
    arrived = [
        moved(after(piece, far[0], near[2]), 1, 0)
        for piece in jnp.split(blocks[0], cuts)
    ]
    base, table, near[0] = based(
        experts, arrived, gain, jnp.swapaxes(route_ids[0], 0, 1),
        jnp.swapaxes(route_weights[0], 0, 1),
    )

    if experts > 1:
        near[0] = exchanged(near[0])
    own, other = {}, {}
    for k in (2, 3, 1, 0):
        first = {2: (near[3],), 3: (other.get(2), arrived[0]), 1: (own.get(3),), 0: (own.get(1), other.get(3))}[k]
        if k == 3:
            far[1] = moved(after(near[1], own[2]), 0, 0, 1)
        own[k], sent = mlp(after(near[k], *first), far[k], gain, gate_t, up_t, down)
        other[k] = moved(sent, 0, 0, 1)
    both = {
        k: (own[k].astype(jnp.float32) + other[k].astype(jnp.float32)).astype(jnp.bfloat16)
        for k in (2, 3, 1)
    }
    early = summed_early(own[0], moved(both[2], 0, 2))
    backs = [
        early, moved(both[3], 0, 3), moved(both[1], 0, 1), other[0],
    ]
    if experts > 1:
        backs = [exchanged(sum(back.astype(jnp.float32) for back in backs).astype(jnp.bfloat16))]
    return ended(base, table, backs)[None]


def solution(mesh):
    placed = (
        P("section", ("dp", "expert"), None),
        P("section", None),
        P("section", None, "expert"),
        P("section", None, "expert"),
        P("section", "expert", None),
        P("section", ("dp", "expert"), None),
        P("section", ("dp", "expert"), None),
    )
    return jax.shard_map(
        local,
        mesh=mesh,
        in_specs=placed,
        out_specs=P("section", ("dp", "expert"), None),
        check_vma=False,
    )
```

```python
import functools

import jax
import jax.numpy as jnp
from jax import lax
from jax.experimental import pallas as pl
from jax.experimental.pallas import tpu as pltpu
from jax.sharding import PartitionSpec as P

HID = 1536
CAP = 32
VMEM = pl.BlockSpec(memory_space=pltpu.VMEM)
HBM = pl.BlockSpec(memory_space=pltpu.HBM)
PARAMS = pltpu.CompilerParams(vmem_limit_bytes=24 * 1024 * 1024)


def after(value, *others):
    return lax.optimization_barrier((value, *others))[0]


def load_kernel(groups, *refs):
    count = sum(groups)
    sources, targets, sems = refs[:count], refs[count:-1], refs[-1]
    copies, i = [], 0
    for group, target in zip(groups, targets):
        start = 0
        for source in sources[i:i + group]:
            rows = target.at[pl.ds(start, source.shape[0])]
            copies.append(pltpu.make_async_copy(source, rows, sems.at[i]))
            start, i = start + source.shape[0], i + 1
    for copy in copies:
        copy.start()
    for copy in copies:
        copy.wait()


def loaded(*groups):
    arrays = [a for group in groups for a in group]
    return pl.pallas_call(
        functools.partial(load_kernel, [len(group) for group in groups]),
        out_shape=tuple(
            jax.ShapeDtypeStruct((sum(a.shape[0] for a in group),) + group[0].shape[1:], group[0].dtype)
            for group in groups
        ),
        in_specs=[HBM] * len(arrays),
        out_specs=(VMEM,) * len(groups),
        scratch_shapes=[pltpu.SemaphoreType.DMA((len(arrays),))],
        compiler_params=PARAMS,
        cost_estimate=pl.CostEstimate(flops=0, bytes_accessed=6 * 1024 * 1024, transcendentals=0),
    )(*(pltpu.with_memory_space_constraint(a, pltpu.HBM) for a in arrays))


def slot_rows(ids, e):
    count = ids.shape[1]
    earlier = lax.broadcasted_iota(jnp.int32, (count, count), 0)
    later = lax.broadcasted_iota(jnp.int32, (count, count), 1)
    before = jnp.where(earlier < later, 1.0, 0.0).astype(jnp.bfloat16)
    slot = lax.broadcasted_iota(jnp.int32, (CAP, count), 0).astype(jnp.float32)
    hit = jnp.max(jnp.where(ids == e, 1.0, 0.0), axis=0, keepdims=True)
    hit = jnp.broadcast_to(hit, (CAP, count))
    rank = jnp.dot(hit.astype(jnp.bfloat16), before, preferred_element_type=jnp.float32)
    return jnp.where(rank == slot, hit, 0.0)


def pick_kernel(experts, ids_ref, block_ref, out_ref):
    for e in range(experts):
        table = slot_rows(ids_ref[...], e).astype(jnp.bfloat16)
        rows = jnp.dot(table, block_ref[...], preferred_element_type=jnp.float32)
        out_ref[e * CAP:(e + 1) * CAP, :] = rows.astype(jnp.bfloat16)


def picked_rows(experts, ids_t, block):
    return pl.pallas_call(
        functools.partial(pick_kernel, experts),
        out_shape=jax.ShapeDtypeStruct((experts * CAP, block.shape[1]), jnp.bfloat16),
        in_specs=[VMEM, VMEM],
        out_specs=VMEM,
        compiler_params=PARAMS,
        cost_estimate=pl.CostEstimate(
            flops=2 * experts * CAP * block.size, bytes_accessed=block.size, transcendentals=0
        ),
    )(ids_t, block)


def mlp_kernel(near_ref, far_ref, gain_ref, both_ref, down_ref, near_out, far_out):
    count, hidden = near_ref.shape[0], down_ref.shape[0]
    rows = jnp.concatenate([near_ref[...], far_ref[...]], axis=0).astype(jnp.float32)
    inverse = lax.rsqrt(jnp.mean(rows * rows, axis=-1, keepdims=True) + 1e-06)
    normed = (rows * inverse * gain_ref[...].astype(jnp.float32)).astype(jnp.bfloat16)
    across = (((1,), (1,)), ((), ()))
    both = lax.dot_general(normed, both_ref[...], across, preferred_element_type=jnp.float32)
    gate, up = both[:, :hidden], both[:, hidden:]
    inner = (gate / (1.0 + jnp.exp(-gate)) * up).astype(jnp.bfloat16)
    partial = jnp.dot(inner, down_ref[...], preferred_element_type=jnp.float32)
    partial = partial.astype(jnp.bfloat16)
    near_out[...] = partial[:count]
    far_out[...] = partial[count:]


def mlp(near, far, gain, both_t, down):
    rows = 2 * near.shape[0]
    width, hidden = down.shape[1], down.shape[0]
    out = jax.ShapeDtypeStruct(near.shape, jnp.bfloat16)
    return pl.pallas_call(
        mlp_kernel,
        out_shape=(out, out),
        in_specs=[VMEM] * 5,
        out_specs=(VMEM, VMEM),
        compiler_params=PARAMS,
        cost_estimate=pl.CostEstimate(
            flops=6 * rows * width * hidden, bytes_accessed=6 * width * hidden, transcendentals=0
        ),
    )(near, far, gain, both_t, down)


def parts_of(value):
    terms = []
    for _ in range(3):
        terms.append(value.astype(jnp.bfloat16))
        value = value - terms[-1].astype(jnp.float32)
    return terms


def base_kernel(experts, gain_ref, ids_ref, weights_ref, *refs):
    block_refs, (out_ref, table_ref, pick_ref) = refs[:-3], refs[-3:]
    ids, weights = ids_ref[...], weights_ref[...]
    count = ids.shape[1]
    zero = jnp.sum(jnp.where(ids >= experts, weights, 0.0), axis=0, keepdims=True)
    same = lax.broadcasted_iota(jnp.int32, (count, count), 0) == lax.broadcasted_iota(
        jnp.int32, (count, count), 1
    )
    zero = jnp.sum(jnp.where(same, zero, 0.0), axis=1, keepdims=True)
    start = 0
    for ref in block_refs:
        end = start + ref.shape[0]
        rows = ref[...].astype(jnp.float32)
        inverse = lax.rsqrt(jnp.mean(rows * rows, axis=-1, keepdims=True) + 1e-06)
        normed = (rows * inverse * gain_ref[...].astype(jnp.float32)).astype(jnp.bfloat16)
        out_ref[start:end] = rows + zero[start:end] * normed.astype(jnp.float32)
        start = end
    tables = []
    for e in range(experts):
        weight = jnp.sum(jnp.where(ids == e, weights, 0.0), axis=0, keepdims=True)
        slots = slot_rows(ids, e)
        tables.append(slots * weight)
        start, total = 0, 0.0
        for ref in block_refs:
            end = start + ref.shape[0]
            part = slots[:, start:end].astype(jnp.bfloat16)
            total += jnp.dot(part, ref[...], preferred_element_type=jnp.float32)
            start = end
        pick_ref[e * CAP:(e + 1) * CAP, :] = total.astype(jnp.bfloat16)
    terms = parts_of(jnp.concatenate(tables, axis=0).T)
    table_ref[...] = jnp.concatenate(terms + terms[:2], axis=1)


def based(experts, blocks, gain, ids_t, weights_t):
    count, width = ids_t.shape[1], blocks[0].shape[1]
    return pl.pallas_call(
        functools.partial(base_kernel, experts),
        out_shape=(
            jax.ShapeDtypeStruct((count, width), jnp.float32),
            jax.ShapeDtypeStruct((count, 5 * experts * CAP), jnp.bfloat16),
            jax.ShapeDtypeStruct((experts * CAP, width), jnp.bfloat16),
        ),
        in_specs=[VMEM] * (3 + len(blocks)),
        out_specs=(VMEM, VMEM, VMEM),
        compiler_params=PARAMS,
        cost_estimate=pl.CostEstimate(
            flops=8 * count * width, bytes_accessed=6 * count * width, transcendentals=0
        ),
    )(gain, ids_t, weights_t, *blocks)


def end_kernel(steps, base_ref, table_ref, *refs):
    back_refs, (out_ref, done, sems) = refs[:-3], refs[-3:]
    columns = base_ref.shape[1] // steps
    copies = []
    for step in range(steps):
        here = slice(step * columns, (step + 1) * columns)
        total = back_refs[0][:, here].astype(jnp.float32)
        for ref in back_refs[1:]:
            total = total + ref[:, here].astype(jnp.float32)
        high, low, _ = parts_of(total)
        rows = jnp.concatenate([high, high, high, low, low], axis=0)
        added = jnp.dot(table_ref[...], rows, preferred_element_type=jnp.float32)
        done[:, here] = (base_ref[:, here] + added).astype(jnp.bfloat16)
        copies.append(
            pltpu.make_async_copy(done.at[:, here], out_ref.at[:, here], sems.at[step])
        )
        copies[-1].start()
    for copy in copies:
        copy.wait()


def ended(base, table, backs):
    count, width = base.shape
    steps = 6
    return pl.pallas_call(
        functools.partial(end_kernel, steps),
        out_shape=jax.ShapeDtypeStruct((count, width), jnp.bfloat16),
        in_specs=[VMEM] * (2 + len(backs)),
        out_specs=HBM,
        scratch_shapes=[pltpu.VMEM((count, width), jnp.bfloat16), pltpu.SemaphoreType.DMA((steps,))],
        compiler_params=PARAMS,
        cost_estimate=pl.CostEstimate(
            flops=2 * count * width * table.shape[0], bytes_accessed=6 * count * width,
            transcendentals=0,
        ),
    )(base, table, *backs)


def early_kernel(left_ref, right_ref, out_ref):
    out_ref[...] = left_ref[...].astype(jnp.float32) + right_ref[...].astype(jnp.float32)


def summed_early(left, right):
    return pl.pallas_call(
        early_kernel,
        out_shape=jax.ShapeDtypeStruct(left.shape, jnp.float32),
        in_specs=[VMEM, VMEM],
        out_specs=VMEM,
        compiler_params=PARAMS,
        cost_estimate=pl.CostEstimate(
            flops=left.size, bytes_accessed=128 * left.size, transcendentals=0
        ),
    )(left, right)


def local(blocks, norm_gain, w_gate, w_up, w_down, route_ids, route_weights):
    slice_width = w_gate.shape[2]
    slice_count = HID // slice_width
    sections = lax.axis_size("section")
    devices = lax.axis_size("expert")
    experts = devices // slice_count
    same_slice = [[e * slice_count + k for e in range(experts)] for k in range(slice_count)]
    places = slice_count // 2
    token_count, width = blocks.shape[1:]

    def moved(value, sections_on, flip, side=0):
        pairs = []
        for s in range(sections):
            for d in range(devices):
                target = d ^ (2 * flip + side)
                pairs.append((s * devices + d, (s + sections_on) % sections * devices + target))
        return lax.ppermute(value, ("section", "expert"), pairs)

    def exchanged(rows):
        rows = rows.reshape(experts, CAP, width)
        return lax.all_to_all(
            rows, "expert", split_axis=0, concat_axis=0, tiled=True, axis_index_groups=same_slice
        ).reshape(experts * CAP, width)

    next_ids = moved(route_ids, -1, 0)[0]
    block, = loaded((blocks[0],))
    picked = picked_rows(experts, jnp.swapaxes(next_ids, 0, 1), block)
    if experts > 1:
        picked = exchanged(picked)
    both_t, down, gain = loaded(
        (after(jnp.swapaxes(w_gate[0], 0, 1), picked), jnp.swapaxes(w_up[0], 0, 1)), (w_down[0],), (norm_gain,)
    )

    near, far = {}, {}
    near[2] = moved(picked, 1, 2)
    far[0] = moved(picked, 1, 0, 1)
    far[2] = moved(after(near[2], gain), 0, 0, 1)
    near[3] = moved(near[2], 0, 1)
    far[3] = moved(far[2], 0, 1)
    near[1] = moved(after(picked, near[2]), 1, 1)
    cuts = [CAP * 3 // 2]
    arrived = [
        moved(after(piece, far[0], near[2]), 1, 0)
        for piece in jnp.split(blocks[0], cuts)
    ]
    base, table, near[0] = based(
        experts, arrived, gain, jnp.swapaxes(route_ids[0], 0, 1),
        jnp.swapaxes(route_weights[0], 0, 1),
    )

    if experts > 1:
        near[0] = exchanged(near[0])
    own, other = {}, {}
    for k in (2, 3, 1, 0):
        first = {2: (near[3],), 3: (other.get(2), arrived[0]), 1: (own.get(3),), 0: (own.get(1), other.get(3))}[k]
        if k == 3:
            far[1] = moved(after(near[1], own[2]), 0, 0, 1)
        own[k], sent = mlp(after(near[k], *first), far[k], gain, both_t, down)
        other[k] = moved(sent, 0, 0, 1)
    both = {
        k: (own[k].astype(jnp.float32) + other[k].astype(jnp.float32)).astype(jnp.bfloat16)
        for k in (2, 3, 1)
    }
    early = summed_early(own[0], moved(both[2], 0, 2))
    backs = [
        early, moved(both[3], 0, 3), moved(both[1], 0, 1), other[0],
    ]
    if experts > 1:
        backs = [exchanged(sum(back.astype(jnp.float32) for back in backs).astype(jnp.bfloat16))]
    return ended(base, table, backs)[None]


def solution(mesh):
    placed = (
        P("section", ("dp", "expert"), None),
        P("section", None),
        P("section", None, "expert"),
        P("section", None, "expert"),
        P("section", "expert", None),
        P("section", ("dp", "expert"), None),
        P("section", ("dp", "expert"), None),
    )
    return jax.shard_map(
        local,
        mesh=mesh,
        in_specs=placed,
        out_specs=P("section", ("dp", "expert"), None),
        check_vma=False,
    )
```

```python
import functools

import jax
import jax.numpy as jnp
from jax import lax
from jax.experimental import pallas as pl
from jax.experimental.pallas import tpu as pltpu
from jax.sharding import PartitionSpec as P

HID = 1536
CAP = 32
VMEM = pl.BlockSpec(memory_space=pltpu.VMEM)
HBM = pl.BlockSpec(memory_space=pltpu.HBM)
PARAMS = pltpu.CompilerParams(vmem_limit_bytes=24 * 1024 * 1024)


def after(value, *others):
    return lax.optimization_barrier((value, *others))[0]


def load_kernel(count, *refs):
    sources, targets, sems = refs[:count], refs[count:2 * count], refs[2 * count]
    copies = [
        pltpu.make_async_copy(a, b, sems.at[i]) for i, (a, b) in enumerate(zip(sources, targets))
    ]
    for copy in copies:
        copy.start()
    for copy in copies:
        copy.wait()


def loaded(*arrays):
    return pl.pallas_call(
        functools.partial(load_kernel, len(arrays)),
        out_shape=tuple(jax.ShapeDtypeStruct(a.shape, a.dtype) for a in arrays),
        in_specs=[HBM] * len(arrays),
        out_specs=(VMEM,) * len(arrays),
        scratch_shapes=[pltpu.SemaphoreType.DMA((len(arrays),))],
        compiler_params=PARAMS,
        cost_estimate=pl.CostEstimate(flops=0, bytes_accessed=6 * 1024 * 1024, transcendentals=0),
    )(*(pltpu.with_memory_space_constraint(a, pltpu.HBM) for a in arrays))


def slot_rows(ids, e):
    count = ids.shape[1]
    earlier = lax.broadcasted_iota(jnp.int32, (count, count), 0)
    later = lax.broadcasted_iota(jnp.int32, (count, count), 1)
    before = jnp.where(earlier < later, 1.0, 0.0).astype(jnp.bfloat16)
    slot = lax.broadcasted_iota(jnp.int32, (CAP, count), 0).astype(jnp.float32)
    hit = jnp.max(jnp.where(ids == e, 1.0, 0.0), axis=0, keepdims=True)
    hit = jnp.broadcast_to(hit, (CAP, count))
    rank = jnp.dot(hit.astype(jnp.bfloat16), before, preferred_element_type=jnp.float32)
    return jnp.where(rank == slot, hit, 0.0)


def pick_kernel(experts, ids_ref, block_ref, out_ref):
    for e in range(experts):
        table = slot_rows(ids_ref[...], e).astype(jnp.bfloat16)
        rows = jnp.dot(table, block_ref[...], preferred_element_type=jnp.float32)
        out_ref[e * CAP:(e + 1) * CAP, :] = rows.astype(jnp.bfloat16)


def picked_rows(experts, ids_t, block):
    return pl.pallas_call(
        functools.partial(pick_kernel, experts),
        out_shape=jax.ShapeDtypeStruct((experts * CAP, block.shape[1]), jnp.bfloat16),
        in_specs=[VMEM, VMEM],
        out_specs=VMEM,
        compiler_params=PARAMS,
        cost_estimate=pl.CostEstimate(
            flops=2 * experts * CAP * block.size, bytes_accessed=block.size, transcendentals=0
        ),
    )(ids_t, block)


def mlp_kernel(near_ref, far_ref, gain_ref, gate_ref, up_ref, down_ref, near_out, far_out):
    count = near_ref.shape[0]
    rows = jnp.concatenate([near_ref[...], far_ref[...]], axis=0).astype(jnp.float32)
    inverse = lax.rsqrt(jnp.mean(rows * rows, axis=-1, keepdims=True) + 1e-06)
    normed = (rows * inverse * gain_ref[...].astype(jnp.float32)).astype(jnp.bfloat16)
    across = (((1,), (1,)), ((), ()))
    gate = lax.dot_general(normed, gate_ref[...], across, preferred_element_type=jnp.float32)
    up = lax.dot_general(normed, up_ref[...], across, preferred_element_type=jnp.float32)
    hidden = (gate / (1.0 + jnp.exp(-gate)) * up).astype(jnp.bfloat16)
    partial = jnp.dot(hidden, down_ref[...], preferred_element_type=jnp.float32)
    partial = partial.astype(jnp.bfloat16)
    near_out[...] = partial[:count]
    far_out[...] = partial[count:]


def mlp(near, far, gain, gate_t, up_t, down):
    rows = 2 * near.shape[0]
    width, hidden = down.shape[1], down.shape[0]
    out = jax.ShapeDtypeStruct(near.shape, jnp.bfloat16)
    return pl.pallas_call(
        mlp_kernel,
        out_shape=(out, out),
        in_specs=[VMEM] * 6,
        out_specs=(VMEM, VMEM),
        compiler_params=PARAMS,
        cost_estimate=pl.CostEstimate(
            flops=6 * rows * width * hidden, bytes_accessed=6 * width * hidden, transcendentals=0
        ),
    )(near, far, gain, gate_t, up_t, down)


def parts_of(value):
    terms = []
    for _ in range(3):
        terms.append(value.astype(jnp.bfloat16))
        value = value - terms[-1].astype(jnp.float32)
    return terms


def base_kernel(experts, gain_ref, ids_ref, weights_ref, *refs):
    block_refs, (out_ref, table_ref, pick_ref) = refs[:-3], refs[-3:]
    ids, weights = ids_ref[...], weights_ref[...]
    count = ids.shape[1]
    zero = jnp.sum(jnp.where(ids >= experts, weights, 0.0), axis=0, keepdims=True)
    same = lax.broadcasted_iota(jnp.int32, (count, count), 0) == lax.broadcasted_iota(
        jnp.int32, (count, count), 1
    )
    zero = jnp.sum(jnp.where(same, zero, 0.0), axis=1, keepdims=True)
    start = 0
    for ref in block_refs:
        end = start + ref.shape[0]
        rows = ref[...].astype(jnp.float32)
        inverse = lax.rsqrt(jnp.mean(rows * rows, axis=-1, keepdims=True) + 1e-06)
        normed = (rows * inverse * gain_ref[...].astype(jnp.float32)).astype(jnp.bfloat16)
        out_ref[start:end] = rows + zero[start:end] * normed.astype(jnp.float32)
        start = end
    tables = []
    for e in range(experts):
        weight = jnp.sum(jnp.where(ids == e, weights, 0.0), axis=0, keepdims=True)
        slots = slot_rows(ids, e)
        tables.append(slots * weight)
        start, total = 0, 0.0
        for ref in block_refs:
            end = start + ref.shape[0]
            part = slots[:, start:end].astype(jnp.bfloat16)
            total += jnp.dot(part, ref[...], preferred_element_type=jnp.float32)
            start = end
        pick_ref[e * CAP:(e + 1) * CAP, :] = total.astype(jnp.bfloat16)
    terms = parts_of(jnp.concatenate(tables, axis=0).T)
    table_ref[...] = jnp.concatenate(terms + terms[:2], axis=1)


def based(experts, blocks, gain, ids_t, weights_t):
    count, width = ids_t.shape[1], blocks[0].shape[1]
    return pl.pallas_call(
        functools.partial(base_kernel, experts),
        out_shape=(
            jax.ShapeDtypeStruct((count, width), jnp.float32),
            jax.ShapeDtypeStruct((count, 5 * experts * CAP), jnp.bfloat16),
            jax.ShapeDtypeStruct((experts * CAP, width), jnp.bfloat16),
        ),
        in_specs=[VMEM] * (3 + len(blocks)),
        out_specs=(VMEM, VMEM, VMEM),
        compiler_params=PARAMS,
        cost_estimate=pl.CostEstimate(
            flops=8 * count * width, bytes_accessed=6 * count * width, transcendentals=0
        ),
    )(gain, ids_t, weights_t, *blocks)


def end_kernel(steps, base_ref, table_ref, *refs):
    back_refs, (out_ref, done, sems) = refs[:-3], refs[-3:]
    columns = base_ref.shape[1] // steps
    copies = []
    for step in range(steps):
        here = slice(step * columns, (step + 1) * columns)
        total = back_refs[0][:, here].astype(jnp.float32)
        for ref in back_refs[1:]:
            total = total + ref[:, here].astype(jnp.float32)
        high, low, _ = parts_of(total)
        rows = jnp.concatenate([high, high, high, low, low], axis=0)
        added = jnp.dot(table_ref[...], rows, preferred_element_type=jnp.float32)
        done[:, here] = (base_ref[:, here] + added).astype(jnp.bfloat16)
        copies.append(
            pltpu.make_async_copy(done.at[:, here], out_ref.at[:, here], sems.at[step])
        )
        copies[-1].start()
    for copy in copies:
        copy.wait()


def ended(base, table, backs):
    count, width = base.shape
    steps = 6
    return pl.pallas_call(
        functools.partial(end_kernel, steps),
        out_shape=jax.ShapeDtypeStruct((count, width), jnp.bfloat16),
        in_specs=[VMEM] * (2 + len(backs)),
        out_specs=HBM,
        scratch_shapes=[pltpu.VMEM((count, width), jnp.bfloat16), pltpu.SemaphoreType.DMA((steps,))],
        compiler_params=PARAMS,
        cost_estimate=pl.CostEstimate(
            flops=2 * count * width * table.shape[0], bytes_accessed=6 * count * width,
            transcendentals=0,
        ),
    )(base, table, *backs)


def early_kernel(left_ref, right_ref, out_ref):
    out_ref[...] = left_ref[...].astype(jnp.float32) + right_ref[...].astype(jnp.float32)


def summed_early(left, right):
    return pl.pallas_call(
        early_kernel,
        out_shape=jax.ShapeDtypeStruct(left.shape, jnp.float32),
        in_specs=[VMEM, VMEM],
        out_specs=VMEM,
        compiler_params=PARAMS,
        cost_estimate=pl.CostEstimate(
            flops=left.size, bytes_accessed=128 * left.size, transcendentals=0
        ),
    )(left, right)


def local(blocks, norm_gain, w_gate, w_up, w_down, route_ids, route_weights):
    slice_width = w_gate.shape[2]
    slice_count = HID // slice_width
    sections = lax.axis_size("section")
    devices = lax.axis_size("expert")
    experts = devices // slice_count
    same_slice = [[e * slice_count + k for e in range(experts)] for k in range(slice_count)]
    places = slice_count // 2
    token_count, width = blocks.shape[1:]

    def moved(value, sections_on, flip, side=0):
        pairs = []
        for s in range(sections):
            for d in range(devices):
                target = d ^ (2 * flip + side)
                pairs.append((s * devices + d, (s + sections_on) % sections * devices + target))
        return lax.ppermute(value, ("section", "expert"), pairs)

    def exchanged(rows):
        rows = rows.reshape(experts, CAP, width)
        return lax.all_to_all(
            rows, "expert", split_axis=0, concat_axis=0, tiled=True, axis_index_groups=same_slice
        ).reshape(experts * CAP, width)

    next_ids = moved(route_ids, -1, 0)[0]
    block, = loaded(blocks[0])
    picked = picked_rows(experts, jnp.swapaxes(next_ids, 0, 1), block)
    if experts > 1:
        picked = exchanged(picked)
    gate_t, up_t, down, gain = loaded(
        after(jnp.swapaxes(w_gate[0], 0, 1), picked), jnp.swapaxes(w_up[0], 0, 1), w_down[0], norm_gain
    )

    near, far = {}, {}
    near[2] = moved(picked, 1, 2)
    far[0] = moved(picked, 1, 0, 1)
    far[2] = moved(after(near[2], gain), 0, 0, 1)
    near[3] = moved(near[2], 0, 1)
    far[3] = moved(far[2], 0, 1)
    near[1] = moved(after(picked, near[2]), 1, 1)
    cuts = [CAP * 3 // 2]
    arrived = [
        moved(after(piece, far[0], near[2]), 1, 0)
        for piece in jnp.split(blocks[0], cuts)
    ]
    base, table, near[0] = based(
        experts, arrived, gain, jnp.swapaxes(route_ids[0], 0, 1),
        jnp.swapaxes(route_weights[0], 0, 1),
    )

    if experts > 1:
        near[0] = exchanged(near[0])
    own, other = {}, {}
    for k in (2, 3, 1, 0):
        first = {2: (near[3],), 3: (other.get(2), arrived[0]), 1: (own.get(3),), 0: (own.get(1), other.get(3))}[k]
        if k == 3:
            far[1] = moved(after(near[1], own[2]), 0, 0, 1)
        own[k], sent = mlp(after(near[k], *first), far[k], gain, gate_t, up_t, down)
        other[k] = moved(sent, 0, 0, 1)
    both = {
        k: (own[k].astype(jnp.float32) + other[k].astype(jnp.float32)).astype(jnp.bfloat16)
        for k in (2, 3, 1)
    }
    early = summed_early(own[0], moved(both[2], 0, 2))
    backs = [
        early, moved(both[3], 0, 3), moved(both[1], 0, 1), other[0],
    ]
    if experts > 1:
        backs = [exchanged(sum(back.astype(jnp.float32) for back in backs).astype(jnp.bfloat16))]
    return ended(base, table, backs)[None]


def solution(mesh):
    placed = (
        P("section", ("dp", "expert"), None),
        P("section", None),
        P("section", None, "expert"),
        P("section", None, "expert"),
        P("section", "expert", None),
        P("section", ("dp", "expert"), None),
        P("section", ("dp", "expert"), None),
    )
    return jax.shard_map(
        local,
        mesh=mesh,
        in_specs=placed,
        out_specs=P("section", ("dp", "expert"), None),
        check_vma=False,
    )
```

```python
import functools

import jax
import jax.numpy as jnp
from jax import lax
from jax.experimental import pallas as pl
from jax.experimental.pallas import tpu as pltpu
from jax.sharding import PartitionSpec as P

HID = 1536
CAP = 32
VMEM = pl.BlockSpec(memory_space=pltpu.VMEM)
HBM = pl.BlockSpec(memory_space=pltpu.HBM)
PARAMS = pltpu.CompilerParams(vmem_limit_bytes=24 * 1024 * 1024)


def after(value, *others):
    return lax.optimization_barrier((value, *others))[0]


def load_kernel(count, *refs):
    sources, targets, sems = refs[:count], refs[count:2 * count], refs[2 * count]
    copies = [
        pltpu.make_async_copy(a, b, sems.at[i]) for i, (a, b) in enumerate(zip(sources, targets))
    ]
    for copy in copies:
        copy.start()
    for copy in copies:
        copy.wait()


def loaded(*arrays):
    return pl.pallas_call(
        functools.partial(load_kernel, len(arrays)),
        out_shape=tuple(jax.ShapeDtypeStruct(a.shape, a.dtype) for a in arrays),
        in_specs=[HBM] * len(arrays),
        out_specs=(VMEM,) * len(arrays),
        scratch_shapes=[pltpu.SemaphoreType.DMA((len(arrays),))],
        compiler_params=PARAMS,
        cost_estimate=pl.CostEstimate(flops=0, bytes_accessed=6 * 1024 * 1024, transcendentals=0),
    )(*(pltpu.with_memory_space_constraint(a, pltpu.HBM) for a in arrays))


def slot_rows(ids, e):
    count = ids.shape[1]
    earlier = lax.broadcasted_iota(jnp.int32, (count, count), 0)
    later = lax.broadcasted_iota(jnp.int32, (count, count), 1)
    before = jnp.where(earlier < later, 1.0, 0.0).astype(jnp.bfloat16)
    slot = lax.broadcasted_iota(jnp.int32, (CAP, count), 0).astype(jnp.float32)
    hit = jnp.max(jnp.where(ids == e, 1.0, 0.0), axis=0, keepdims=True)
    hit = jnp.broadcast_to(hit, (CAP, count))
    rank = jnp.dot(hit.astype(jnp.bfloat16), before, preferred_element_type=jnp.float32)
    return jnp.where(rank == slot, hit, 0.0)


def pick_kernel(experts, ids_ref, block_ref, out_ref):
    for e in range(experts):
        table = slot_rows(ids_ref[...], e).astype(jnp.bfloat16)
        rows = jnp.dot(table, block_ref[...], preferred_element_type=jnp.float32)
        out_ref[e * CAP:(e + 1) * CAP, :] = rows.astype(jnp.bfloat16)


def picked_rows(experts, ids_t, block):
    return pl.pallas_call(
        functools.partial(pick_kernel, experts),
        out_shape=jax.ShapeDtypeStruct((experts * CAP, block.shape[1]), jnp.bfloat16),
        in_specs=[VMEM, VMEM],
        out_specs=VMEM,
        compiler_params=PARAMS,
        cost_estimate=pl.CostEstimate(
            flops=2 * experts * CAP * block.size, bytes_accessed=block.size, transcendentals=0
        ),
    )(ids_t, block)


def mlp_kernel(near_ref, far_ref, gain_ref, gate_ref, up_ref, down_ref, near_out, far_out):
    count = near_ref.shape[0]
    rows = jnp.concatenate([near_ref[...], far_ref[...]], axis=0).astype(jnp.float32)
    inverse = lax.rsqrt(jnp.mean(rows * rows, axis=-1, keepdims=True) + 1e-06)
    normed = (rows * inverse * gain_ref[...].astype(jnp.float32)).astype(jnp.bfloat16)
    across = (((1,), (1,)), ((), ()))
    gate = lax.dot_general(gate_ref[...], normed, across, preferred_element_type=jnp.float32)
    up = lax.dot_general(up_ref[...], normed, across, preferred_element_type=jnp.float32)
    hidden = (gate / (1.0 + jnp.exp(-gate)) * up).astype(jnp.bfloat16)
    first = (((0,), (0,)), ((), ()))
    partial = lax.dot_general(hidden, down_ref[...], first, preferred_element_type=jnp.float32)
    partial = partial.astype(jnp.bfloat16)
    near_out[...] = partial[:count]
    far_out[...] = partial[count:]


def mlp(near, far, gain, gate_t, up_t, down):
    rows = 2 * near.shape[0]
    width, hidden = down.shape[1], down.shape[0]
    out = jax.ShapeDtypeStruct(near.shape, jnp.bfloat16)
    return pl.pallas_call(
        mlp_kernel,
        out_shape=(out, out),
        in_specs=[VMEM] * 6,
        out_specs=(VMEM, VMEM),
        compiler_params=PARAMS,
        cost_estimate=pl.CostEstimate(
            flops=6 * rows * width * hidden, bytes_accessed=6 * width * hidden, transcendentals=0
        ),
    )(near, far, gain, gate_t, up_t, down)


def parts_of(value):
    terms = []
    for _ in range(3):
        terms.append(value.astype(jnp.bfloat16))
        value = value - terms[-1].astype(jnp.float32)
    return terms


def base_kernel(experts, gain_ref, ids_ref, weights_ref, *refs):
    block_refs, (out_ref, table_ref, pick_ref) = refs[:-3], refs[-3:]
    ids, weights = ids_ref[...], weights_ref[...]
    count = ids.shape[1]
    zero = jnp.sum(jnp.where(ids >= experts, weights, 0.0), axis=0, keepdims=True)
    same = lax.broadcasted_iota(jnp.int32, (count, count), 0) == lax.broadcasted_iota(
        jnp.int32, (count, count), 1
    )
    zero = jnp.sum(jnp.where(same, zero, 0.0), axis=1, keepdims=True)
    start = 0
    for ref in block_refs:
        end = start + ref.shape[0]
        rows = ref[...].astype(jnp.float32)
        inverse = lax.rsqrt(jnp.mean(rows * rows, axis=-1, keepdims=True) + 1e-06)
        normed = (rows * inverse * gain_ref[...].astype(jnp.float32)).astype(jnp.bfloat16)
        out_ref[start:end] = rows + zero[start:end] * normed.astype(jnp.float32)
        start = end
    tables = []
    for e in range(experts):
        weight = jnp.sum(jnp.where(ids == e, weights, 0.0), axis=0, keepdims=True)
        slots = slot_rows(ids, e)
        tables.append(slots * weight)
        start, total = 0, 0.0
        for ref in block_refs:
            end = start + ref.shape[0]
            part = slots[:, start:end].astype(jnp.bfloat16)
            total += jnp.dot(part, ref[...], preferred_element_type=jnp.float32)
            start = end
        pick_ref[e * CAP:(e + 1) * CAP, :] = total.astype(jnp.bfloat16)
    terms = parts_of(jnp.concatenate(tables, axis=0).T)
    table_ref[...] = jnp.concatenate(terms + terms[:2], axis=1)


def based(experts, blocks, gain, ids_t, weights_t):
    count, width = ids_t.shape[1], blocks[0].shape[1]
    return pl.pallas_call(
        functools.partial(base_kernel, experts),
        out_shape=(
            jax.ShapeDtypeStruct((count, width), jnp.float32),
            jax.ShapeDtypeStruct((count, 5 * experts * CAP), jnp.bfloat16),
            jax.ShapeDtypeStruct((experts * CAP, width), jnp.bfloat16),
        ),
        in_specs=[VMEM] * (3 + len(blocks)),
        out_specs=(VMEM, VMEM, VMEM),
        compiler_params=PARAMS,
        cost_estimate=pl.CostEstimate(
            flops=8 * count * width, bytes_accessed=6 * count * width, transcendentals=0
        ),
    )(gain, ids_t, weights_t, *blocks)


def end_kernel(steps, base_ref, table_ref, *refs):
    back_refs, (out_ref, done, sems) = refs[:-3], refs[-3:]
    columns = base_ref.shape[1] // steps
    copies = []
    for step in range(steps):
        here = slice(step * columns, (step + 1) * columns)
        total = back_refs[0][:, here].astype(jnp.float32)
        for ref in back_refs[1:]:
            total = total + ref[:, here].astype(jnp.float32)
        high, low, _ = parts_of(total)
        rows = jnp.concatenate([high, high, high, low, low], axis=0)
        added = jnp.dot(table_ref[...], rows, preferred_element_type=jnp.float32)
        done[:, here] = (base_ref[:, here] + added).astype(jnp.bfloat16)
        copies.append(
            pltpu.make_async_copy(done.at[:, here], out_ref.at[:, here], sems.at[step])
        )
        copies[-1].start()
    for copy in copies:
        copy.wait()


def ended(base, table, backs):
    count, width = base.shape
    steps = 6
    return pl.pallas_call(
        functools.partial(end_kernel, steps),
        out_shape=jax.ShapeDtypeStruct((count, width), jnp.bfloat16),
        in_specs=[VMEM] * (2 + len(backs)),
        out_specs=HBM,
        scratch_shapes=[pltpu.VMEM((count, width), jnp.bfloat16), pltpu.SemaphoreType.DMA((steps,))],
        compiler_params=PARAMS,
        cost_estimate=pl.CostEstimate(
            flops=2 * count * width * table.shape[0], bytes_accessed=6 * count * width,
            transcendentals=0,
        ),
    )(base, table, *backs)


def early_kernel(left_ref, right_ref, out_ref):
    out_ref[...] = left_ref[...].astype(jnp.float32) + right_ref[...].astype(jnp.float32)


def summed_early(left, right):
    return pl.pallas_call(
        early_kernel,
        out_shape=jax.ShapeDtypeStruct(left.shape, jnp.float32),
        in_specs=[VMEM, VMEM],
        out_specs=VMEM,
        compiler_params=PARAMS,
        cost_estimate=pl.CostEstimate(
            flops=left.size, bytes_accessed=128 * left.size, transcendentals=0
        ),
    )(left, right)


def local(blocks, norm_gain, w_gate, w_up, w_down, route_ids, route_weights):
    slice_width = w_gate.shape[2]
    slice_count = HID // slice_width
    sections = lax.axis_size("section")
    devices = lax.axis_size("expert")
    experts = devices // slice_count
    same_slice = [[e * slice_count + k for e in range(experts)] for k in range(slice_count)]
    places = slice_count // 2
    token_count, width = blocks.shape[1:]

    def moved(value, sections_on, flip, side=0):
        pairs = []
        for s in range(sections):
            for d in range(devices):
                target = d ^ (2 * flip + side)
                pairs.append((s * devices + d, (s + sections_on) % sections * devices + target))
        return lax.ppermute(value, ("section", "expert"), pairs)

    def exchanged(rows):
        rows = rows.reshape(experts, CAP, width)
        return lax.all_to_all(
            rows, "expert", split_axis=0, concat_axis=0, tiled=True, axis_index_groups=same_slice
        ).reshape(experts * CAP, width)

    next_ids = moved(route_ids, -1, 0)[0]
    block, = loaded(blocks[0])
    picked = picked_rows(experts, jnp.swapaxes(next_ids, 0, 1), block)
    if experts > 1:
        picked = exchanged(picked)
    gate_t, up_t, down, gain = loaded(
        after(jnp.swapaxes(w_gate[0], 0, 1), picked), jnp.swapaxes(w_up[0], 0, 1), w_down[0], norm_gain
    )

    near, far = {}, {}
    near[2] = moved(picked, 1, 2)
    far[0] = moved(picked, 1, 0, 1)
    far[2] = moved(after(near[2], gain), 0, 0, 1)
    near[3] = moved(near[2], 0, 1)
    far[3] = moved(far[2], 0, 1)
    near[1] = moved(after(picked, near[2]), 1, 1)
    cuts = [CAP * 3 // 2]
    arrived = [
        moved(after(piece, far[0], near[2]), 1, 0)
        for piece in jnp.split(blocks[0], cuts)
    ]
    base, table, near[0] = based(
        experts, arrived, gain, jnp.swapaxes(route_ids[0], 0, 1),
        jnp.swapaxes(route_weights[0], 0, 1),
    )

    if experts > 1:
        near[0] = exchanged(near[0])
    own, other = {}, {}
    for k in (2, 3, 1, 0):
        first = {2: (near[3],), 3: (other.get(2), arrived[0]), 1: (own.get(3),), 0: (own.get(1), other.get(3))}[k]
        if k == 3:
            far[1] = moved(after(near[1], own[2]), 0, 0, 1)
        own[k], sent = mlp(after(near[k], *first), far[k], gain, gate_t, up_t, down)
        other[k] = moved(sent, 0, 0, 1)
    both = {
        k: (own[k].astype(jnp.float32) + other[k].astype(jnp.float32)).astype(jnp.bfloat16)
        for k in (2, 3, 1)
    }
    early = summed_early(own[0], moved(both[2], 0, 2))
    backs = [
        early, moved(both[3], 0, 3), moved(both[1], 0, 1), other[0],
    ]
    if experts > 1:
        backs = [exchanged(sum(back.astype(jnp.float32) for back in backs).astype(jnp.bfloat16))]
    return ended(base, table, backs)[None]


def solution(mesh):
    placed = (
        P("section", ("dp", "expert"), None),
        P("section", None),
        P("section", None, "expert"),
        P("section", None, "expert"),
        P("section", "expert", None),
        P("section", ("dp", "expert"), None),
        P("section", ("dp", "expert"), None),
    )
    return jax.shard_map(
        local,
        mesh=mesh,
        in_specs=placed,
        out_specs=P("section", ("dp", "expert"), None),
        check_vma=False,
    )
```

```python
import functools

import jax
import jax.numpy as jnp
from jax import lax
from jax.experimental import pallas as pl
from jax.experimental.pallas import tpu as pltpu
from jax.sharding import PartitionSpec as P

HID = 1536
CAP = 32
VMEM = pl.BlockSpec(memory_space=pltpu.VMEM)
HBM = pl.BlockSpec(memory_space=pltpu.HBM)
PARAMS = pltpu.CompilerParams(vmem_limit_bytes=24 * 1024 * 1024)


def after(value, *others):
    return lax.optimization_barrier((value, *others))[0]


def load_kernel(count, *refs):
    sources, targets, sems = refs[:count], refs[count:2 * count], refs[2 * count]
    copies = [
        pltpu.make_async_copy(a, b, sems.at[i]) for i, (a, b) in enumerate(zip(sources, targets))
    ]
    for copy in copies:
        copy.start()
    for copy in copies:
        copy.wait()


def loaded(*arrays):
    return pl.pallas_call(
        functools.partial(load_kernel, len(arrays)),
        out_shape=tuple(jax.ShapeDtypeStruct(a.shape, a.dtype) for a in arrays),
        in_specs=[HBM] * len(arrays),
        out_specs=(VMEM,) * len(arrays),
        scratch_shapes=[pltpu.SemaphoreType.DMA((len(arrays),))],
        compiler_params=PARAMS,
        cost_estimate=pl.CostEstimate(flops=0, bytes_accessed=6 * 1024 * 1024, transcendentals=0),
    )(*(pltpu.with_memory_space_constraint(a, pltpu.HBM) for a in arrays))


def slot_rows(ids, e):
    count = ids.shape[1]
    earlier = lax.broadcasted_iota(jnp.int32, (count, count), 0)
    later = lax.broadcasted_iota(jnp.int32, (count, count), 1)
    before = jnp.where(earlier < later, 1.0, 0.0).astype(jnp.bfloat16)
    slot = lax.broadcasted_iota(jnp.int32, (CAP, count), 0).astype(jnp.float32)
    hit = jnp.max(jnp.where(ids == e, 1.0, 0.0), axis=0, keepdims=True)
    hit = jnp.broadcast_to(hit, (CAP, count))
    rank = jnp.dot(hit.astype(jnp.bfloat16), before, preferred_element_type=jnp.float32)
    return jnp.where(rank == slot, hit, 0.0)


def pick_kernel(experts, ids_ref, block_ref, out_ref):
    for e in range(experts):
        table = slot_rows(ids_ref[...], e).astype(jnp.bfloat16)
        rows = jnp.dot(table, block_ref[...], preferred_element_type=jnp.float32)
        out_ref[e * CAP:(e + 1) * CAP, :] = rows.astype(jnp.bfloat16)


def picked_rows(experts, ids_t, block):
    return pl.pallas_call(
        functools.partial(pick_kernel, experts),
        out_shape=jax.ShapeDtypeStruct((experts * CAP, block.shape[1]), jnp.bfloat16),
        in_specs=[VMEM, VMEM],
        out_specs=VMEM,
        compiler_params=PARAMS,
        cost_estimate=pl.CostEstimate(
            flops=2 * experts * CAP * block.size, bytes_accessed=block.size, transcendentals=0
        ),
    )(ids_t, block)


def mlp_kernel(near_ref, far_ref, gain_ref, gate_ref, up_ref, down_ref, near_out, far_out):
    count = near_ref.shape[0]
    rows = jnp.concatenate([near_ref[...], far_ref[...]], axis=0)
    scaled = rows * gain_ref[...]
    across = (((1,), (1,)), ((), ()))
    gate = lax.dot_general(scaled, gate_ref[...], across, preferred_element_type=jnp.float32)
    up = lax.dot_general(scaled, up_ref[...], across, preferred_element_type=jnp.float32)
    wide = rows.astype(jnp.float32)
    inverse = lax.rsqrt(jnp.mean(wide * wide, axis=-1, keepdims=True) + 1e-06)
    gate, up = gate * inverse, up * inverse
    hidden = (gate / (1.0 + jnp.exp(-gate)) * up).astype(jnp.bfloat16)
    partial = jnp.dot(hidden, down_ref[...], preferred_element_type=jnp.float32)
    partial = partial.astype(jnp.bfloat16)
    near_out[...] = partial[:count]
    far_out[...] = partial[count:]


def mlp(near, far, gain, gate_t, up_t, down):
    rows = 2 * near.shape[0]
    width, hidden = down.shape[1], down.shape[0]
    out = jax.ShapeDtypeStruct(near.shape, jnp.bfloat16)
    return pl.pallas_call(
        mlp_kernel,
        out_shape=(out, out),
        in_specs=[VMEM] * 6,
        out_specs=(VMEM, VMEM),
        compiler_params=PARAMS,
        cost_estimate=pl.CostEstimate(
            flops=6 * rows * width * hidden, bytes_accessed=6 * width * hidden, transcendentals=0
        ),
    )(near, far, gain, gate_t, up_t, down)


def parts_of(value):
    terms = []
    for _ in range(3):
        terms.append(value.astype(jnp.bfloat16))
        value = value - terms[-1].astype(jnp.float32)
    return terms


def base_kernel(experts, gain_ref, ids_ref, weights_ref, *refs):
    block_refs, (out_ref, table_ref, pick_ref) = refs[:-3], refs[-3:]
    ids, weights = ids_ref[...], weights_ref[...]
    count = ids.shape[1]
    zero = jnp.sum(jnp.where(ids >= experts, weights, 0.0), axis=0, keepdims=True)
    same = lax.broadcasted_iota(jnp.int32, (count, count), 0) == lax.broadcasted_iota(
        jnp.int32, (count, count), 1
    )
    zero = jnp.sum(jnp.where(same, zero, 0.0), axis=1, keepdims=True)
    start = 0
    for ref in block_refs:
        end = start + ref.shape[0]
        rows = ref[...].astype(jnp.float32)
        inverse = lax.rsqrt(jnp.mean(rows * rows, axis=-1, keepdims=True) + 1e-06)
        normed = (rows * inverse * gain_ref[...].astype(jnp.float32)).astype(jnp.bfloat16)
        out_ref[start:end] = rows + zero[start:end] * normed.astype(jnp.float32)
        start = end
    tables = []
    for e in range(experts):
        weight = jnp.sum(jnp.where(ids == e, weights, 0.0), axis=0, keepdims=True)
        slots = slot_rows(ids, e)
        tables.append(slots * weight)
        start, total = 0, 0.0
        for ref in block_refs:
            end = start + ref.shape[0]
            part = slots[:, start:end].astype(jnp.bfloat16)
            total += jnp.dot(part, ref[...], preferred_element_type=jnp.float32)
            start = end
        pick_ref[e * CAP:(e + 1) * CAP, :] = total.astype(jnp.bfloat16)
    terms = parts_of(jnp.concatenate(tables, axis=0).T)
    table_ref[...] = jnp.concatenate(terms + terms[:2], axis=1)


def based(experts, blocks, gain, ids_t, weights_t):
    count, width = ids_t.shape[1], blocks[0].shape[1]
    return pl.pallas_call(
        functools.partial(base_kernel, experts),
        out_shape=(
            jax.ShapeDtypeStruct((count, width), jnp.float32),
            jax.ShapeDtypeStruct((count, 5 * experts * CAP), jnp.bfloat16),
            jax.ShapeDtypeStruct((experts * CAP, width), jnp.bfloat16),
        ),
        in_specs=[VMEM] * (3 + len(blocks)),
        out_specs=(VMEM, VMEM, VMEM),
        compiler_params=PARAMS,
        cost_estimate=pl.CostEstimate(
            flops=8 * count * width, bytes_accessed=6 * count * width, transcendentals=0
        ),
    )(gain, ids_t, weights_t, *blocks)


def end_kernel(steps, base_ref, table_ref, *refs):
    back_refs, (out_ref, done, sems) = refs[:-3], refs[-3:]
    columns = base_ref.shape[1] // steps
    copies = []
    for step in range(steps):
        here = slice(step * columns, (step + 1) * columns)
        total = back_refs[0][:, here].astype(jnp.float32)
        for ref in back_refs[1:]:
            total = total + ref[:, here].astype(jnp.float32)
        high, low, _ = parts_of(total)
        rows = jnp.concatenate([high, high, high, low, low], axis=0)
        added = jnp.dot(table_ref[...], rows, preferred_element_type=jnp.float32)
        done[:, here] = (base_ref[:, here] + added).astype(jnp.bfloat16)
        copies.append(
            pltpu.make_async_copy(done.at[:, here], out_ref.at[:, here], sems.at[step])
        )
        copies[-1].start()
    for copy in copies:
        copy.wait()


def ended(base, table, backs):
    count, width = base.shape
    steps = 6
    return pl.pallas_call(
        functools.partial(end_kernel, steps),
        out_shape=jax.ShapeDtypeStruct((count, width), jnp.bfloat16),
        in_specs=[VMEM] * (2 + len(backs)),
        out_specs=HBM,
        scratch_shapes=[pltpu.VMEM((count, width), jnp.bfloat16), pltpu.SemaphoreType.DMA((steps,))],
        compiler_params=PARAMS,
        cost_estimate=pl.CostEstimate(
            flops=2 * count * width * table.shape[0], bytes_accessed=6 * count * width,
            transcendentals=0,
        ),
    )(base, table, *backs)


def early_kernel(left_ref, right_ref, out_ref):
    out_ref[...] = left_ref[...].astype(jnp.float32) + right_ref[...].astype(jnp.float32)


def summed_early(left, right):
    return pl.pallas_call(
        early_kernel,
        out_shape=jax.ShapeDtypeStruct(left.shape, jnp.float32),
        in_specs=[VMEM, VMEM],
        out_specs=VMEM,
        compiler_params=PARAMS,
        cost_estimate=pl.CostEstimate(
            flops=left.size, bytes_accessed=128 * left.size, transcendentals=0
        ),
    )(left, right)


def local(blocks, norm_gain, w_gate, w_up, w_down, route_ids, route_weights):
    slice_width = w_gate.shape[2]
    slice_count = HID // slice_width
    sections = lax.axis_size("section")
    devices = lax.axis_size("expert")
    experts = devices // slice_count
    same_slice = [[e * slice_count + k for e in range(experts)] for k in range(slice_count)]
    places = slice_count // 2
    token_count, width = blocks.shape[1:]

    def moved(value, sections_on, flip, side=0):
        pairs = []
        for s in range(sections):
            for d in range(devices):
                target = d ^ (2 * flip + side)
                pairs.append((s * devices + d, (s + sections_on) % sections * devices + target))
        return lax.ppermute(value, ("section", "expert"), pairs)

    def exchanged(rows):
        rows = rows.reshape(experts, CAP, width)
        return lax.all_to_all(
            rows, "expert", split_axis=0, concat_axis=0, tiled=True, axis_index_groups=same_slice
        ).reshape(experts * CAP, width)

    next_ids = moved(route_ids, -1, 0)[0]
    block, = loaded(blocks[0])
    picked = picked_rows(experts, jnp.swapaxes(next_ids, 0, 1), block)
    if experts > 1:
        picked = exchanged(picked)
    gate_t, up_t, down, gain = loaded(
        after(jnp.swapaxes(w_gate[0], 0, 1), picked), jnp.swapaxes(w_up[0], 0, 1), w_down[0], norm_gain
    )

    near, far = {}, {}
    near[2] = moved(picked, 1, 2)
    far[0] = moved(picked, 1, 0, 1)
    far[2] = moved(after(near[2], gain), 0, 0, 1)
    near[3] = moved(near[2], 0, 1)
    far[3] = moved(far[2], 0, 1)
    near[1] = moved(after(picked, near[2]), 1, 1)
    cuts = [CAP * 3 // 2]
    arrived = [
        moved(after(piece, far[0], near[2]), 1, 0)
        for piece in jnp.split(blocks[0], cuts)
    ]
    base, table, near[0] = based(
        experts, arrived, gain, jnp.swapaxes(route_ids[0], 0, 1),
        jnp.swapaxes(route_weights[0], 0, 1),
    )

    if experts > 1:
        near[0] = exchanged(near[0])
    own, other = {}, {}
    for k in (2, 3, 1, 0):
        first = {2: (near[3],), 3: (other.get(2), arrived[0]), 1: (own.get(3),), 0: (own.get(1), other.get(3))}[k]
        if k == 3:
            far[1] = moved(after(near[1], own[2]), 0, 0, 1)
        own[k], sent = mlp(after(near[k], *first), far[k], gain, gate_t, up_t, down)
        other[k] = moved(sent, 0, 0, 1)
    both = {
        k: (own[k].astype(jnp.float32) + other[k].astype(jnp.float32)).astype(jnp.bfloat16)
        for k in (2, 3, 1)
    }
    early = summed_early(own[0], moved(both[2], 0, 2))
    backs = [
        early, moved(both[3], 0, 3), moved(both[1], 0, 1), other[0],
    ]
    if experts > 1:
        backs = [exchanged(sum(back.astype(jnp.float32) for back in backs).astype(jnp.bfloat16))]
    return ended(base, table, backs)[None]


def solution(mesh):
    placed = (
        P("section", ("dp", "expert"), None),
        P("section", None),
        P("section", None, "expert"),
        P("section", None, "expert"),
        P("section", "expert", None),
        P("section", ("dp", "expert"), None),
        P("section", ("dp", "expert"), None),
    )
    return jax.shard_map(
        local,
        mesh=mesh,
        in_specs=placed,
        out_specs=P("section", ("dp", "expert"), None),
        check_vma=False,
    )
```

```python
import functools

import jax
import jax.numpy as jnp
from jax import lax
from jax.experimental import pallas as pl
from jax.experimental.pallas import tpu as pltpu
from jax.sharding import PartitionSpec as P

HID = 1536
CAP = 32
VMEM = pl.BlockSpec(memory_space=pltpu.VMEM)
HBM = pl.BlockSpec(memory_space=pltpu.HBM)
PARAMS = pltpu.CompilerParams(vmem_limit_bytes=24 * 1024 * 1024)


def after(value, *others):
    return lax.optimization_barrier((value, *others))[0]


def load_kernel(count, *refs):
    sources, targets, sems = refs[:count], refs[count:2 * count], refs[2 * count]
    copies = [
        pltpu.make_async_copy(a, b, sems.at[i]) for i, (a, b) in enumerate(zip(sources, targets))
    ]
    for copy in copies:
        copy.start()
    for copy in copies:
        copy.wait()


def loaded(*arrays):
    return pl.pallas_call(
        functools.partial(load_kernel, len(arrays)),
        out_shape=tuple(jax.ShapeDtypeStruct(a.shape, a.dtype) for a in arrays),
        in_specs=[HBM] * len(arrays),
        out_specs=(VMEM,) * len(arrays),
        scratch_shapes=[pltpu.SemaphoreType.DMA((len(arrays),))],
        compiler_params=PARAMS,
        cost_estimate=pl.CostEstimate(flops=0, bytes_accessed=6 * 1024 * 1024, transcendentals=0),
    )(*(pltpu.with_memory_space_constraint(a, pltpu.HBM) for a in arrays))


def slot_rows(ids, e):
    count = ids.shape[1]
    earlier = lax.broadcasted_iota(jnp.int32, (count, count), 0)
    later = lax.broadcasted_iota(jnp.int32, (count, count), 1)
    before = jnp.where(earlier < later, 1.0, 0.0).astype(jnp.bfloat16)
    slot = lax.broadcasted_iota(jnp.int32, (CAP, count), 0).astype(jnp.float32)
    hit = jnp.max(jnp.where(ids == e, 1.0, 0.0), axis=0, keepdims=True)
    hit = jnp.broadcast_to(hit, (CAP, count))
    rank = jnp.dot(hit.astype(jnp.bfloat16), before, preferred_element_type=jnp.float32)
    return jnp.where(rank == slot, hit, 0.0)


def pick_kernel(experts, ids_ref, block_ref, out_ref):
    for e in range(experts):
        table = slot_rows(ids_ref[...], e).astype(jnp.bfloat16)
        rows = jnp.dot(table, block_ref[...], preferred_element_type=jnp.float32)
        out_ref[e * CAP:(e + 1) * CAP, :] = rows.astype(jnp.bfloat16)


def picked_rows(experts, ids_t, block):
    return pl.pallas_call(
        functools.partial(pick_kernel, experts),
        out_shape=jax.ShapeDtypeStruct((experts * CAP, block.shape[1]), jnp.bfloat16),
        in_specs=[VMEM, VMEM],
        out_specs=VMEM,
        compiler_params=PARAMS,
        cost_estimate=pl.CostEstimate(
            flops=2 * experts * CAP * block.size, bytes_accessed=block.size, transcendentals=0
        ),
    )(ids_t, block)


def mlp_kernel(near_ref, far_ref, gain_ref, gate_ref, up_ref, down_ref, near_out, far_out):
    count = near_ref.shape[0]
    rows = jnp.concatenate([near_ref[...], far_ref[...]], axis=0)
    scaled = rows * gain_ref[...]
    across = (((1,), (1,)), ((), ()))
    gate = lax.dot_general(scaled, gate_ref[...], across, preferred_element_type=jnp.float32)
    up = lax.dot_general(scaled, up_ref[...], across, preferred_element_type=jnp.float32)
    wide = rows.astype(jnp.float32)
    inverse = lax.rsqrt(jnp.mean(wide * wide, axis=-1, keepdims=True) + 1e-06)
    gate, up = gate * inverse, up * inverse
    hidden = (gate / (1.0 + jnp.exp(-gate)) * up).astype(jnp.bfloat16)
    partial = jnp.dot(hidden, down_ref[...], preferred_element_type=jnp.float32)
    partial = partial.astype(jnp.bfloat16)
    near_out[...] = partial[:count]
    far_out[...] = partial[count:]


def mlp(near, far, gain, gate_t, up_t, down):
    rows = 2 * near.shape[0]
    width, hidden = down.shape[1], down.shape[0]
    out = jax.ShapeDtypeStruct(near.shape, jnp.bfloat16)
    return pl.pallas_call(
        mlp_kernel,
        out_shape=(out, out),
        in_specs=[VMEM] * 6,
        out_specs=(VMEM, VMEM),
        compiler_params=PARAMS,
        cost_estimate=pl.CostEstimate(
            flops=6 * rows * width * hidden, bytes_accessed=6 * width * hidden, transcendentals=0
        ),
    )(near, far, gain, gate_t, up_t, down)


def parts_of(value):
    terms = []
    for _ in range(3):
        terms.append(value.astype(jnp.bfloat16))
        value = value - terms[-1].astype(jnp.float32)
    return terms


def base_kernel(experts, gain_ref, ids_ref, weights_ref, *refs):
    block_refs, (out_ref, table_ref, pick_ref) = refs[:-3], refs[-3:]
    ids, weights = ids_ref[...], weights_ref[...]
    count = ids.shape[1]
    zero = jnp.sum(jnp.where(ids >= experts, weights, 0.0), axis=0, keepdims=True)
    same = lax.broadcasted_iota(jnp.int32, (count, count), 0) == lax.broadcasted_iota(
        jnp.int32, (count, count), 1
    )
    zero = jnp.sum(jnp.where(same, zero, 0.0), axis=1, keepdims=True)
    start = 0
    for ref in block_refs:
        end = start + ref.shape[0]
        rows = ref[...].astype(jnp.float32)
        inverse = lax.rsqrt(jnp.mean(rows * rows, axis=-1, keepdims=True) + 1e-06)
        normed = (rows * inverse * gain_ref[...].astype(jnp.float32)).astype(jnp.bfloat16)
        out_ref[start:end] = rows + zero[start:end] * normed.astype(jnp.float32)
        start = end
    tables = []
    for e in range(experts):
        weight = jnp.sum(jnp.where(ids == e, weights, 0.0), axis=0, keepdims=True)
        slots = slot_rows(ids, e)
        tables.append(slots * weight)
        whole = jnp.concatenate([ref[...] for ref in block_refs], axis=0)
        total = jnp.dot(slots.astype(jnp.bfloat16), whole, preferred_element_type=jnp.float32)
        pick_ref[e * CAP:(e + 1) * CAP, :] = total.astype(jnp.bfloat16)
    terms = parts_of(jnp.concatenate(tables, axis=0).T)
    table_ref[...] = jnp.concatenate(terms + terms[:2], axis=1)


def based(experts, blocks, gain, ids_t, weights_t):
    count, width = ids_t.shape[1], blocks[0].shape[1]
    return pl.pallas_call(
        functools.partial(base_kernel, experts),
        out_shape=(
            jax.ShapeDtypeStruct((count, width), jnp.float32),
            jax.ShapeDtypeStruct((count, 5 * experts * CAP), jnp.bfloat16),
            jax.ShapeDtypeStruct((experts * CAP, width), jnp.bfloat16),
        ),
        in_specs=[VMEM] * (3 + len(blocks)),
        out_specs=(VMEM, VMEM, VMEM),
        compiler_params=PARAMS,
        cost_estimate=pl.CostEstimate(
            flops=8 * count * width, bytes_accessed=6 * count * width, transcendentals=0
        ),
    )(gain, ids_t, weights_t, *blocks)


def end_kernel(steps, base_ref, table_ref, *refs):
    back_refs, (out_ref, done, sems) = refs[:-3], refs[-3:]
    columns = base_ref.shape[1] // steps
    copies = []
    for step in range(steps):
        here = slice(step * columns, (step + 1) * columns)
        total = back_refs[0][:, here].astype(jnp.float32)
        for ref in back_refs[1:]:
            total = total + ref[:, here].astype(jnp.float32)
        high, low, _ = parts_of(total)
        rows = jnp.concatenate([high, high, high, low, low], axis=0)
        added = jnp.dot(table_ref[...], rows, preferred_element_type=jnp.float32)
        done[:, here] = (base_ref[:, here] + added).astype(jnp.bfloat16)
        copies.append(
            pltpu.make_async_copy(done.at[:, here], out_ref.at[:, here], sems.at[step])
        )
        copies[-1].start()
    for copy in copies:
        copy.wait()


def ended(base, table, backs):
    count, width = base.shape
    steps = 6
    return pl.pallas_call(
        functools.partial(end_kernel, steps),
        out_shape=jax.ShapeDtypeStruct((count, width), jnp.bfloat16),
        in_specs=[VMEM] * (2 + len(backs)),
        out_specs=HBM,
        scratch_shapes=[pltpu.VMEM((count, width), jnp.bfloat16), pltpu.SemaphoreType.DMA((steps,))],
        compiler_params=PARAMS,
        cost_estimate=pl.CostEstimate(
            flops=2 * count * width * table.shape[0], bytes_accessed=6 * count * width,
            transcendentals=0,
        ),
    )(base, table, *backs)


def early_kernel(left_ref, right_ref, out_ref):
    out_ref[...] = left_ref[...].astype(jnp.float32) + right_ref[...].astype(jnp.float32)


def summed_early(left, right):
    return pl.pallas_call(
        early_kernel,
        out_shape=jax.ShapeDtypeStruct(left.shape, jnp.float32),
        in_specs=[VMEM, VMEM],
        out_specs=VMEM,
        compiler_params=PARAMS,
        cost_estimate=pl.CostEstimate(
            flops=left.size, bytes_accessed=128 * left.size, transcendentals=0
        ),
    )(left, right)


def local(blocks, norm_gain, w_gate, w_up, w_down, route_ids, route_weights):
    slice_width = w_gate.shape[2]
    slice_count = HID // slice_width
    sections = lax.axis_size("section")
    devices = lax.axis_size("expert")
    experts = devices // slice_count
    same_slice = [[e * slice_count + k for e in range(experts)] for k in range(slice_count)]
    places = slice_count // 2
    token_count, width = blocks.shape[1:]

    def moved(value, sections_on, flip, side=0):
        pairs = []
        for s in range(sections):
            for d in range(devices):
                target = d ^ (2 * flip + side)
                pairs.append((s * devices + d, (s + sections_on) % sections * devices + target))
        return lax.ppermute(value, ("section", "expert"), pairs)

    def exchanged(rows):
        rows = rows.reshape(experts, CAP, width)
        return lax.all_to_all(
            rows, "expert", split_axis=0, concat_axis=0, tiled=True, axis_index_groups=same_slice
        ).reshape(experts * CAP, width)

    next_ids = moved(route_ids, -1, 0)[0]
    block, = loaded(blocks[0])
    picked = picked_rows(experts, jnp.swapaxes(next_ids, 0, 1), block)
    if experts > 1:
        picked = exchanged(picked)
    gate_t, up_t, down, gain = loaded(
        after(jnp.swapaxes(w_gate[0], 0, 1), picked), jnp.swapaxes(w_up[0], 0, 1), w_down[0], norm_gain
    )

    near, far = {}, {}
    near[2] = moved(picked, 1, 2)
    far[0] = moved(picked, 1, 0, 1)
    far[2] = moved(after(near[2], gain), 0, 0, 1)
    near[3] = moved(near[2], 0, 1)
    far[3] = moved(far[2], 0, 1)
    near[1] = moved(after(picked, near[2]), 1, 1)
    cuts = [CAP * 3 // 2]
    arrived = [
        moved(after(piece, far[0], near[2]), 1, 0)
        for piece in jnp.split(blocks[0], cuts)
    ]
    base, table, near[0] = based(
        experts, arrived, gain, jnp.swapaxes(route_ids[0], 0, 1),
        jnp.swapaxes(route_weights[0], 0, 1),
    )

    if experts > 1:
        near[0] = exchanged(near[0])
    own, other = {}, {}
    for k in (2, 3, 1, 0):
        first = {2: (near[3],), 3: (other.get(2), arrived[0]), 1: (own.get(3),), 0: (own.get(1), other.get(3))}[k]
        if k == 3:
            far[1] = moved(after(near[1], own[2]), 0, 0, 1)
        own[k], sent = mlp(after(near[k], *first), far[k], gain, gate_t, up_t, down)
        other[k] = moved(sent, 0, 0, 1)
    both = {
        k: (own[k].astype(jnp.float32) + other[k].astype(jnp.float32)).astype(jnp.bfloat16)
        for k in (2, 3, 1)
    }
    early = summed_early(own[0], moved(both[2], 0, 2))
    backs = [
        early, moved(both[3], 0, 3), moved(both[1], 0, 1), other[0],
    ]
    if experts > 1:
        backs = [exchanged(sum(back.astype(jnp.float32) for back in backs).astype(jnp.bfloat16))]
    return ended(base, table, backs)[None]


def solution(mesh):
    placed = (
        P("section", ("dp", "expert"), None),
        P("section", None),
        P("section", None, "expert"),
        P("section", None, "expert"),
        P("section", "expert", None),
        P("section", ("dp", "expert"), None),
        P("section", ("dp", "expert"), None),
    )
    return jax.shard_map(
        local,
        mesh=mesh,
        in_specs=placed,
        out_specs=P("section", ("dp", "expert"), None),
        check_vma=False,
    )
```

```python
import functools

import jax
import jax.numpy as jnp
from jax import lax
from jax.experimental import pallas as pl
from jax.experimental.pallas import tpu as pltpu
from jax.sharding import PartitionSpec as P

HID = 1536
CAP = 32
VMEM = pl.BlockSpec(memory_space=pltpu.VMEM)
HBM = pl.BlockSpec(memory_space=pltpu.HBM)
PARAMS = pltpu.CompilerParams(vmem_limit_bytes=24 * 1024 * 1024)


def after(value, *others):
    return lax.optimization_barrier((value, *others))[0]


def load_kernel(count, *refs):
    sources, targets, sems = refs[:count], refs[count:2 * count], refs[2 * count]
    copies = [
        pltpu.make_async_copy(a, b, sems.at[i]) for i, (a, b) in enumerate(zip(sources, targets))
    ]
    for copy in copies:
        copy.start()
    for copy in copies:
        copy.wait()


def loaded(*arrays):
    return pl.pallas_call(
        functools.partial(load_kernel, len(arrays)),
        out_shape=tuple(jax.ShapeDtypeStruct(a.shape, a.dtype) for a in arrays),
        in_specs=[HBM] * len(arrays),
        out_specs=(VMEM,) * len(arrays),
        scratch_shapes=[pltpu.SemaphoreType.DMA((len(arrays),))],
        compiler_params=PARAMS,
        cost_estimate=pl.CostEstimate(flops=0, bytes_accessed=6 * 1024 * 1024, transcendentals=0),
    )(*(pltpu.with_memory_space_constraint(a, pltpu.HBM) for a in arrays))


def slot_rows(ids, e):
    count = ids.shape[1]
    earlier = lax.broadcasted_iota(jnp.int32, (count, count), 0)
    later = lax.broadcasted_iota(jnp.int32, (count, count), 1)
    before = jnp.where(earlier < later, 1.0, 0.0).astype(jnp.bfloat16)
    slot = lax.broadcasted_iota(jnp.int32, (CAP, count), 0).astype(jnp.float32)
    hit = jnp.max(jnp.where(ids == e, 1.0, 0.0), axis=0, keepdims=True)
    hit = jnp.broadcast_to(hit, (CAP, count))
    rank = jnp.dot(hit.astype(jnp.bfloat16), before, preferred_element_type=jnp.float32)
    return jnp.where(rank == slot, hit, 0.0)


def pick_kernel(experts, ids_ref, block_ref, out_ref):
    for e in range(experts):
        table = slot_rows(ids_ref[...], e).astype(jnp.bfloat16)
        rows = jnp.dot(table, block_ref[...], preferred_element_type=jnp.float32)
        out_ref[e * CAP:(e + 1) * CAP, :] = rows.astype(jnp.bfloat16)


def picked_rows(experts, ids_t, block):
    return pl.pallas_call(
        functools.partial(pick_kernel, experts),
        out_shape=jax.ShapeDtypeStruct((experts * CAP, block.shape[1]), jnp.bfloat16),
        in_specs=[VMEM, VMEM],
        out_specs=VMEM,
        compiler_params=PARAMS,
        cost_estimate=pl.CostEstimate(
            flops=2 * experts * CAP * block.size, bytes_accessed=block.size, transcendentals=0
        ),
    )(ids_t, block)


def mlp_kernel(near_ref, far_ref, gain_ref, gate_ref, up_ref, down_ref, near_out, far_out):
    count = near_ref.shape[0]
    rows = jnp.concatenate([near_ref[...], far_ref[...]], axis=0)
    scaled = rows * gain_ref[...]
    across = (((1,), (1,)), ((), ()))
    gate = lax.dot_general(scaled, gate_ref[...], across, preferred_element_type=jnp.float32)
    up = lax.dot_general(scaled, up_ref[...], across, preferred_element_type=jnp.float32)
    wide = rows.astype(jnp.float32)
    inverse = lax.rsqrt(jnp.mean(wide * wide, axis=-1, keepdims=True) + 1e-06)
    gate, up = gate * inverse, up * inverse
    hidden = (gate / (1.0 + jnp.exp(-gate)) * up).astype(jnp.bfloat16)
    partial = jnp.dot(hidden, down_ref[...], preferred_element_type=jnp.float32)
    partial = partial.astype(jnp.bfloat16)
    near_out[...] = partial[:count]
    far_out[...] = partial[count:]


def mlp(near, far, gain, gate_t, up_t, down):
    rows = 2 * near.shape[0]
    width, hidden = down.shape[1], down.shape[0]
    out = jax.ShapeDtypeStruct(near.shape, jnp.bfloat16)
    return pl.pallas_call(
        mlp_kernel,
        out_shape=(out, out),
        in_specs=[VMEM] * 6,
        out_specs=(VMEM, VMEM),
        compiler_params=PARAMS,
        cost_estimate=pl.CostEstimate(
            flops=6 * rows * width * hidden, bytes_accessed=6 * width * hidden, transcendentals=0
        ),
    )(near, far, gain, gate_t, up_t, down)


def parts_of(value):
    terms = []
    for _ in range(3):
        terms.append(value.astype(jnp.bfloat16))
        value = value - terms[-1].astype(jnp.float32)
    return terms


def base_kernel(experts, gain_ref, ids_ref, weights_ref, *refs):
    block_refs, (out_ref, table_ref, pick_ref) = refs[:-3], refs[-3:]
    ids, weights = ids_ref[...], weights_ref[...]
    count = ids.shape[1]
    zero = jnp.sum(jnp.where(ids >= experts, weights, 0.0), axis=0, keepdims=True)
    same = lax.broadcasted_iota(jnp.int32, (count, count), 0) == lax.broadcasted_iota(
        jnp.int32, (count, count), 1
    )
    zero = jnp.sum(jnp.where(same, zero, 0.0), axis=1, keepdims=True)
    start = 0
    for ref in block_refs:
        end = start + ref.shape[0]
        rows = ref[...].astype(jnp.float32)
        inverse = lax.rsqrt(jnp.mean(rows * rows, axis=-1, keepdims=True) + 1e-06)
        normed = (rows * inverse * gain_ref[...].astype(jnp.float32)).astype(jnp.bfloat16)
        out_ref[start:end] = rows + zero[start:end] * normed.astype(jnp.float32)
        start = end
    tables = []
    for e in range(experts):
        weight = jnp.sum(jnp.where(ids == e, weights, 0.0), axis=0, keepdims=True)
        slots = slot_rows(ids, e)
        tables.append(slots * weight)
        whole = jnp.concatenate([ref[...] for ref in block_refs], axis=0)
        total = jnp.dot(slots.astype(jnp.bfloat16), whole, preferred_element_type=jnp.float32)
        pick_ref[e * CAP:(e + 1) * CAP, :] = total.astype(jnp.bfloat16)
    terms = parts_of(jnp.concatenate(tables, axis=0).T)
    table_ref[...] = jnp.concatenate(terms + terms[:2], axis=1)


def based(experts, blocks, gain, ids_t, weights_t):
    count, width = ids_t.shape[1], blocks[0].shape[1]
    return pl.pallas_call(
        functools.partial(base_kernel, experts),
        out_shape=(
            jax.ShapeDtypeStruct((count, width), jnp.float32),
            jax.ShapeDtypeStruct((count, 5 * experts * CAP), jnp.bfloat16),
            jax.ShapeDtypeStruct((experts * CAP, width), jnp.bfloat16),
        ),
        in_specs=[VMEM] * (3 + len(blocks)),
        out_specs=(VMEM, VMEM, VMEM),
        compiler_params=PARAMS,
        cost_estimate=pl.CostEstimate(
            flops=8 * count * width, bytes_accessed=6 * count * width, transcendentals=0
        ),
    )(gain, ids_t, weights_t, *blocks)


def end_kernel(steps, base_ref, table_ref, *refs):
    back_refs, (out_ref, done, sems) = refs[:-3], refs[-3:]
    columns = base_ref.shape[1] // steps
    copies = []
    for step in range(steps):
        here = slice(step * columns, (step + 1) * columns)
        total = back_refs[0][:, here].astype(jnp.float32)
        for ref in back_refs[1:]:
            total = total + ref[:, here].astype(jnp.float32)
        high, low, _ = parts_of(total)
        rows = jnp.concatenate([high, high, high, low, low], axis=0)
        added = jnp.dot(table_ref[...], rows, preferred_element_type=jnp.float32)
        done[:, here] = (base_ref[:, here] + added).astype(jnp.bfloat16)
        copies.append(
            pltpu.make_async_copy(done.at[:, here], out_ref.at[:, here], sems.at[step])
        )
        copies[-1].start()
    for copy in copies:
        copy.wait()


def ended(base, table, backs):
    count, width = base.shape
    steps = 6
    return pl.pallas_call(
        functools.partial(end_kernel, steps),
        out_shape=jax.ShapeDtypeStruct((count, width), jnp.bfloat16),
        in_specs=[VMEM] * (2 + len(backs)),
        out_specs=HBM,
        scratch_shapes=[pltpu.VMEM((count, width), jnp.bfloat16), pltpu.SemaphoreType.DMA((steps,))],
        compiler_params=PARAMS,
        cost_estimate=pl.CostEstimate(
            flops=2 * count * width * table.shape[0], bytes_accessed=6 * count * width,
            transcendentals=0,
        ),
    )(base, table, *backs)


def early_kernel(left_ref, right_ref, out_ref):
    out_ref[...] = left_ref[...].astype(jnp.float32) + right_ref[...].astype(jnp.float32)


def summed_early(left, right):
    return pl.pallas_call(
        early_kernel,
        out_shape=jax.ShapeDtypeStruct(left.shape, jnp.float32),
        in_specs=[VMEM, VMEM],
        out_specs=VMEM,
        compiler_params=PARAMS,
        cost_estimate=pl.CostEstimate(
            flops=left.size, bytes_accessed=128 * left.size, transcendentals=0
        ),
    )(left, right)


def local(blocks, norm_gain, w_gate, w_up, w_down, route_ids, route_weights):
    slice_width = w_gate.shape[2]
    slice_count = HID // slice_width
    sections = lax.axis_size("section")
    devices = lax.axis_size("expert")
    experts = devices // slice_count
    same_slice = [[e * slice_count + k for e in range(experts)] for k in range(slice_count)]
    places = slice_count // 2
    token_count, width = blocks.shape[1:]

    def moved(value, sections_on, flip, side=0):
        pairs = []
        for s in range(sections):
            for d in range(devices):
                target = d ^ (2 * flip + side)
                pairs.append((s * devices + d, (s + sections_on) % sections * devices + target))
        return lax.ppermute(value, ("section", "expert"), pairs)

    def exchanged(rows):
        rows = rows.reshape(experts, CAP, width)
        return lax.all_to_all(
            rows, "expert", split_axis=0, concat_axis=0, tiled=True, axis_index_groups=same_slice
        ).reshape(experts * CAP, width)

    next_ids = moved(route_ids, -1, 0)[0]
    block, = loaded(blocks[0])
    picked = picked_rows(experts, jnp.swapaxes(next_ids, 0, 1), block)
    if experts > 1:
        picked = exchanged(picked)
    gate_t, up_t, down, gain = loaded(
        after(jnp.swapaxes(w_gate[0], 0, 1), picked), jnp.swapaxes(w_up[0], 0, 1), w_down[0], norm_gain
    )

    near, far = {}, {}
    near[2] = moved(picked, 1, 2)
    far[0] = moved(picked, 1, 0, 1)
    far[2] = moved(after(near[2], gain), 0, 0, 1)
    near[3] = moved(near[2], 0, 1)
    far[3] = moved(far[2], 0, 1)
    near[1] = moved(after(picked, near[2]), 1, 1)
    cuts = [CAP * 3 // 2]
    arrived = [
        moved(after(piece, far[0], near[2]), 1, 0)
        for piece in jnp.split(blocks[0], cuts)
    ]
    base, table, near[0] = based(
        experts, arrived, gain, jnp.swapaxes(route_ids[0], 0, 1),
        jnp.swapaxes(route_weights[0], 0, 1),
    )

    if experts > 1:
        near[0] = exchanged(near[0])
    own, other = {}, {}
    for k in (2, 3, 1, 0):
        first = {2: (gain,), 3: (other.get(2), arrived[0]), 1: (own.get(3),), 0: (own.get(1), other.get(3))}[k]
        if k == 3:
            far[1] = moved(after(near[1], own[2]), 0, 0, 1)
        own[k], sent = mlp(after(near[k], *first), far[k], gain, gate_t, up_t, down)
        other[k] = moved(sent, 0, 0, 1)
    both = {
        k: (own[k].astype(jnp.float32) + other[k].astype(jnp.float32)).astype(jnp.bfloat16)
        for k in (2, 3, 1)
    }
    early = summed_early(own[0], moved(both[2], 0, 2))
    backs = [
        early, moved(both[3], 0, 3), moved(both[1], 0, 1), other[0],
    ]
    if experts > 1:
        backs = [exchanged(sum(back.astype(jnp.float32) for back in backs).astype(jnp.bfloat16))]
    return ended(base, table, backs)[None]


def solution(mesh):
    placed = (
        P("section", ("dp", "expert"), None),
        P("section", None),
        P("section", None, "expert"),
        P("section", None, "expert"),
        P("section", "expert", None),
        P("section", ("dp", "expert"), None),
        P("section", ("dp", "expert"), None),
    )
    return jax.shard_map(
        local,
        mesh=mesh,
        in_specs=placed,
        out_specs=P("section", ("dp", "expert"), None),
        check_vma=False,
    )
```

```python
import functools

import jax
import jax.numpy as jnp
from jax import lax
from jax.experimental import pallas as pl
from jax.experimental.pallas import tpu as pltpu
from jax.sharding import PartitionSpec as P

HID = 1536
CAP = 32
VMEM = pl.BlockSpec(memory_space=pltpu.VMEM)
HBM = pl.BlockSpec(memory_space=pltpu.HBM)
PARAMS = pltpu.CompilerParams(vmem_limit_bytes=24 * 1024 * 1024)


def after(value, *others):
    return lax.optimization_barrier((value, *others))[0]


def load_kernel(count, *refs):
    sources, targets, sems = refs[:count], refs[count:2 * count], refs[2 * count]
    copies = [
        pltpu.make_async_copy(a, b, sems.at[i]) for i, (a, b) in enumerate(zip(sources, targets))
    ]
    for copy in copies:
        copy.start()
    for copy in copies:
        copy.wait()


def loaded(*arrays):
    return pl.pallas_call(
        functools.partial(load_kernel, len(arrays)),
        out_shape=tuple(jax.ShapeDtypeStruct(a.shape, a.dtype) for a in arrays),
        in_specs=[HBM] * len(arrays),
        out_specs=(VMEM,) * len(arrays),
        scratch_shapes=[pltpu.SemaphoreType.DMA((len(arrays),))],
        compiler_params=PARAMS,
        cost_estimate=pl.CostEstimate(flops=0, bytes_accessed=6 * 1024 * 1024, transcendentals=0),
    )(*(pltpu.with_memory_space_constraint(a, pltpu.HBM) for a in arrays))


def slot_rows(ids, e):
    count = ids.shape[1]
    earlier = lax.broadcasted_iota(jnp.int32, (count, count), 0)
    later = lax.broadcasted_iota(jnp.int32, (count, count), 1)
    before = jnp.where(earlier < later, 1.0, 0.0).astype(jnp.bfloat16)
    slot = lax.broadcasted_iota(jnp.int32, (CAP, count), 0).astype(jnp.float32)
    hit = jnp.max(jnp.where(ids == e, 1.0, 0.0), axis=0, keepdims=True)
    hit = jnp.broadcast_to(hit, (CAP, count))
    rank = jnp.dot(hit.astype(jnp.bfloat16), before, preferred_element_type=jnp.float32)
    return jnp.where(rank == slot, hit, 0.0)


def pick_kernel(experts, ids_ref, block_ref, out_ref):
    for e in range(experts):
        table = slot_rows(ids_ref[...], e).astype(jnp.bfloat16)
        rows = jnp.dot(table, block_ref[...], preferred_element_type=jnp.float32)
        out_ref[e * CAP:(e + 1) * CAP, :] = rows.astype(jnp.bfloat16)


def picked_rows(experts, ids_t, block):
    return pl.pallas_call(
        functools.partial(pick_kernel, experts),
        out_shape=jax.ShapeDtypeStruct((experts * CAP, block.shape[1]), jnp.bfloat16),
        in_specs=[VMEM, VMEM],
        out_specs=VMEM,
        compiler_params=PARAMS,
        cost_estimate=pl.CostEstimate(
            flops=2 * experts * CAP * block.size, bytes_accessed=block.size, transcendentals=0
        ),
    )(ids_t, block)


def mlp_kernel(near_ref, far_ref, gain_ref, gate_ref, up_ref, down_ref, near_out, far_out):
    count = near_ref.shape[0]
    rows = jnp.concatenate([near_ref[...], far_ref[...]], axis=0)
    scaled = rows * gain_ref[...]
    across = (((1,), (1,)), ((), ()))
    gate = lax.dot_general(scaled, gate_ref[...], across, preferred_element_type=jnp.float32)
    up = lax.dot_general(scaled, up_ref[...], across, preferred_element_type=jnp.float32)
    wide = rows.astype(jnp.float32)
    inverse = lax.rsqrt(jnp.mean(wide * wide, axis=-1, keepdims=True) + 1e-06)
    gate, up = gate * inverse, up * inverse
    hidden = (gate / (1.0 + jnp.exp(-gate)) * up).astype(jnp.bfloat16)
    partial = jnp.dot(hidden, down_ref[...], preferred_element_type=jnp.float32)
    partial = partial.astype(jnp.bfloat16)
    near_out[...] = partial[:count]
    far_out[...] = partial[count:]


def mlp(near, far, gain, gate_t, up_t, down):
    rows = 2 * near.shape[0]
    width, hidden = down.shape[1], down.shape[0]
    out = jax.ShapeDtypeStruct(near.shape, jnp.bfloat16)
    return pl.pallas_call(
        mlp_kernel,
        out_shape=(out, out),
        in_specs=[VMEM] * 6,
        out_specs=(VMEM, VMEM),
        compiler_params=PARAMS,
        cost_estimate=pl.CostEstimate(
            flops=6 * rows * width * hidden, bytes_accessed=6 * width * hidden, transcendentals=0
        ),
    )(near, far, gain, gate_t, up_t, down)


def parts_of(value):
    terms = []
    for _ in range(3):
        terms.append(value.astype(jnp.bfloat16))
        value = value - terms[-1].astype(jnp.float32)
    return terms


def base_kernel(experts, gain_ref, ids_ref, weights_ref, *refs):
    block_refs, (out_ref, table_ref, pick_ref) = refs[:-3], refs[-3:]
    ids, weights = ids_ref[...], weights_ref[...]
    count = ids.shape[1]
    zero = jnp.sum(jnp.where(ids >= experts, weights, 0.0), axis=0, keepdims=True)
    same = lax.broadcasted_iota(jnp.int32, (count, count), 0) == lax.broadcasted_iota(
        jnp.int32, (count, count), 1
    )
    zero = jnp.sum(jnp.where(same, zero, 0.0), axis=1, keepdims=True)
    start = 0
    for ref in block_refs:
        end = start + ref.shape[0]
        rows = ref[...].astype(jnp.float32)
        inverse = lax.rsqrt(jnp.mean(rows * rows, axis=-1, keepdims=True) + 1e-06)
        normed = (rows * inverse * gain_ref[...].astype(jnp.float32)).astype(jnp.bfloat16)
        out_ref[start:end] = rows + zero[start:end] * normed.astype(jnp.float32)
        start = end
    tables = []
    for e in range(experts):
        weight = jnp.sum(jnp.where(ids == e, weights, 0.0), axis=0, keepdims=True)
        slots = slot_rows(ids, e)
        tables.append(slots * weight)
        whole = jnp.concatenate([ref[...] for ref in block_refs], axis=0)
        total = jnp.dot(slots.astype(jnp.bfloat16), whole, preferred_element_type=jnp.float32)
        pick_ref[e * CAP:(e + 1) * CAP, :] = total.astype(jnp.bfloat16)
    terms = parts_of(jnp.concatenate(tables, axis=0).T)
    table_ref[...] = jnp.concatenate(terms + terms[:2], axis=1)


def based(experts, blocks, gain, ids_t, weights_t):
    count, width = ids_t.shape[1], blocks[0].shape[1]
    return pl.pallas_call(
        functools.partial(base_kernel, experts),
        out_shape=(
            jax.ShapeDtypeStruct((count, width), jnp.float32),
            jax.ShapeDtypeStruct((count, 5 * experts * CAP), jnp.bfloat16),
            jax.ShapeDtypeStruct((experts * CAP, width), jnp.bfloat16),
        ),
        in_specs=[VMEM] * (3 + len(blocks)),
        out_specs=(VMEM, VMEM, VMEM),
        compiler_params=PARAMS,
        cost_estimate=pl.CostEstimate(
            flops=8 * count * width, bytes_accessed=6 * count * width, transcendentals=0
        ),
    )(gain, ids_t, weights_t, *blocks)


def end_kernel(steps, base_ref, table_ref, *refs):
    back_refs, (out_ref, done, sems) = refs[:-3], refs[-3:]
    columns = base_ref.shape[1] // steps
    copies = []
    for step in range(steps):
        here = slice(step * columns, (step + 1) * columns)
        total = back_refs[0][:, here].astype(jnp.float32)
        for ref in back_refs[1:]:
            total = total + ref[:, here].astype(jnp.float32)
        high, low, _ = parts_of(total)
        rows = jnp.concatenate([high, high, high, low, low], axis=0)
        added = jnp.dot(table_ref[...], rows, preferred_element_type=jnp.float32)
        done[:, here] = (base_ref[:, here] + added).astype(jnp.bfloat16)
        copies.append(
            pltpu.make_async_copy(done.at[:, here], out_ref.at[:, here], sems.at[step])
        )
        copies[-1].start()
    for copy in copies:
        copy.wait()


def ended(base, table, backs):
    count, width = base.shape
    steps = 6
    return pl.pallas_call(
        functools.partial(end_kernel, steps),
        out_shape=jax.ShapeDtypeStruct((count, width), jnp.bfloat16),
        in_specs=[VMEM] * (2 + len(backs)),
        out_specs=HBM,
        scratch_shapes=[pltpu.VMEM((count, width), jnp.bfloat16), pltpu.SemaphoreType.DMA((steps,))],
        compiler_params=PARAMS,
        cost_estimate=pl.CostEstimate(
            flops=2 * count * width * table.shape[0], bytes_accessed=6 * count * width,
            transcendentals=0,
        ),
    )(base, table, *backs)


def early_kernel(left_ref, right_ref, out_ref):
    out_ref[...] = left_ref[...].astype(jnp.float32) + right_ref[...].astype(jnp.float32)


def summed_early(left, right):
    return pl.pallas_call(
        early_kernel,
        out_shape=jax.ShapeDtypeStruct(left.shape, jnp.float32),
        in_specs=[VMEM, VMEM],
        out_specs=VMEM,
        compiler_params=PARAMS,
        cost_estimate=pl.CostEstimate(
            flops=left.size, bytes_accessed=128 * left.size, transcendentals=0
        ),
    )(left, right)


def local(blocks, norm_gain, w_gate, w_up, w_down, route_ids, route_weights):
    slice_width = w_gate.shape[2]
    slice_count = HID // slice_width
    sections = lax.axis_size("section")
    devices = lax.axis_size("expert")
    experts = devices // slice_count
    same_slice = [[e * slice_count + k for e in range(experts)] for k in range(slice_count)]
    places = slice_count // 2
    token_count, width = blocks.shape[1:]

    def moved(value, sections_on, flip, side=0):
        pairs = []
        for s in range(sections):
            for d in range(devices):
                target = d ^ (2 * flip + side)
                pairs.append((s * devices + d, (s + sections_on) % sections * devices + target))
        return lax.ppermute(value, ("section", "expert"), pairs)

    def exchanged(rows):
        rows = rows.reshape(experts, CAP, width)
        return lax.all_to_all(
            rows, "expert", split_axis=0, concat_axis=0, tiled=True, axis_index_groups=same_slice
        ).reshape(experts * CAP, width)

    next_ids = moved(route_ids, -1, 0)[0]
    block, = loaded(blocks[0])
    picked = picked_rows(experts, jnp.swapaxes(next_ids, 0, 1), block)
    if experts > 1:
        picked = exchanged(picked)
    gate_t, up_t, down, gain = loaded(
        after(jnp.swapaxes(w_gate[0], 0, 1), picked), jnp.swapaxes(w_up[0], 0, 1), w_down[0], norm_gain
    )

    near, far = {}, {}
    near[2] = moved(picked, 1, 2)
    far[0] = moved(picked, 1, 0, 1)
    far[2] = moved(after(near[2], gain), 0, 0, 1)
    near[3] = moved(near[2], 0, 1)
    far[3] = moved(far[2], 0, 1)
    near[1] = moved(after(picked, near[2]), 1, 1)
    cuts = [CAP]
    arrived = [
        moved(after(piece, far[0], near[2]), 1, 0)
        for piece in jnp.split(blocks[0], cuts)
    ]
    base, table, near[0] = based(
        experts, arrived, gain, jnp.swapaxes(route_ids[0], 0, 1),
        jnp.swapaxes(route_weights[0], 0, 1),
    )

    if experts > 1:
        near[0] = exchanged(near[0])
    own, other = {}, {}
    for k in (2, 3, 1, 0):
        first = {2: (gain,), 3: (other.get(2), arrived[0]), 1: (own.get(3),), 0: (own.get(1), other.get(3))}[k]
        if k == 3:
            far[1] = moved(after(near[1], own[2]), 0, 0, 1)
        own[k], sent = mlp(after(near[k], *first), far[k], gain, gate_t, up_t, down)
        other[k] = moved(sent, 0, 0, 1)
    both = {
        k: (own[k].astype(jnp.float32) + other[k].astype(jnp.float32)).astype(jnp.bfloat16)
        for k in (2, 3, 1)
    }
    early = summed_early(own[0], moved(both[2], 0, 2))
    backs = [
        early, moved(both[3], 0, 3), moved(both[1], 0, 1), other[0],
    ]
    if experts > 1:
        backs = [exchanged(sum(back.astype(jnp.float32) for back in backs).astype(jnp.bfloat16))]
    return ended(base, table, backs)[None]


def solution(mesh):
    placed = (
        P("section", ("dp", "expert"), None),
        P("section", None),
        P("section", None, "expert"),
        P("section", None, "expert"),
        P("section", "expert", None),
        P("section", ("dp", "expert"), None),
        P("section", ("dp", "expert"), None),
    )
    return jax.shard_map(
        local,
        mesh=mesh,
        in_specs=placed,
        out_specs=P("section", ("dp", "expert"), None),
        check_vma=False,
    )
```
